32 devices in a mesh: segment: 2 (over core), angle: 8 (over z, x), tile: 2 (over y).
Axes of the slice: x: 2, y: 2, z: 4, core: 2. Of those that a mesh axis runs over, the one named last changes fastest.
Arguments:
- sinogram: float32 [32, 32, 4096], P(('segment', 'angle'), 'tile'), may hold values from -6 to 6
- paganin_width: float32 [1], replicated, may hold values from 2 to 8
- window_block: int32 [32, 2], replicated, may hold values from 0 to 28
Outputs:
- volume: float32 [2, 32, 32768], P('tile', None, ('segment', 'angle'))
The draws below stay inside these ranges and needn't reach their ends.
All inputs are finite; a program needn't handle non-finite values.
Results may differ from the reference program's by a relative error of at most 0.0035.
Values may be sent and summed in bfloat16 or wider, within the bound.
No kernel may reach another device: no remote copies, remote signals or barrier semaphores. Data moves between devices by JAX's collectives and lax.ppermute only.
A program may use at most 64 MiB of HBM per device.

```python
import math
import jax
import jax.numpy as jnp
from jax import lax

W = 4096
WIN = 512
BAND = 128
SLICES = 32
TCOLS = 256
ANGLES = 32
TROWS = 128
TILES = 2


def touch_ends(drawn, stream_key, smallest, top_value):
    longest = drawn.shape.index(max(drawn.shape))
    spots = []
    for shift in (0, 1):
        where = [jax.random.randint(jax.random.fold_in(stream_key, axis), (), 0, length) for axis, length in enumerate(drawn.shape)]
        where[longest] = (where[longest] + shift) % drawn.shape[longest]
        spots.append(tuple(where))
    return drawn.at[spots[0]].set(smallest).at[spots[1]].set(top_value)


def block_scale(stream_key, shape, shards, low, largest):
    loudness = 1.0
    for dim, parts in shards:
        steps = jax.random.uniform(jax.random.fold_in(jax.random.fold_in(stream_key, 6), dim), (parts,), jnp.float32, low / len(shards), largest / len(shards))
        loudness = loudness * jnp.repeat(jnp.exp(steps), shape[dim] // parts).reshape((-1,) + (1,) * (len(shape) - 1 - dim))
    return loudness


def normal_values(own_key, shape, deviation, most, shards=(), held_as=jnp.bfloat16):
    loudness = block_scale(own_key, shape, shards, -0.22, 0.18) if shards else 1.0
    drawn = jax.random.normal(own_key, shape, jnp.float32) * deviation * loudness
    return jnp.minimum(jnp.maximum(drawn, -most), most).astype(held_as)


def setup_inputs(seed: int = 0) -> dict:
    key_list = jax.random.split(jax.random.key(seed), 4)
    return {
        "sinogram": normal_values(key_list[0], (ANGLES, SLICES, W), 1.0, 6.0, ((0, 16), (1, 2)), jnp.float32),
        "paganin_width": jnp.clip(jnp.exp(jax.random.uniform(key_list[1], (1,), jnp.float32, math.log(2.0), math.log(8.0))), 2.0, 8.0),
        "window_block": touch_ends(jax.random.randint(key_list[2], (ANGLES, TILES), 0, (W - WIN) // 128 + 1), jax.random.fold_in(key_list[2], 1), 0, ((W - WIN) // 128 + 1) - 1).astype(jnp.int32),
    }


def band_kernels(width):
    inner = jnp.arange(128, dtype=jnp.int32)
    offsets = (jnp.arange(3, dtype=jnp.int32) - 1)[:, None, None] * 128 + inner[None, :, None] - inner[None, None, :]
    spread = offsets.astype(jnp.float32)
    inside = jnp.abs(offsets) <= BAND
    taps = jnp.arange(-BAND, BAND + 1).astype(jnp.float32)
    normal_total = jnp.sum(jnp.exp(-jnp.abs(taps) / width))
    paganin = jnp.where(inside, jnp.exp(-jnp.abs(spread) / width) / normal_total, 0.0)
    squared = jnp.maximum(spread * spread, 1.0)
    odd_taps = jnp.where(inside & (offsets % 2 == 1), -1.0 / (math.pi * math.pi * squared), 0.0)
    ramp = jnp.where(offsets == 0, 0.25, odd_taps)
    return paganin, ramp


def apply_band(rows, kernels):
    row_count, bins = rows.shape
    blocks = bins // 128
    shaped = rows.reshape(row_count, blocks, 128)
    padded = jnp.pad(shaped, ((0, 0), (1, 1), (0, 0)))
    result = jnp.zeros_like(shaped)
    for offset in range(3):
        result = result + jnp.einsum("rbi,io->rbo", padded[:, offset:offset + blocks], kernels[offset], precision=lax.Precision.HIGHEST)
    return result.reshape(row_count, bins)


def hat_block(angles, angle_total, row_first, row_count, tile_rows):
    theta = math.pi * angles.astype(jnp.float32) / angle_total
    rows_here = (row_first + jnp.arange(row_count, dtype=jnp.int32)).astype(jnp.float32) - (tile_rows - 1) / 2.0
    columns = jnp.arange(TCOLS).astype(jnp.float32) - (TCOLS - 1) / 2.0
    across = columns[None, None, :] * jnp.cos(theta)[:, None, None] + rows_here[None, :, None] * jnp.sin(theta)[:, None, None]
    across = across.reshape(angles.shape[0], row_count * TCOLS) + WIN / 2.0
    detector = jnp.arange(WIN).astype(jnp.float32)
    weight = jnp.maximum(0.0, 1.0 - jnp.abs(across[:, None, :] - detector[None, :, None]))
    return weight.astype(jnp.bfloat16)


def reference(sinogram, paganin_width, window_block):
    smoothing, ramping = band_kernels(paganin_width[0])
    rows = sinogram.reshape(ANGLES * SLICES, W)
    filtered = apply_band(apply_band(rows, smoothing), ramping).astype(jnp.bfloat16).reshape(ANGLES, SLICES, W)

    def one_tile(tile_index):
        def advance(total, angle):
            start = (window_block[angle, tile_index] * 128).astype(jnp.int32)
            window = lax.dynamic_slice_in_dim(filtered[angle], start, WIN, 1)
            weights = hat_block(angle[None], ANGLES, 0, TROWS, TROWS)[0]
            return total + jnp.dot(window, weights, preferred_element_type=jnp.float32), None

        start_total = jnp.zeros((SLICES, TROWS * TCOLS), jnp.float32)
        total, ignored = lax.scan(advance, start_total, jnp.arange(ANGLES, dtype=jnp.int32))
        return total

    return lax.map(one_tile, jnp.arange(TILES, dtype=jnp.int32))
```

```python
import functools
import math

import jax
import jax.numpy as jnp
import numpy as np
from jax import lax
from jax.experimental import pallas as pl
from jax.experimental.pallas import tpu as pltpu
from jax.sharding import PartitionSpec as P

WIN = 512
BAND = 128
ROWS_DEV = 8
TCOLS = 256
LANES = 128
CHUNK = 64
DEPTH = 80


def split(value):
    high = value.astype(jnp.bfloat16)
    return high, (value - high.astype(jnp.float32)).astype(jnp.bfloat16)


def three_dots(rows, taps):
    (row_high, row_low), (tap_high, tap_low) = rows, taps
    dot = functools.partial(jnp.dot, preferred_element_type=jnp.float32)
    return dot(row_high, tap_high) + (dot(row_low, tap_high) + dot(row_high, tap_low))


def offsets(depth, width, shift):
    return (
        lax.broadcasted_iota(jnp.int32, (depth, width), 0)
        - lax.broadcasted_iota(jnp.int32, (depth, width), 1)
        - shift
    )


def filter_kernel(plan, place, blocks, width, rows_ref, *refs):
    tiles, outs, first_bin = plan
    outputs, (raw, smooth) = refs[:tiles], refs[tiles:]
    local, slices, bins = rows_ref.shape
    block_total = bins // LANES
    raw_blocks = raw.shape[1] // LANES
    smooth_blocks = smooth.shape[1] // LANES
    height = local * slices

    starts = []
    for turn in range(tiles):
        tile = lax.rem(place[1] - turn + tiles, tiles)
        for angle in range(local):
            start = blocks[place[0] + angle, tile]
            starts.append(start)
            at = turn * height + angle * slices
            for j in range(raw_blocks):
                block = start - 2 + j
                held = jnp.clip(block, 0, block_total - 1)
                lanes = pl.ds(pl.multiple_of(held * LANES, LANES), LANES)
                value = rows_ref[angle, :, lanes]
                inside = jnp.logical_and(block >= 0, block < block_total)
                raw[at : at + slices, j * LANES : (j + 1) * LANES] = jnp.where(inside, value, 0.0)

    decay = width[0]
    steps = (lax.broadcasted_iota(jnp.int32, (1, BAND), 1) + 1).astype(jnp.float32)
    total = 1.0 + 2.0 * jnp.sum(jnp.exp(-steps / decay), axis=1, keepdims=True)
    away = offsets(2 * 256, 256, BAND)
    spread = jnp.abs(away)
    paganin = jnp.where(
        spread <= BAND, jnp.exp(-spread.astype(jnp.float32) / decay) / total, 0.0
    )
    paganin = split(paganin)
    high, low = split(raw[...])
    for pair in range(smooth_blocks // 2):
        at = slice(pair * 256, pair * 256 + 512)
        smooth[:, pair * 256 : (pair + 1) * 256] = three_dots(
            (high[:, at], low[:, at]), paganin
        )
    for index, start in enumerate(starts):
        at = slice(index * slices, (index + 1) * slices)
        for j in range(smooth_blocks):
            if 1 <= j <= WIN // LANES:
                continue
            block = start - 1 + j
            inside = jnp.logical_and(block >= 0, block < block_total)
            lanes = slice(j * LANES, (j + 1) * LANES)
            smooth[at, lanes] = jnp.where(inside, smooth[at, lanes], 0.0)

    away = offsets(512, LANES, BAND + first_bin)
    spread = jnp.abs(away)
    squared = jnp.maximum(spread * spread, 1).astype(jnp.float32)
    odd = jnp.logical_and(spread <= BAND, (spread & 1) == 1)
    ramp = jnp.where(odd, -1.0 / (math.pi * math.pi * squared), 0.0)
    ramp = split(jnp.where(away == 0, 0.25, ramp))
    high, low = split(smooth[...])
    for j in range(outs):
        at = slice(j * LANES, j * LANES + 512)
        value = three_dots((high[:, at], low[:, at]), ramp)
        for turn in range(tiles):
            outputs[turn][:, j * LANES : (j + 1) * LANES] = value[
                turn * height : (turn + 1) * height
            ].astype(jnp.bfloat16)


def project_kernel(plan, place, table, *refs):
    segments, spots, tiles, local, slices, first_bin, tile_rows = plan
    groups = segments * spots
    pieces = refs[: groups * tiles]
    out, held = refs[groups * tiles], refs[groups * tiles + 1]
    angle_total = groups * local
    lane_blocks = held.shape[3] // LANES
    pixels = ROWS_DEV * CHUNK
    slice_total = slices * tiles

    for group in range(groups):
        for turn in range(tiles):
            piece = pieces[group * tiles + turn][...].astype(jnp.float32)
            for angle in range(local):
                held[group, angle, turn * slices : (turn + 1) * slices, :] = piece[
                    angle * slices : (angle + 1) * slices
                ]

    segment, spot, my_tile = place[0], place[1], place[2]
    first_row = ((segment * spots + spot) * ROWS_DEV).astype(jnp.float32) - (tile_rows - 1) / 2.0
    lane = lax.broadcasted_iota(jnp.int32, (8, pixels), 1)
    depth_step = lax.broadcasted_iota(jnp.int32, (8, pixels), 0).astype(jnp.float32)
    y = (lane // CHUNK).astype(jnp.float32) + first_row
    x_in_chunk = (lane % CHUNK).astype(jnp.float32)
    window_lane = lax.broadcasted_iota(jnp.int32, (slice_total, LANES), 1)
    gap = jnp.zeros((LANES - DEPTH, pixels), jnp.bfloat16)
    half = (WIN / 2.0) - first_bin

    sums = []
    for chunk in range(TCOLS // CHUNK):
        left = chunk * CHUNK - (TCOLS - 1) / 2.0
        right = left + CHUNK - 1
        x = x_in_chunk + left

        def step(group, total, x=x, left=left, right=right):
            from_segment = lax.rem(segment + group // spots, segments)
            from_spot = lax.rem(spot + lax.rem(group, spots), spots)
            source = (from_segment * spots + from_spot) * local
            windows, hats = [], []
            for angle in range(local):
                cosine = table[source + angle]
                sine = table[angle_total + source + angle]
                bottom = jnp.minimum(cosine * left, cosine * right) + jnp.minimum(
                    sine * first_row, sine * (first_row + (ROWS_DEV - 1))
                )
                low = (bottom + (half - 0.01)).astype(jnp.int32)
                block = low // LANES
                turn_by = (LANES - (low - block * LANES)) & (LANES - 1)
                near = pl.ds(pl.multiple_of(block * LANES, LANES), LANES)
                after = jnp.minimum(block + 1, lane_blocks - 1)
                far = pl.ds(pl.multiple_of(after * LANES, LANES), LANES)
                near = pltpu.roll(held[group, angle, :, near], turn_by, 1)
                far = pltpu.roll(held[group, angle, :, far], turn_by, 1)
                cut = jnp.where(turn_by == 0, LANES, turn_by)
                windows.append(jnp.where(window_lane < cut, near, far).astype(jnp.bfloat16))
                across = x * cosine + y * sine + (half - low.astype(jnp.float32)) - depth_step
                for j in range(DEPTH // 8):
                    hats.append(jnp.maximum(0.0, 1.0 - jnp.abs(across - 8.0 * j)))
                hats[-(DEPTH // 8) :] = [
                    jnp.concatenate(hats[-(DEPTH // 8) :], axis=0).astype(jnp.bfloat16),
                    gap,
                ]
            return total + jnp.dot(
                jnp.concatenate(windows, axis=1),
                jnp.concatenate(hats, axis=0),
                preferred_element_type=jnp.float32,
            )

        sums.append(lax.fori_loop(0, groups, step, jnp.zeros((slice_total, pixels), jnp.float32)))

    for pair in range(TCOLS // LANES):
        parts = sums[pair * (LANES // CHUNK) : (pair + 1) * (LANES // CHUNK)]
        for row in range(ROWS_DEV):
            value = jnp.concatenate(
                [part[:, row * CHUNK : (row + 1) * CHUNK] for part in parts], axis=1
            )
            at = row * TCOLS + pair * LANES
            if slices % 8 == 0:
                for turn in range(tiles):
                    tile = lax.rem(my_tile + turn, tiles)
                    into = pl.ds(pl.multiple_of(tile * slices, slices), slices)
                    out[0, into, at : at + LANES] = value[turn * slices : (turn + 1) * slices]
            else:
                out[0, :, at : at + LANES] = pltpu.roll(value, my_tile * slices, 0)


def shifted(value, axis, by):
    size = lax.axis_size(axis)
    return lax.ppermute(value, axis, [(i, (i - by) % size) for i in range(size)])


def body(sinogram, paganin_width, window_block):
    local, slices, bins = sinogram.shape
    segments, spots, tiles = (lax.axis_size(name) for name in ("segment", "angle", "tile"))
    segment, spot, tile = (lax.axis_index(name) for name in ("segment", "angle", "tile"))
    groups = segments * spots
    angle_total = local * groups
    tile_rows = ROWS_DEV * groups
    reach = math.hypot((TCOLS - 1) / 2, (tile_rows - 1) / 2)
    first_bin = max(0, int(WIN / 2 - reach - 0.01)) // 16 * 16
    last_bin = min(WIN - 1, int(WIN / 2 + reach + 0.01) + 1)
    outs = -(-(last_bin + 1 - first_bin) // LANES)
    assert first_bin + (outs - 1) * LANES < WIN and first_bin < LANES
    smooth_blocks = -(-(outs + 3) // 2) * 2

    smem = pl.BlockSpec(memory_space=pltpu.SMEM)
    vmem = pl.BlockSpec(memory_space=pltpu.VMEM)
    place = jnp.stack([(segment * spots + spot) * local, tile]).astype(jnp.int32)
    height = local * slices
    cut = pl.pallas_call(
        functools.partial(filter_kernel, (tiles, outs, first_bin)),
        out_shape=[jax.ShapeDtypeStruct((height, outs * LANES), jnp.bfloat16)] * tiles,
        in_specs=[smem, smem, smem, vmem],
        out_specs=[vmem] * tiles,
        scratch_shapes=[
            pltpu.VMEM((height * tiles, (smooth_blocks + 2) * LANES), jnp.float32),
            pltpu.VMEM((height * tiles, smooth_blocks * LANES), jnp.float32),
        ],
        compiler_params=pltpu.CompilerParams(vmem_limit_bytes=32 * 1024 * 1024),
        name="filter",
    )(place, window_block, paganin_width, sinogram)

    own = [cut[0]] + [shifted(cut[turn], "tile", turn) for turn in range(1, tiles)]
    own = jnp.stack(own)
    parts = [own] + [shifted(own, "angle", by) for by in range(1, spots)]
    everything = []
    for by in range(segments):
        everything += [part if by == 0 else shifted(part, "segment", by) for part in parts]
    pieces = [part[turn] for part in everything for turn in range(tiles)]

    theta = math.pi * np.arange(angle_total, dtype=np.float32) / np.float32(angle_total)
    table = np.concatenate([np.cos(theta), np.sin(theta)]).astype(np.float32)
    place = jnp.stack([segment, spot, tile]).astype(jnp.int32)
    plan = (segments, spots, tiles, local, slices, first_bin, tile_rows)
    return pl.pallas_call(
        functools.partial(project_kernel, plan),
        out_shape=jax.ShapeDtypeStruct((1, slices * tiles, ROWS_DEV * TCOLS), jnp.float32),
        in_specs=[smem, smem] + [vmem] * len(pieces),
        out_specs=vmem,
        scratch_shapes=[
            pltpu.VMEM((groups, local, slices * tiles, outs * LANES), jnp.float32),
        ],
        compiler_params=pltpu.CompilerParams(vmem_limit_bytes=32 * 1024 * 1024),
        name="project",
    )(place, jnp.asarray(table), *pieces)


def solution(mesh):
    in_specs = (P(("segment", "angle"), "tile", None), P(), P())
    out_specs = P("tile", None, ("segment", "angle"))
    return jax.shard_map(body, mesh=mesh, in_specs=in_specs, out_specs=out_specs, check_vma=False)
```

```python
import functools
import math

import jax
import jax.numpy as jnp
import numpy as np
from jax import lax
from jax.experimental import pallas as pl
from jax.experimental.pallas import tpu as pltpu
from jax.sharding import PartitionSpec as P

WIN = 512
BAND = 128
ROWS_DEV = 8
TCOLS = 256
LANES = 128
CHUNK = 64
DEPTH = 80


def split(value):
    high = value.astype(jnp.bfloat16)
    return high, (value - high.astype(jnp.float32)).astype(jnp.bfloat16)


def three_dots(rows, taps):
    (row_high, row_low), (tap_high, tap_low) = rows, taps
    dot = functools.partial(jnp.dot, preferred_element_type=jnp.float32)
    return dot(row_high, tap_high) + (dot(row_low, tap_high) + dot(row_high, tap_low))


def offsets(depth, width, shift):
    return (
        lax.broadcasted_iota(jnp.int32, (depth, width), 0)
        - lax.broadcasted_iota(jnp.int32, (depth, width), 1)
        - shift
    )


def filter_kernel(plan, place, blocks, width, rows_ref, *refs):
    outs, first_bin = plan
    output, raw, smooth = refs
    spots, tiles = output.shape[:2]
    local, slices, bins = rows_ref.shape
    block_total = bins // LANES
    raw_blocks = raw.shape[1] // LANES
    smooth_blocks = smooth.shape[1] // LANES
    height = local * slices

    starts = []
    for turn in range(tiles):
        for angle in range(local):
            start = blocks[(place[0] * spots + place[1]) * local + angle, turn]
            starts.append(start)
            at = turn * height + angle * slices
            for j in range(raw_blocks):
                block = start - 2 + j
                held = jnp.clip(block, 0, block_total - 1)
                lanes = pl.ds(pl.multiple_of(held * LANES, LANES), LANES)
                value = rows_ref[angle, :, lanes]
                inside = jnp.logical_and(block >= 0, block < block_total)
                raw[at : at + slices, j * LANES : (j + 1) * LANES] = jnp.where(inside, value, 0.0)

    decay = width[0]
    steps = (lax.broadcasted_iota(jnp.int32, (1, BAND), 1) + 1).astype(jnp.float32)
    total = 1.0 + 2.0 * jnp.sum(jnp.exp(-steps / decay), axis=1, keepdims=True)
    away = offsets(2 * 256, 256, BAND)
    spread = jnp.abs(away)
    paganin = jnp.where(
        spread <= BAND, jnp.exp(-spread.astype(jnp.float32) / decay) / total, 0.0
    )
    paganin = split(paganin)
    high, low = split(raw[...])
    for pair in range(smooth_blocks // 2):
        at = slice(pair * 256, pair * 256 + 512)
        smooth[:, pair * 256 : (pair + 1) * 256] = three_dots(
            (high[:, at], low[:, at]), paganin
        )
    for index, start in enumerate(starts):
        at = slice(index * slices, (index + 1) * slices)
        for j in range(smooth_blocks):
            if 1 <= j <= WIN // LANES:
                continue
            block = start - 1 + j
            inside = jnp.logical_and(block >= 0, block < block_total)
            lanes = slice(j * LANES, (j + 1) * LANES)
            smooth[at, lanes] = jnp.where(inside, smooth[at, lanes], 0.0)

    away = offsets(512, LANES, BAND + first_bin)
    spread = jnp.abs(away)
    squared = jnp.maximum(spread * spread, 1).astype(jnp.float32)
    odd = jnp.logical_and(spread <= BAND, (spread & 1) == 1)
    ramp = jnp.where(odd, -1.0 / (math.pi * math.pi * squared), 0.0)
    ramp = split(jnp.where(away == 0, 0.25, ramp))
    high, low = split(smooth[...])
    for j in range(outs):
        at = slice(j * LANES, j * LANES + 512)
        value = three_dots((high[:, at], low[:, at]), ramp)
        for turn in range(tiles):
            part = value[turn * height : (turn + 1) * height].astype(jnp.bfloat16)
            for spot in range(spots):
                output[spot, turn, :, j * LANES : (j + 1) * LANES] = part


def geometry(place, sizes, angle_total):
    spots, first_bin, tile_rows = sizes
    first_row = ((place[0] * spots + place[1]) * ROWS_DEV).astype(jnp.float32) - (
        tile_rows - 1
    ) / 2.0
    half = (WIN / 2.0) - first_bin

    def lowest(cosine, sine, left):
        right = left + (CHUNK - 1)
        bottom = jnp.minimum(cosine * left, cosine * right) + jnp.minimum(
            sine * first_row, sine * (first_row + (ROWS_DEV - 1))
        )
        return (bottom + (half - 0.01)).astype(jnp.int32)

    return first_row, half, lowest


def chunk_left(chunk):
    return chunk * CHUNK - (TCOLS - 1) / 2.0


def angle_at(place, sizes, segments, part, index, local):
    segment = lax.rem(place[0] + part, segments)
    return segment * (sizes[0] * local) + index


def hat_kernel(plan, place, table, hats):
    sizes, local = plan
    segments, chunks, depth, pixels = hats.shape
    count = depth // LANES
    angle_total = segments * count
    first_row, half, lowest = geometry(place, sizes, angle_total)
    lane = lax.broadcasted_iota(jnp.int32, (8, pixels), 1)
    depth_step = lax.broadcasted_iota(jnp.int32, (8, pixels), 0).astype(jnp.float32)
    y = (lane // CHUNK).astype(jnp.float32) + first_row
    x = (lane % CHUNK).astype(jnp.float32)
    gap = jnp.zeros((LANES - DEPTH, pixels), jnp.bfloat16)
    for part in range(segments):

        def step(index, carry, part=part):
            angle = angle_at(place, sizes, segments, part, index, local)
            cosine, sine = table[angle], table[angle_total + angle]
            at = pl.multiple_of(index * LANES, LANES)
            for chunk in range(chunks):
                left = chunk_left(chunk)
                low = lowest(cosine, sine, left)
                across = (x + left) * cosine + y * sine + (half - low.astype(jnp.float32))
                across = across - depth_step
                rows = [
                    jnp.maximum(0.0, 1.0 - jnp.abs(across - 8.0 * j)) for j in range(DEPTH // 8)
                ]
                hats[part, chunk, pl.ds(at, DEPTH), :] = jnp.concatenate(rows, axis=0).astype(
                    jnp.bfloat16
                )
                hats[part, chunk, pl.ds(at + DEPTH, LANES - DEPTH), :] = gap
            return carry

        lax.fori_loop(0, count, step, 0)


def project_kernel(plan, place, table, windows, hats, *refs):
    sizes, local, part, last = plan
    before, (out, held, near_rows) = refs[:-3], refs[-3:]
    segments, chunks, depth, pixels = hats.shape
    spots, tiles = windows.shape[:2]
    slices = windows.shape[2] // local
    count = depth // LANES
    angle_total = segments * count
    lane_blocks = windows.shape[3] // LANES
    first_row, half, lowest = geometry(place, sizes, angle_total)
    for spot in range(spots):
        for turn in range(tiles):
            piece = windows[spot, turn].astype(jnp.float32)
            for angle in range(local):
                held[spot * local + angle, turn * slices : (turn + 1) * slices, :] = piece[
                    angle * slices : (angle + 1) * slices
                ]
    window_lane = lax.broadcasted_iota(jnp.int32, (slices * tiles, LANES), 1)

    def step(index, carry):
        angle = angle_at(place, sizes, segments, part, index, local)
        cosine, sine = table[angle], table[angle_total + angle]
        at = pl.ds(pl.multiple_of(index * LANES, LANES), LANES)
        for chunk in range(chunks):
            low = lowest(cosine, sine, chunk_left(chunk))
            block = low // LANES
            turn_by = (LANES - (low - block * LANES)) & (LANES - 1)
            near = pl.ds(pl.multiple_of(block * LANES, LANES), LANES)
            after = jnp.minimum(block + 1, lane_blocks - 1)
            far = pl.ds(pl.multiple_of(after * LANES, LANES), LANES)
            near = pltpu.roll(held[index, :, near], turn_by, 1)
            far = pltpu.roll(held[index, :, far], turn_by, 1)
            cut = jnp.where(turn_by == 0, LANES, turn_by)
            near_rows[chunk, :, at] = jnp.where(window_lane < cut, near, far).astype(jnp.bfloat16)
        return carry

    lax.fori_loop(0, count, step, 0, unroll=2)
    sums = []
    for chunk in range(chunks):
        value = jnp.dot(near_rows[chunk], hats[part, chunk], preferred_element_type=jnp.float32)
        if before:
            value = value + before[0][chunk]
        sums.append(value)
        if not last:
            out[chunk] = value
    if not last:
        return
    for pair in range(TCOLS // LANES):
        parts = sums[pair * (LANES // CHUNK) : (pair + 1) * (LANES // CHUNK)]
        for row in range(ROWS_DEV):
            at = row * TCOLS + pair * LANES
            out[0, :, at : at + LANES] = jnp.concatenate(
                [value[:, row * CHUNK : (row + 1) * CHUNK] for value in parts], axis=1
            )


def shifted(value, axis, by):
    size = lax.axis_size(axis)
    return lax.ppermute(value, axis, [(i, (i - by) % size) for i in range(size)])


def body(sinogram, paganin_width, window_block):
    local, slices, bins = sinogram.shape
    segments, spots, tiles = (lax.axis_size(name) for name in ("segment", "angle", "tile"))
    segment, spot = lax.axis_index("segment"), lax.axis_index("angle")
    groups = segments * spots
    angle_total = local * groups
    tile_rows = ROWS_DEV * groups
    reach = math.hypot((TCOLS - 1) / 2, (tile_rows - 1) / 2)
    first_bin = max(0, int(WIN / 2 - reach - 0.01)) // 16 * 16
    last_bin = min(WIN - 1, int(WIN / 2 + reach + 0.01) + 1)
    outs = -(-(last_bin + 1 - first_bin) // LANES)
    assert first_bin + (outs - 1) * LANES < WIN and first_bin < LANES
    smooth_blocks = -(-(outs + 3) // 2) * 2

    smem = pl.BlockSpec(memory_space=pltpu.SMEM)
    vmem = pl.BlockSpec(memory_space=pltpu.VMEM)
    hat_bytes = angle_total * LANES * ROWS_DEV * TCOLS * 2
    params = pltpu.CompilerParams(vmem_limit_bytes=hat_bytes + 12 * 1024 * 1024)
    place = jnp.stack([segment, spot]).astype(jnp.int32)
    height = local * slices
    cut = pl.pallas_call(
        functools.partial(filter_kernel, (outs, first_bin)),
        out_shape=jax.ShapeDtypeStruct((spots, tiles, height, outs * LANES), jnp.bfloat16),
        in_specs=[smem, smem, smem, vmem],
        out_specs=vmem,
        scratch_shapes=[
            pltpu.VMEM((height * tiles, (smooth_blocks + 2) * LANES), jnp.float32),
            pltpu.VMEM((height * tiles, smooth_blocks * LANES), jnp.float32),
        ],
        compiler_params=params,
        name="filter",
    )(place, window_block, paganin_width, sinogram)

    theta = math.pi * np.arange(angle_total, dtype=np.float32) / np.float32(angle_total)
    table = jnp.asarray(np.concatenate([np.cos(theta), np.sin(theta)]).astype(np.float32))
    sizes = (spots, first_bin, tile_rows)
    chunks, pixels = TCOLS // CHUNK, ROWS_DEV * CHUNK
    depth = spots * local * LANES
    hats = pl.pallas_call(
        functools.partial(hat_kernel, (sizes, local)),
        out_shape=jax.ShapeDtypeStruct((segments, chunks, depth, pixels), jnp.bfloat16),
        in_specs=[smem, smem],
        out_specs=vmem,
        compiler_params=params,
        cost_estimate=pl.CostEstimate(
            flops=segments * chunks * depth * pixels * 8, bytes_accessed=0, transcendentals=0
        ),
        name="hats",
    )(place, table)

    pieces = cut.reshape(spots * tiles, height, outs * LANES)
    pieces = lax.all_to_all(pieces, ("angle", "tile"), 0, 0, tiled=True)
    pieces = pieces.reshape(cut.shape)
    parts = [pieces] + [shifted(pieces, "segment", by) for by in range(1, segments)]
    sums = ()
    for part, windows in enumerate(parts):
        last = part == segments - 1
        sums = pl.pallas_call(
            functools.partial(project_kernel, (sizes, local, part, last)),
            out_shape=jax.ShapeDtypeStruct(
                (1, slices * tiles, ROWS_DEV * TCOLS)
                if last
                else (chunks, slices * tiles, pixels),
                jnp.float32,
            ),
            in_specs=[smem, smem] + [vmem] * (2 + len(sums)),
            out_specs=vmem,
            scratch_shapes=[
                pltpu.VMEM((spots * local, slices * tiles, outs * LANES), jnp.float32),
                pltpu.VMEM((chunks, slices * tiles, depth), jnp.bfloat16),
            ],
            compiler_params=params,
            cost_estimate=pl.CostEstimate(
                flops=16 * slices * tiles * chunks * depth * pixels,
                bytes_accessed=0,
                transcendentals=0,
            ),
            name="project",
        )(place, table, windows, hats, *sums)
        sums = (sums,)
    return sums[0]


def solution(mesh):
    in_specs = (P(("segment", "angle"), "tile", None), P(), P())
    out_specs = P("tile", None, ("segment", "angle"))
    return jax.shard_map(body, mesh=mesh, in_specs=in_specs, out_specs=out_specs, check_vma=False)
```

```python
import functools
import math

import jax
import jax.numpy as jnp
import numpy as np
from jax import lax
from jax.experimental import pallas as pl
from jax.experimental.pallas import tpu as pltpu
from jax.sharding import PartitionSpec as P

WIN = 512
BAND = 128
ROWS_DEV = 8
TCOLS = 256
LANES = 128
CHUNK = 32
DEPTH = 48
SLOT = 64
PER = LANES // SLOT


def split(value):
    high = value.astype(jnp.bfloat16)
    return high, (value - high.astype(jnp.float32)).astype(jnp.bfloat16)


def three_dots(rows, taps):
    (row_high, row_low), (tap_high, tap_low) = rows, taps
    dot = functools.partial(jnp.dot, preferred_element_type=jnp.float32)
    return dot(row_high, tap_high) + (dot(row_low, tap_high) + dot(row_high, tap_low))


def offsets(depth, width, shift):
    return (
        lax.broadcasted_iota(jnp.int32, (depth, width), 0)
        - lax.broadcasted_iota(jnp.int32, (depth, width), 1)
        - shift
    )


def filter_kernel(plan, blocks, width, rows_ref, *refs):
    tiles, outs, first_bin = plan
    outputs, (padded, raw, smooth, arrived) = refs[:tiles], refs[tiles:]
    local, slices, bins = rows_ref.shape
    block_total = bins // LANES
    raw_wide = raw.shape[1]
    smooth_blocks = smooth.shape[1] // LANES
    height = local * slices
    ahead = 2 * LANES

    copies = [
        pltpu.make_async_copy(
            rows_ref.at[angle], padded.at[angle, :, pl.ds(ahead, bins)], arrived.at[angle]
        )
        for angle in range(local)
    ]
    for copy in copies:
        copy.start()
    behind = padded.shape[2] - ahead - bins
    padded[:, :, :ahead] = jnp.zeros((local, slices, ahead), jnp.float32)
    padded[:, :, ahead + bins :] = jnp.zeros((local, slices, behind), jnp.float32)

    decay = width[0]
    steps = (lax.broadcasted_iota(jnp.int32, (1, BAND), 1) + 1).astype(jnp.float32)
    total = 1.0 + 2.0 * jnp.sum(jnp.exp(-steps / decay), axis=1, keepdims=True)
    away = offsets(2 * 256, 256, BAND)
    spread = jnp.abs(away)
    paganin = jnp.where(
        spread <= BAND, jnp.exp(-spread.astype(jnp.float32) / decay) / total, 0.0
    )
    paganin = split(paganin)
    away = offsets(512, LANES, BAND + first_bin)
    spread = jnp.abs(away)
    squared = jnp.maximum(spread * spread, 1).astype(jnp.float32)
    odd = jnp.logical_and(spread <= BAND, (spread & 1) == 1)
    ramp = jnp.where(odd, -1.0 / (math.pi * math.pi * squared), 0.0)
    ramp = split(jnp.where(away == 0, 0.25, ramp))

    for copy in copies:
        copy.wait()
    first = (lax.axis_index("segment") * lax.axis_size("angle") + lax.axis_index("angle")) * local
    mine = lax.axis_index("tile")
    starts = []
    for turn in range(tiles):
        tile = lax.rem(mine - turn + tiles, tiles)
        for angle in range(local):
            start = blocks[tile, first + angle]
            starts.append(start)
            at = (turn * local + angle) * slices
            lanes = pl.ds(pl.multiple_of(start * LANES, LANES), raw_wide)
            raw[at : at + slices, :] = padded[angle, :, lanes]
    high, low = split(raw[...])
    for pair in range(smooth_blocks // 2):
        at = slice(pair * 256, pair * 256 + 512)
        smooth[:, pair * 256 : (pair + 1) * 256] = three_dots(
            (high[:, at], low[:, at]), paganin
        )
    for index, start in enumerate(starts):
        at = slice(index * slices, (index + 1) * slices)
        for j in range(smooth_blocks):
            if 1 <= j <= WIN // LANES:
                continue
            block = start - 1 + j
            inside = jnp.logical_and(block >= 0, block < block_total)
            lanes = slice(j * LANES, (j + 1) * LANES)
            smooth[at, lanes] = jnp.where(inside, smooth[at, lanes], 0.0)
    high, low = split(smooth[...])
    for j in range(outs):
        at = slice(j * LANES, j * LANES + 512)
        value = three_dots((high[:, at], low[:, at]), ramp)
        for turn in range(tiles):
            part = value[turn * height : (turn + 1) * height]
            outputs[turn][:, j * LANES : (j + 1) * LANES] = part.astype(jnp.bfloat16)


def hat_kernel(plan, trig, lows, hats):
    from_part, half, tile_rows, angle_total = plan
    parts, chunks, depth, pixels = hats.shape
    count = depth // SLOT
    place = lax.axis_index("segment") * lax.axis_size("angle") + lax.axis_index("angle")
    first_row = (place * ROWS_DEV).astype(jnp.float32) - (tile_rows - 1) / 2.0
    lane = lax.broadcasted_iota(jnp.int32, (8, pixels), 1)
    depth_step = lax.broadcasted_iota(jnp.int32, (8, pixels), 0).astype(jnp.float32)
    y = (lane // CHUNK).astype(jnp.float32) + first_row
    x = (lane % CHUNK).astype(jnp.float32)
    gap = jnp.zeros((SLOT - DEPTH, pixels), jnp.bfloat16)
    for part in range(parts):

        def step(index, carry, part=part):
            angle = (from_part + part) * count + index
            cosine, sine = trig[angle], trig[angle_total + angle]
            at = pl.multiple_of(index * SLOT, SLOT)
            for chunk in range(chunks):
                left = chunk * CHUNK - (TCOLS - 1) / 2.0
                low = lows[angle * chunks + chunk].astype(jnp.float32)
                across = (x + left) * cosine + y * sine + (half - low) - depth_step
                rows = [
                    jnp.maximum(0.0, 1.0 - jnp.abs(across - 8.0 * j)) for j in range(DEPTH // 8)
                ]
                rows = jnp.concatenate(rows, axis=0).astype(jnp.bfloat16)
                hats[part, chunk, pl.ds(at, DEPTH), :] = rows
                hats[part, chunk, pl.ds(at + DEPTH, SLOT - DEPTH), :] = gap
            return carry

        lax.fori_loop(0, count, step, 0)


def project_kernel(plan, lows, windows, hats, *refs):
    part, hat_part, local, last = plan
    before, (out, held, cut) = refs[:-3], refs[-3:]
    chunks, depth, pixels = hats.shape[1:]
    sources, tiles, height, wide = windows.shape
    slices = height // local
    count = depth // SLOT
    lane_blocks = wide // LANES
    for source in range(sources):
        for turn in range(tiles):
            piece = windows[source, turn].astype(held.dtype)
            for angle in range(local):
                held[source * local + angle, turn * slices : (turn + 1) * slices, :] = piece[
                    angle * slices : (angle + 1) * slices
                ]
    lane = lax.broadcasted_iota(jnp.int32, (slices * tiles, LANES), 1)

    def step(pair, carry):
        for chunk in range(chunks):
            merged = None
            for spot in range(PER):
                index = pair * PER + spot
                low = lows[(part * count + index) * chunks + chunk]
                block = low // LANES
                past = low - block * LANES
                after = jnp.minimum(block + 1, lane_blocks - 1)
                near = pl.ds(pl.multiple_of(block * LANES, LANES), LANES)
                far = pl.ds(pl.multiple_of(after * LANES, LANES), LANES)
                value = jnp.where(lane >= past, held[index, :, near], held[index, :, far])
                turn_by = (spot * SLOT + LANES - past) & (LANES - 1)
                value = pltpu.roll(value, turn_by, 1)
                merged = value if spot == 0 else jnp.where(lane < spot * SLOT, merged, value)
            at = pl.ds(pl.multiple_of(pair * LANES, LANES), LANES)
            cut[chunk, :, at] = merged.astype(jnp.bfloat16)
        return carry

    lax.fori_loop(0, count // PER, step, 0, unroll=2)
    sums = []
    for chunk in range(chunks):
        value = jnp.dot(cut[chunk], hats[hat_part, chunk], preferred_element_type=jnp.float32)
        if before:
            value = value + before[0][chunk]
        sums.append(value)
        if not last:
            out[chunk] = value
    if not last:
        return
    mine = lax.axis_index("tile")
    for pair in range(TCOLS // LANES):
        near = sums[pair * (LANES // CHUNK) : (pair + 1) * (LANES // CHUNK)]
        for row in range(ROWS_DEV):
            value = jnp.concatenate(
                [part[:, row * CHUNK : (row + 1) * CHUNK] for part in near], axis=1
            )
            at = row * TCOLS + pair * LANES
            if slices % 8 == 0:
                for turn in range(tiles):
                    tile = lax.rem(mine + turn, tiles)
                    into = pl.ds(pl.multiple_of(tile * slices, slices), slices)
                    out[0, into, at : at + LANES] = value[turn * slices : (turn + 1) * slices]
            else:
                out[0, :, at : at + LANES] = pltpu.roll(value, mine * slices, 0)


def shifted(value, axis, by):
    size = lax.axis_size(axis)
    return lax.ppermute(value, axis, [(i, (i - by) % size) for i in range(size)])


def swapped(value, axis, by):
    return lax.ppermute(value, axis, [(i, i ^ by) for i in range(lax.axis_size(axis))])


def body(sinogram, paganin_width, window_block):
    local, slices, bins = sinogram.shape
    segments, spots, tiles = (lax.axis_size(name) for name in ("segment", "angle", "tile"))
    segment, spot = lax.axis_index("segment"), lax.axis_index("angle")
    groups = segments * spots
    angle_total = local * groups
    tile_rows = ROWS_DEV * groups
    reach = math.hypot((TCOLS - 1) / 2, (tile_rows - 1) / 2)
    first_bin = max(0, int(WIN / 2 - reach - 0.01)) // 16 * 16
    last_bin = min(WIN - 1, int(WIN / 2 + reach + 0.01) + 1)
    outs = -(-(last_bin + 1 - first_bin) // LANES)
    assert first_bin + (outs - 1) * LANES < WIN and first_bin < LANES
    assert spots & (spots - 1) == 0 and spots > 1
    smooth_blocks = -(-(outs + 3) // 2) * 2
    chunks, pixels = TCOLS // CHUNK, ROWS_DEV * CHUNK
    half = WIN / 2.0 - first_bin

    smem = pl.BlockSpec(memory_space=pltpu.SMEM)
    vmem = pl.BlockSpec(memory_space=pltpu.VMEM)
    hat_bytes = angle_total * SLOT * ROWS_DEV * TCOLS * 2
    params = pltpu.CompilerParams(vmem_limit_bytes=hat_bytes + 12 * 1024 * 1024)
    height = local * slices
    block_total = bins // LANES
    cut = pl.pallas_call(
        functools.partial(filter_kernel, (tiles, outs, first_bin)),
        out_shape=[jax.ShapeDtypeStruct((height, outs * LANES), jnp.bfloat16)] * tiles,
        in_specs=[smem, smem, pl.BlockSpec(memory_space=pltpu.HBM)],
        out_specs=[vmem] * tiles,
        scratch_shapes=[
            pltpu.VMEM(
                (local, slices, (block_total - WIN // LANES + smooth_blocks + 2) * LANES),
                jnp.float32,
            ),
            pltpu.VMEM((height * tiles, (smooth_blocks + 2) * LANES), jnp.float32),
            pltpu.VMEM((height * tiles, smooth_blocks * LANES), jnp.float32),
            pltpu.SemaphoreType.DMA((local,)),
        ],
        compiler_params=params,
        name="filter",
    )(window_block.T, paganin_width, sinogram)

    reached = [0]
    for bit in reversed(range(1, spots.bit_length() - 1)):
        reached += [other ^ (1 << bit) for other in reached]
    order = np.array([[other ^ swap for other in reached] for swap in (0, 1)], np.int32)
    order = np.repeat(order.reshape(-1), local), np.tile(np.arange(local), spots)
    where = np.arange(groups)[:, None]
    by = np.arange(segments)[:, None] + where[:, :, None] // spots
    angles = (where % spots ^ order[0]) * local + order[1]
    angles = by % segments * (spots * local) + angles[:, None]
    theta = math.pi * angles.reshape(groups, angle_total) / angle_total
    cosine, sine = np.cos(theta), np.sin(theta)
    left = np.arange(chunks) * CHUNK - (TCOLS - 1) / 2.0
    edges = np.minimum(cosine[..., None] * left, cosine[..., None] * (left + (CHUNK - 1)))
    top = where * ROWS_DEV - (tile_rows - 1) / 2.0
    rise = np.minimum(sine * top, sine * (top + (ROWS_DEV - 1)))
    lows = np.floor(edges + rise[..., None] + (half - 0.01)).astype(np.int32)
    mine = segment * spots + spot
    lows = jnp.asarray(lows.reshape(groups, -1))[mine]
    trig = jnp.asarray(np.concatenate([cosine, sine], axis=1).astype(np.float32))[mine]

    depth = spots * local // 2 * SLOT
    def hats_of(by, after):
        ready = lax.optimization_barrier((trig, lows, *after))[:2]
        return pl.pallas_call(
            functools.partial(hat_kernel, (2 * by, half, tile_rows, angle_total)),
            out_shape=jax.ShapeDtypeStruct((2, chunks, depth, pixels), jnp.bfloat16),
            in_specs=[smem, smem],
            out_specs=vmem,
            compiler_params=params,
            cost_estimate=pl.CostEstimate(
                flops=2 * chunks * depth * pixels * 16, bytes_accessed=0, transcendentals=0
            ),
            name="hats",
        )(*ready)

    arrived = [cut[0]] + [shifted(cut[turn], "tile", turn) for turn in range(1, tiles)]
    hats = [hats_of(0, cut)]
    arrived, hats[0] = lax.optimization_barrier((arrived, hats[0]))
    pieces = jnp.stack(arrived)[None]
    for bit in reversed(range(1, spots.bit_length() - 1)):
        sent = swapped(pieces, "angle", 1 << bit)
        if len(hats) < segments:
            hats.append(hats_of(len(hats), (pieces,)))
            sent, hats[-1] = lax.optimization_barrier((sent, hats[-1]))
        pieces = jnp.concatenate([pieces, sent])
    while len(hats) < segments:
        hats.append(hats_of(len(hats), (pieces,)))
    crossed = swapped(pieces, "angle", 1)
    parts = []
    for which, value in enumerate((pieces, crossed)):
        for by in range(segments):
            parts.append((by, which, value if by == 0 else shifted(value, "segment", by)))
    held_type = jnp.bfloat16 if slices % 16 == 0 else jnp.float32
    sums = ()
    for turn, (by, which, windows) in enumerate(parts):
        last = turn == len(parts) - 1
        sums = pl.pallas_call(
            functools.partial(project_kernel, (2 * by + which, which, local, last)),
            out_shape=jax.ShapeDtypeStruct(
                (1, slices * tiles, ROWS_DEV * TCOLS)
                if last
                else (chunks, slices * tiles, pixels),
                jnp.float32,
            ),
            in_specs=[smem] + [vmem] * (2 + len(sums)),
            out_specs=vmem,
            scratch_shapes=[
                pltpu.VMEM((spots * local // 2, slices * tiles, outs * LANES), held_type),
                pltpu.VMEM((chunks, slices * tiles, depth), jnp.bfloat16),
            ],
            compiler_params=params,
            cost_estimate=pl.CostEstimate(
                flops=32 * slices * tiles * chunks * depth * pixels,
                bytes_accessed=0,
                transcendentals=0,
            ),
            name="project",
        )(lows, windows, hats[by], *sums)
        sums = (sums,)
    return sums[0]


def solution(mesh):
    in_specs = (P(("segment", "angle"), "tile", None), P(), P())
    out_specs = P("tile", None, ("segment", "angle"))
    return jax.shard_map(body, mesh=mesh, in_specs=in_specs, out_specs=out_specs, check_vma=False)
```

```python
import functools
import math

import jax
import jax.numpy as jnp
import numpy as np
from jax import lax
from jax.experimental import pallas as pl
from jax.experimental.pallas import tpu as pltpu
from jax.sharding import PartitionSpec as P

WIN = 512
BAND = 128
ROWS_DEV = 8
TCOLS = 256
LANES = 128
CHUNK = 32
DEPTH = 48
SLOT = 64
PER = LANES // SLOT


def split(value):
    high = value.astype(jnp.bfloat16)
    return high, (value - high.astype(jnp.float32)).astype(jnp.bfloat16)


def three_dots(rows, taps):
    (row_high, row_low), (tap_high, tap_low) = rows, taps
    dot = functools.partial(jnp.dot, preferred_element_type=jnp.float32)
    return dot(row_high, tap_high) + (dot(row_low, tap_high) + dot(row_high, tap_low))


def offsets(depth, width, shift):
    return (
        lax.broadcasted_iota(jnp.int32, (depth, width), 0)
        - lax.broadcasted_iota(jnp.int32, (depth, width), 1)
        - shift
    )


def filter_kernel(plan, width, blocks_ref, table, rows_ref, *refs):
    tiles, outs, first_bin = plan
    outputs, (info, blocks, padded, raw, smooth, arrived) = refs[:tiles], refs[tiles:]
    local, slices, bins = rows_ref.shape
    block_total = bins // LANES
    raw_wide = raw.shape[1]
    smooth_blocks = smooth.shape[1] // LANES
    height = local * slices
    ahead = 2 * LANES

    place = lax.axis_index("segment") * lax.axis_size("angle") + lax.axis_index("angle")
    copies = [
        pltpu.make_async_copy(blocks_ref, blocks, arrived.at[local]),
        pltpu.make_async_copy(table.at[place], info, arrived.at[local + 1]),
    ]
    copies += [
        pltpu.make_async_copy(
            rows_ref.at[angle], padded.at[angle, :, pl.ds(ahead, bins)], arrived.at[angle]
        )
        for angle in range(local)
    ]
    for copy in copies:
        copy.start()
    behind = padded.shape[2] - ahead - bins
    padded[:, :, :ahead] = jnp.zeros((local, slices, ahead), jnp.float32)
    padded[:, :, ahead + bins :] = jnp.zeros((local, slices, behind), jnp.float32)

    decay = width[0]
    steps = (lax.broadcasted_iota(jnp.int32, (1, BAND), 1) + 1).astype(jnp.float32)
    total = 1.0 + 2.0 * jnp.sum(jnp.exp(-steps / decay), axis=1, keepdims=True)
    away = offsets(2 * 256, 256, BAND)
    spread = jnp.abs(away)
    paganin = jnp.where(
        spread <= BAND, jnp.exp(-spread.astype(jnp.float32) / decay) / total, 0.0
    )
    paganin = split(paganin)
    away = offsets(512, LANES, BAND + first_bin)
    spread = jnp.abs(away)
    squared = jnp.maximum(spread * spread, 1).astype(jnp.float32)
    odd = jnp.logical_and(spread <= BAND, (spread & 1) == 1)
    ramp = jnp.where(odd, -1.0 / (math.pi * math.pi * squared), 0.0)
    ramp = split(jnp.where(away == 0, 0.25, ramp))

    for copy in copies:
        copy.wait()
    first = place * local
    mine = lax.axis_index("tile")
    starts = []
    for turn in range(tiles):
        tile = lax.rem(mine - turn + tiles, tiles)
        for angle in range(local):
            start = blocks[tile, first + angle]
            starts.append(start)
            at = (turn * local + angle) * slices
            lanes = pl.ds(pl.multiple_of(start * LANES, LANES), raw_wide)
            raw[at : at + slices, :] = padded[angle, :, lanes]
    high, low = split(raw[...])
    for pair in range(smooth_blocks // 2):
        at = slice(pair * 256, pair * 256 + 512)
        smooth[:, pair * 256 : (pair + 1) * 256] = three_dots(
            (high[:, at], low[:, at]), paganin
        )
    for index, start in enumerate(starts):
        at = slice(index * slices, (index + 1) * slices)
        for j in range(smooth_blocks):
            if 1 <= j <= WIN // LANES:
                continue
            block = start - 1 + j
            inside = jnp.logical_and(block >= 0, block < block_total)
            lanes = slice(j * LANES, (j + 1) * LANES)
            smooth[at, lanes] = jnp.where(inside, smooth[at, lanes], 0.0)
    high, low = split(smooth[...])
    for j in range(outs):
        at = slice(j * LANES, j * LANES + 512)
        value = three_dots((high[:, at], low[:, at]), ramp)
        for turn in range(tiles):
            part = value[turn * height : (turn + 1) * height]
            outputs[turn][:, j * LANES : (j + 1) * LANES] = part.astype(jnp.bfloat16)


def read(info, index):
    return info[index // LANES, index % LANES]


def hat_kernel(plan, info, hats):
    from_part, half, tile_rows, angle_total = plan
    parts, chunks, depth, pixels = hats.shape
    count = depth // SLOT
    place = lax.axis_index("segment") * lax.axis_size("angle") + lax.axis_index("angle")
    first_row = (place * ROWS_DEV).astype(jnp.float32) - (tile_rows - 1) / 2.0
    lane = lax.broadcasted_iota(jnp.int32, (8, pixels), 1)
    depth_step = lax.broadcasted_iota(jnp.int32, (8, pixels), 0).astype(jnp.float32)
    y = (lane // CHUNK).astype(jnp.float32) + first_row
    x = (lane % CHUNK).astype(jnp.float32)
    gap = jnp.zeros((SLOT - DEPTH, pixels), jnp.bfloat16)
    for part in range(parts):

        def step(index, carry, part=part):
            angle = (from_part + part) * count + index
            cosine, sine = read(info, angle), read(info, angle_total + angle)
            at = pl.multiple_of(index * SLOT, SLOT)
            for chunk in range(chunks):
                left = chunk * CHUNK - (TCOLS - 1) / 2.0
                low = read(info, 2 * angle_total + angle * chunks + chunk)
                across = (x + left) * cosine + y * sine + (half - low) - depth_step
                rows = [
                    jnp.maximum(0.0, 1.0 - jnp.abs(across - 8.0 * j)) for j in range(DEPTH // 8)
                ]
                rows = jnp.concatenate(rows, axis=0).astype(jnp.bfloat16)
                hats[part, chunk, pl.ds(at, DEPTH), :] = rows
                hats[part, chunk, pl.ds(at + DEPTH, SLOT - DEPTH), :] = gap
            return carry

        lax.fori_loop(0, count, step, 0)


def project_kernel(plan, info, windows, hats, *refs):
    part, hat_part, local, angle_total, last = plan
    before, (out, held, cut) = refs[:-3], refs[-3:]
    chunks, depth, pixels = hats.shape[1:]
    sources, tiles, height, wide = windows.shape
    slices = height // local
    count = depth // SLOT
    lane_blocks = wide // LANES
    for source in range(sources):
        for turn in range(tiles):
            piece = windows[source, turn].astype(held.dtype)
            for angle in range(local):
                held[source * local + angle, turn * slices : (turn + 1) * slices, :] = piece[
                    angle * slices : (angle + 1) * slices
                ]
    lane = lax.broadcasted_iota(jnp.int32, (slices * tiles, LANES), 1)

    def step(pair, carry):
        for chunk in range(chunks):
            merged = None
            for spot in range(PER):
                index = pair * PER + spot
                low = read(info, 2 * angle_total + (part * count + index) * chunks + chunk)
                low = low.astype(jnp.int32)
                block = low // LANES
                past = low - block * LANES
                after = jnp.minimum(block + 1, lane_blocks - 1)
                near = pl.ds(pl.multiple_of(block * LANES, LANES), LANES)
                far = pl.ds(pl.multiple_of(after * LANES, LANES), LANES)
                value = jnp.where(lane >= past, held[index, :, near], held[index, :, far])
                turn_by = (spot * SLOT + LANES - past) & (LANES - 1)
                value = pltpu.roll(value, turn_by, 1)
                merged = value if spot == 0 else jnp.where(lane < spot * SLOT, merged, value)
            at = pl.ds(pl.multiple_of(pair * LANES, LANES), LANES)
            cut[chunk, :, at] = merged.astype(jnp.bfloat16)
        return carry

    lax.fori_loop(0, count // PER, step, 0, unroll=4)
    sums = []
    for chunk in range(chunks):
        value = jnp.dot(cut[chunk], hats[hat_part, chunk], preferred_element_type=jnp.float32)
        if before:
            value = value + before[0][chunk]
        sums.append(value)
        if not last:
            out[chunk] = value
    if not last:
        return
    mine = lax.axis_index("tile")
    for pair in range(TCOLS // LANES):
        near = sums[pair * (LANES // CHUNK) : (pair + 1) * (LANES // CHUNK)]
        for row in range(ROWS_DEV):
            value = jnp.concatenate(
                [part[:, row * CHUNK : (row + 1) * CHUNK] for part in near], axis=1
            )
            at = row * TCOLS + pair * LANES
            if slices % 8 == 0:
                for turn in range(tiles):
                    tile = lax.rem(mine + turn, tiles)
                    into = pl.ds(pl.multiple_of(tile * slices, slices), slices)
                    out[0, into, at : at + LANES] = value[turn * slices : (turn + 1) * slices]
            else:
                out[0, :, at : at + LANES] = pltpu.roll(value, mine * slices, 0)


def shifted(value, axis, by):
    size = lax.axis_size(axis)
    return lax.ppermute(value, axis, [(i, (i - by) % size) for i in range(size)])


def swapped(value, axis, by):
    return lax.ppermute(value, axis, [(i, i ^ by) for i in range(lax.axis_size(axis))])


def body(sinogram, paganin_width, window_block):
    local, slices, bins = sinogram.shape
    segments, spots, tiles = (lax.axis_size(name) for name in ("segment", "angle", "tile"))
    segment, spot = lax.axis_index("segment"), lax.axis_index("angle")
    groups = segments * spots
    angle_total = local * groups
    tile_rows = ROWS_DEV * groups
    reach = math.hypot((TCOLS - 1) / 2, (tile_rows - 1) / 2)
    first_bin = max(0, int(WIN / 2 - reach - 0.01)) // 16 * 16
    last_bin = min(WIN - 1, int(WIN / 2 + reach + 0.01) + 1)
    outs = -(-(last_bin + 1 - first_bin) // LANES)
    assert first_bin + (outs - 1) * LANES < WIN and first_bin < LANES
    assert spots & (spots - 1) == 0 and spots > 1
    smooth_blocks = -(-(outs + 3) // 2) * 2
    chunks, pixels = TCOLS // CHUNK, ROWS_DEV * CHUNK
    half = WIN / 2.0 - first_bin

    smem = pl.BlockSpec(memory_space=pltpu.SMEM)
    vmem = pl.BlockSpec(memory_space=pltpu.VMEM)
    hat_bytes = angle_total * SLOT * ROWS_DEV * TCOLS * 2
    params = pltpu.CompilerParams(vmem_limit_bytes=hat_bytes + 12 * 1024 * 1024)
    height = local * slices
    block_total = bins // LANES
    reached = [0]
    for bit in reversed(range(1, spots.bit_length() - 1)):
        reached += [other ^ (1 << bit) for other in reached]
    order = np.array([[other ^ swap for other in reached] for swap in (0, 1)], np.int32)
    order = np.repeat(order.reshape(-1), local), np.tile(np.arange(local), spots)
    where = np.arange(groups)[:, None]
    by = np.arange(segments)[:, None] + where[:, :, None] // spots
    angles = (where % spots ^ order[0]) * local + order[1]
    angles = by % segments * (spots * local) + angles[:, None]
    theta = math.pi * angles.reshape(groups, angle_total) / angle_total
    cosine, sine = np.cos(theta), np.sin(theta)
    left = np.arange(chunks) * CHUNK - (TCOLS - 1) / 2.0
    edges = np.minimum(cosine[..., None] * left, cosine[..., None] * (left + (CHUNK - 1)))
    top = where * ROWS_DEV - (tile_rows - 1) / 2.0
    rise = np.minimum(sine * top, sine * (top + (ROWS_DEV - 1)))
    lows = np.floor(edges + rise[..., None] + (half - 0.01)).astype(np.int32)
    lows = lows.astype(np.float32).reshape(groups, -1)
    table = np.concatenate([cosine.astype(np.float32), sine.astype(np.float32), lows], axis=1)
    info_rows = -(-table.shape[1] // (8 * LANES)) * 8
    table = np.pad(table, ((0, 0), (0, info_rows * LANES - table.shape[1])))
    table = jnp.asarray(table.reshape(groups, info_rows, LANES))

    *cut, info = pl.pallas_call(
        functools.partial(filter_kernel, (tiles, outs, first_bin)),
        out_shape=[jax.ShapeDtypeStruct((height, outs * LANES), jnp.bfloat16)] * tiles
        + [jax.ShapeDtypeStruct((info_rows, LANES), jnp.float32)],
        in_specs=[smem] + [pl.BlockSpec(memory_space=pltpu.HBM)] * 3,
        out_specs=[vmem] * (tiles + 1),
        scratch_shapes=[
            pltpu.SMEM(window_block.T.shape, jnp.int32),
            pltpu.VMEM(
                (local, slices, (block_total - WIN // LANES + smooth_blocks + 2) * LANES),
                jnp.float32,
            ),
            pltpu.VMEM((height * tiles, (smooth_blocks + 2) * LANES), jnp.float32),
            pltpu.VMEM((height * tiles, smooth_blocks * LANES), jnp.float32),
            pltpu.SemaphoreType.DMA((local + 2,)),
        ],
        compiler_params=params,
        name="filter",
    )(
        paganin_width,
        *(pltpu.with_memory_space_constraint(v, pltpu.HBM) for v in (window_block.T, table, sinogram)),
    )

    depth = spots * local // 2 * SLOT
    def hats_of(by, after):
        ready = lax.optimization_barrier((info, *after))[0]
        return pl.pallas_call(
            functools.partial(hat_kernel, (2 * by, half, tile_rows, angle_total)),
            out_shape=jax.ShapeDtypeStruct((2, chunks, depth, pixels), jnp.bfloat16),
            in_specs=[smem],
            out_specs=vmem,
            compiler_params=params,
            cost_estimate=pl.CostEstimate(
                flops=2 * chunks * depth * pixels * 16, bytes_accessed=0, transcendentals=0
            ),
            name="hats",
        )(ready)

    arrived = [cut[0]] + [shifted(cut[turn], "tile", turn) for turn in range(1, tiles)]
    hats = [hats_of(0, cut)]
    arrived, hats[0] = lax.optimization_barrier((arrived, hats[0]))
    pieces = jnp.stack(arrived)[None]
    for bit in reversed(range(1, spots.bit_length() - 1)):
        sent = swapped(pieces, "angle", 1 << bit)
        if len(hats) < segments:
            hats.append(hats_of(len(hats), (pieces,)))
            sent, hats[-1] = lax.optimization_barrier((sent, hats[-1]))
        pieces = jnp.concatenate([pieces, sent])
    while len(hats) < segments:
        hats.append(hats_of(len(hats), (pieces,)))
    held_type = jnp.bfloat16 if slices % 16 == 0 else jnp.float32

    def project(by, which, windows, sums, last=False):
        value = pl.pallas_call(
            functools.partial(project_kernel, (2 * by + which, which, local, angle_total, last)),
            out_shape=jax.ShapeDtypeStruct(
                (1, slices * tiles, ROWS_DEV * TCOLS)
                if last
                else (chunks, slices * tiles, pixels),
                jnp.float32,
            ),
            in_specs=[smem] + [vmem] * (2 + len(sums)),
            out_specs=vmem,
            scratch_shapes=[
                pltpu.VMEM((spots * local // 2, slices * tiles, outs * LANES), held_type),
                pltpu.VMEM((chunks, slices * tiles, depth), jnp.bfloat16),
            ],
            compiler_params=params,
            cost_estimate=pl.CostEstimate(
                flops=32 * slices * tiles * chunks * depth * pixels,
                bytes_accessed=0,
                transcendentals=0,
            ),
            name="project",
        )(info, windows, hats[by], *sums)
        return (value,)

    crossed = swapped(pieces, "angle", 1)
    sums = project(0, 0, pieces, ())
    for by in range(1, segments):
        sums = project(by, 0, shifted(pieces, "segment", by), sums)
    crossed, sums = lax.optimization_barrier((crossed, sums))
    others = [shifted(crossed, "segment", by) for by in range(1, segments)]
    sums = project(0, 1, crossed, sums, segments == 1)
    for by in range(1, segments):
        sums = project(by, 1, others[by - 1], sums, by == segments - 1)
    return sums[0]


def solution(mesh):
    in_specs = (P(("segment", "angle"), "tile", None), P(), P())
    out_specs = P("tile", None, ("segment", "angle"))
    return jax.shard_map(body, mesh=mesh, in_specs=in_specs, out_specs=out_specs, check_vma=False)
```

```python
import functools
import math

import jax
import jax.numpy as jnp
import numpy as np
from jax import lax
from jax.experimental import pallas as pl
from jax.experimental.pallas import tpu as pltpu
from jax.sharding import PartitionSpec as P

WIN = 512
BAND = 128
ROWS_DEV = 8
TCOLS = 256
LANES = 128
LANE_BITS = 7
CHUNK = 32
DEPTH = 48
SLOT = 64
PER = LANES // SLOT


def split(value):
    high = value.astype(jnp.bfloat16)
    return high, (value - high.astype(jnp.float32)).astype(jnp.bfloat16)


def banded(value, taps, starts):
    tap_high, tap_low = taps
    dot = functools.partial(jnp.dot, preferred_element_type=jnp.float32)
    cut = [value[:, start : start + tap_high.shape[0]] for start in starts]
    high, low = split(jnp.concatenate(cut, axis=0))
    both = dot(jnp.concatenate([high, low], axis=0), tap_high)
    result = both[: high.shape[0]] + (both[high.shape[0] :] + dot(high, tap_low))
    rows = value.shape[0]
    return [result[index * rows : (index + 1) * rows] for index in range(len(starts))]


def offsets(depth, width, shift):
    return (
        lax.broadcasted_iota(jnp.int32, (depth, width), 0)
        - lax.broadcasted_iota(jnp.int32, (depth, width), 1)
        - shift
    )


def filter_kernel(plan, width, blocks_ref, table, rows_ref, *refs):
    tiles, outs, first_bin = plan
    outputs, (info, blocks, padded, raw, smooth, arrived) = refs[:tiles], refs[tiles:]
    local, slices, bins = rows_ref.shape
    block_total = bins // LANES
    raw_wide = raw.shape[1]
    smooth_blocks = smooth.shape[1] // LANES
    height = local * slices
    ahead = 2 * LANES

    place = lax.axis_index("segment") * lax.axis_size("angle") + lax.axis_index("angle")
    copies = [
        pltpu.make_async_copy(blocks_ref, blocks, arrived.at[local]),
        pltpu.make_async_copy(table.at[place], info, arrived.at[local + 1]),
    ]
    copies += [
        pltpu.make_async_copy(
            rows_ref.at[angle], padded.at[angle, :, pl.ds(ahead, bins)], arrived.at[angle]
        )
        for angle in range(local)
    ]
    for copy in copies:
        copy.start()
    behind = padded.shape[2] - ahead - bins
    padded[:, :, :ahead] = jnp.zeros((local, slices, ahead), jnp.float32)
    padded[:, :, ahead + bins :] = jnp.zeros((local, slices, behind), jnp.float32)

    decay = width[0]
    steps = (lax.broadcasted_iota(jnp.int32, (1, BAND), 1) + 1).astype(jnp.float32)
    total = 1.0 + 2.0 * jnp.sum(jnp.exp(-steps / decay), axis=1, keepdims=True)
    away = offsets(2 * 256, 256, BAND)
    spread = jnp.abs(away)
    paganin = jnp.where(
        spread <= BAND, jnp.exp(-spread.astype(jnp.float32) / decay) / total, 0.0
    )
    paganin = split(paganin)
    away = offsets(512, LANES, BAND + first_bin)
    spread = jnp.abs(away)
    squared = jnp.maximum(spread * spread, 1).astype(jnp.float32)
    odd = jnp.logical_and(spread <= BAND, (spread & 1) == 1)
    ramp = jnp.where(odd, -1.0 / (math.pi * math.pi * squared), 0.0)
    ramp = split(jnp.where(away == 0, 0.25, ramp))

    for copy in copies:
        copy.wait()
    first = place * local
    mine = lax.axis_index("tile")
    starts = []
    for turn in range(tiles):
        tile = lax.rem(mine - turn + tiles, tiles)
        for angle in range(local):
            start = blocks[tile, first + angle]
            starts.append(start)
            at = (turn * local + angle) * slices
            lanes = pl.ds(pl.multiple_of(start * LANES, LANES), raw_wide)
            raw[at : at + slices, :] = padded[angle, :, lanes]
    pairs = range(0, smooth_blocks * LANES, 256)
    for at, value in zip(pairs, banded(raw[...], paganin, pairs)):
        smooth[:, at : at + 256] = value
    for index, start in enumerate(starts):
        at = slice(index * slices, (index + 1) * slices)
        for j in range(smooth_blocks):
            if 1 <= j <= WIN // LANES:
                continue
            block = start - 1 + j
            inside = jnp.logical_and(block >= 0, block < block_total)
            lanes = slice(j * LANES, (j + 1) * LANES)
            smooth[at, lanes] = jnp.where(inside, smooth[at, lanes], 0.0)
    lanes = range(0, outs * LANES, LANES)
    for j, value in enumerate(banded(smooth[...], ramp, lanes)):
        for turn in range(tiles):
            part = value[turn * height : (turn + 1) * height]
            outputs[turn][:, j * LANES : (j + 1) * LANES] = part.astype(jnp.bfloat16)


def read(info, index):
    return info[index >> LANE_BITS, index & (LANES - 1)]


def hat_kernel(plan, info, hats):
    part, half, tile_rows, angle_total = plan
    chunks, depth, pixels = hats.shape
    count = depth // SLOT
    place = lax.axis_index("segment") * lax.axis_size("angle") + lax.axis_index("angle")
    first_row = (place * ROWS_DEV).astype(jnp.float32) - (tile_rows - 1) / 2.0
    lane = lax.broadcasted_iota(jnp.int32, (8, pixels), 1)
    depth_step = lax.broadcasted_iota(jnp.int32, (8, pixels), 0).astype(jnp.float32)
    y = (lane // CHUNK).astype(jnp.float32) + first_row
    x = (lane % CHUNK).astype(jnp.float32)
    gap = jnp.zeros((SLOT - DEPTH, pixels), jnp.bfloat16)

    def step(index, carry):
        angle = part * count + index
        cosine, sine = read(info, angle), read(info, angle_total + angle)
        at = pl.multiple_of(index * SLOT, SLOT)
        for chunk in range(chunks):
            left = chunk * CHUNK - (TCOLS - 1) / 2.0
            low = read(info, 2 * angle_total + angle * chunks + chunk)
            across = (x + left) * cosine + y * sine + (half - low) - depth_step
            rows = [jnp.maximum(0.0, 1.0 - jnp.abs(across - 8.0 * j)) for j in range(DEPTH // 8)]
            rows = jnp.concatenate(rows, axis=0).astype(jnp.bfloat16)
            hats[chunk, pl.ds(at, DEPTH), :] = rows
            hats[chunk, pl.ds(at + DEPTH, SLOT - DEPTH), :] = gap
        return carry

    lax.fori_loop(0, count, step, 0)


def project_kernel(plan, info, windows, hats, *refs):
    part, local, angle_total, last = plan
    before, (out, held, cut) = refs[:-3], refs[-3:]
    chunks, depth, pixels = hats.shape
    sources, tiles, height, wide = windows.shape
    slices = height // local
    count = depth // SLOT
    lane_blocks = wide // LANES
    for source in range(sources):
        for turn in range(tiles):
            piece = windows[source, turn].astype(held.dtype)
            for angle in range(local):
                held[source * local + angle, turn * slices : (turn + 1) * slices, :] = piece[
                    angle * slices : (angle + 1) * slices
                ]
    lane = lax.broadcasted_iota(jnp.int32, (slices * tiles, LANES), 1)

    def step(pair, carry):
        for chunk in range(chunks):
            merged = None
            for spot in range(PER):
                index = pair * PER + spot
                low = read(info, 2 * angle_total + (part * count + index) * chunks + chunk)
                low = low.astype(jnp.int32)
                block = low >> LANE_BITS
                past = low & (LANES - 1)
                after = jnp.minimum(block + 1, lane_blocks - 1)
                near = pl.ds(pl.multiple_of(block * LANES, LANES), LANES)
                far = pl.ds(pl.multiple_of(after * LANES, LANES), LANES)
                value = jnp.where(lane >= past, held[index, :, near], held[index, :, far])
                turn_by = (spot * SLOT + LANES - past) & (LANES - 1)
                value = pltpu.roll(value, turn_by, 1)
                merged = value if spot == 0 else jnp.where(lane < spot * SLOT, merged, value)
            at = pl.ds(pl.multiple_of(pair * LANES, LANES), LANES)
            cut[chunk, :, at] = merged.astype(jnp.bfloat16)
        return carry

    lax.fori_loop(0, count // PER, step, 0, unroll=4)
    sums = []
    for chunk in range(chunks):
        value = jnp.dot(cut[chunk], hats[chunk], preferred_element_type=jnp.float32)
        if before:
            value = value + before[0][chunk]
        sums.append(value)
        if not last:
            out[chunk] = value
    if not last:
        return
    mine = lax.axis_index("tile")
    for pair in range(TCOLS // LANES):
        near = sums[pair * (LANES // CHUNK) : (pair + 1) * (LANES // CHUNK)]
        for row in range(ROWS_DEV):
            value = jnp.concatenate(
                [part[:, row * CHUNK : (row + 1) * CHUNK] for part in near], axis=1
            )
            at = row * TCOLS + pair * LANES
            if slices % 8 == 0:
                for turn in range(tiles):
                    tile = lax.rem(mine + turn, tiles)
                    into = pl.ds(pl.multiple_of(tile * slices, slices), slices)
                    out[0, into, at : at + LANES] = value[turn * slices : (turn + 1) * slices]
            else:
                out[0, :, at : at + LANES] = pltpu.roll(value, mine * slices, 0)


def shifted(value, axis, by):
    size = lax.axis_size(axis)
    return lax.ppermute(value, axis, [(i, (i - by) % size) for i in range(size)])


def swapped(value, axis, by):
    return lax.ppermute(value, axis, [(i, i ^ by) for i in range(lax.axis_size(axis))])


def body(sinogram, paganin_width, window_block):
    local, slices, bins = sinogram.shape
    segments, spots, tiles = (lax.axis_size(name) for name in ("segment", "angle", "tile"))
    segment, spot = lax.axis_index("segment"), lax.axis_index("angle")
    groups = segments * spots
    angle_total = local * groups
    tile_rows = ROWS_DEV * groups
    reach = math.hypot((TCOLS - 1) / 2, (tile_rows - 1) / 2)
    first_bin = max(0, int(WIN / 2 - reach - 0.01)) // 16 * 16
    last_bin = min(WIN - 1, int(WIN / 2 + reach + 0.01) + 1)
    outs = -(-(last_bin + 1 - first_bin) // LANES)
    assert first_bin + (outs - 1) * LANES < WIN and first_bin < LANES
    assert spots & (spots - 1) == 0 and spots > 1
    smooth_blocks = -(-(outs + 3) // 2) * 2
    chunks, pixels = TCOLS // CHUNK, ROWS_DEV * CHUNK
    half = WIN / 2.0 - first_bin

    smem = pl.BlockSpec(memory_space=pltpu.SMEM)
    vmem = pl.BlockSpec(memory_space=pltpu.VMEM)
    hat_bytes = angle_total * SLOT * ROWS_DEV * TCOLS * 2
    params = pltpu.CompilerParams(vmem_limit_bytes=hat_bytes + 12 * 1024 * 1024)
    height = local * slices
    block_total = bins // LANES
    reached = [0]
    for bit in reversed(range(1, spots.bit_length() - 1)):
        reached += [other ^ (1 << bit) for other in reached]
    order = np.array([[other ^ swap for other in reached] for swap in (0, 1)], np.int32)
    order = np.repeat(order.reshape(-1), local), np.tile(np.arange(local), spots)
    where = np.arange(groups)[:, None]
    by = np.arange(segments)[:, None] + where[:, :, None] // spots
    angles = (where % spots ^ order[0]) * local + order[1]
    angles = by % segments * (spots * local) + angles[:, None]
    theta = math.pi * angles.reshape(groups, angle_total) / angle_total
    cosine, sine = np.cos(theta), np.sin(theta)
    left = np.arange(chunks) * CHUNK - (TCOLS - 1) / 2.0
    edges = np.minimum(cosine[..., None] * left, cosine[..., None] * (left + (CHUNK - 1)))
    top = where * ROWS_DEV - (tile_rows - 1) / 2.0
    rise = np.minimum(sine * top, sine * (top + (ROWS_DEV - 1)))
    lows = np.floor(edges + rise[..., None] + (half - 0.01)).astype(np.int32)
    lows = lows.astype(np.float32).reshape(groups, -1)
    table = np.concatenate([cosine.astype(np.float32), sine.astype(np.float32), lows], axis=1)
    info_rows = -(-table.shape[1] // (8 * LANES)) * 8
    table = np.pad(table, ((0, 0), (0, info_rows * LANES - table.shape[1])))
    table = jnp.asarray(table.reshape(groups, info_rows, LANES))

    *cut, info = pl.pallas_call(
        functools.partial(filter_kernel, (tiles, outs, first_bin)),
        out_shape=[jax.ShapeDtypeStruct((height, outs * LANES), jnp.bfloat16)] * tiles
        + [jax.ShapeDtypeStruct((info_rows, LANES), jnp.float32)],
        in_specs=[smem] + [pl.BlockSpec(memory_space=pltpu.HBM)] * 3,
        out_specs=[vmem] * (tiles + 1),
        scratch_shapes=[
            pltpu.SMEM(window_block.T.shape, jnp.int32),
            pltpu.VMEM(
                (local, slices, (block_total - WIN // LANES + smooth_blocks + 2) * LANES),
                jnp.float32,
            ),
            pltpu.VMEM((height * tiles, (smooth_blocks + 2) * LANES), jnp.float32),
            pltpu.VMEM((height * tiles, smooth_blocks * LANES), jnp.float32),
            pltpu.SemaphoreType.DMA((local + 2,)),
        ],
        compiler_params=params,
        name="filter",
    )(
        paganin_width,
        *(pltpu.with_memory_space_constraint(v, pltpu.HBM) for v in (window_block.T, table, sinogram)),
    )

    depth = spots * local // 2 * SLOT
    def hats_of(by, which, after):
        ready = lax.optimization_barrier((info, *after))[0]
        return pl.pallas_call(
            functools.partial(hat_kernel, (2 * by + which, half, tile_rows, angle_total)),
            out_shape=jax.ShapeDtypeStruct((chunks, depth, pixels), jnp.bfloat16),
            in_specs=[smem],
            out_specs=vmem,
            compiler_params=params,
            cost_estimate=pl.CostEstimate(
                flops=chunks * depth * pixels * 16, bytes_accessed=0, transcendentals=0
            ),
            name="hats",
        )(ready)

    hats = {}
    left_over = [(by, which) for which in (0, 1) for by in range(segments)]

    def beside(moved, after, count=1):
        names = [left_over.pop(0) for _ in range(min(count, len(left_over)))]
        made = [hats_of(*name, after) for name in names]
        moved, made = lax.optimization_barrier((moved, made))
        hats.update(zip(names, made))
        return moved

    moved = [shifted(cut[turn], "tile", turn) for turn in range(1, tiles)]
    pieces = jnp.stack([cut[0]] + beside(moved, cut))[None]
    for bit in reversed(range(1, spots.bit_length() - 1)):
        moved = beside(swapped(pieces, "angle", 1 << bit), (pieces,))
        pieces = jnp.concatenate([pieces, moved])
    held_type = jnp.bfloat16 if slices % 16 == 0 else jnp.float32

    def project(by, which, windows, sums, last=False):
        value = pl.pallas_call(
            functools.partial(project_kernel, (2 * by + which, local, angle_total, last)),
            out_shape=jax.ShapeDtypeStruct(
                (1, slices * tiles, ROWS_DEV * TCOLS)
                if last
                else (chunks, slices * tiles, pixels),
                jnp.float32,
            ),
            in_specs=[smem] + [vmem] * (2 + len(sums)),
            out_specs=vmem,
            scratch_shapes=[
                pltpu.VMEM((spots * local // 2, slices * tiles, outs * LANES), held_type),
                pltpu.VMEM((chunks, slices * tiles, depth), jnp.bfloat16),
            ],
            compiler_params=params,
            cost_estimate=pl.CostEstimate(
                flops=32 * slices * tiles * chunks * depth * pixels,
                bytes_accessed=0,
                transcendentals=0,
            ),
            name="project",
        )(info, windows, hats[by, which], *sums)
        return (value,)

    crossed = swapped(pieces, "angle", 1)
    sums = project(0, 0, pieces, ())
    for by in range(1, segments):
        sums = project(by, 0, shifted(pieces, "segment", by), sums)
    crossed, sums = beside((crossed, sums), (pieces,), len(left_over))
    others = [shifted(crossed, "segment", by) for by in range(1, segments)]
    sums = project(0, 1, crossed, sums, segments == 1)
    for by in range(1, segments):
        sums = project(by, 1, others[by - 1], sums, by == segments - 1)
    return sums[0]


def solution(mesh):
    in_specs = (P(("segment", "angle"), "tile", None), P(), P())
    out_specs = P("tile", None, ("segment", "angle"))
    return jax.shard_map(body, mesh=mesh, in_specs=in_specs, out_specs=out_specs, check_vma=False)
```

```python
import functools
import math

import jax
import jax.numpy as jnp
import numpy as np
from jax import lax
from jax.experimental import pallas as pl
from jax.experimental.pallas import tpu as pltpu
from jax.sharding import PartitionSpec as P

WIN = 512
BAND = 128
ROWS_DEV = 8
TCOLS = 256
LANES = 128
LANE_BITS = 7
CHUNK = 32
DEPTH = 48
SLOT = 64
PER = LANES // SLOT


def split(value):
    high = value.astype(jnp.bfloat16)
    return high, (value - high.astype(jnp.float32)).astype(jnp.bfloat16)


def banded(value, taps, starts):
    tap_high, tap_low = taps
    dot = functools.partial(jnp.dot, preferred_element_type=jnp.float32)
    cut = [value[:, start : start + tap_high.shape[0]] for start in starts]
    high, low = split(jnp.concatenate(cut, axis=0))
    both = dot(jnp.concatenate([high, low], axis=0), tap_high)
    result = both[: high.shape[0]] + (both[high.shape[0] :] + dot(high, tap_low))
    rows = value.shape[0]
    return [result[index * rows : (index + 1) * rows] for index in range(len(starts))]


def offsets(depth, width, shift):
    return (
        lax.broadcasted_iota(jnp.int32, (depth, width), 0)
        - lax.broadcasted_iota(jnp.int32, (depth, width), 1)
        - shift
    )


def filter_kernel(plan, width, blocks_ref, table, rows_ref, *refs):
    tiles, outs, first_bin = plan
    outputs, (info, blocks, padded, raw, smooth, arrived) = refs[:tiles], refs[tiles:]
    local, slices, bins = rows_ref.shape
    block_total = bins // LANES
    raw_wide = raw.shape[1]
    smooth_blocks = smooth.shape[1] // LANES
    height = local * slices
    ahead = 2 * LANES

    place = lax.axis_index("segment") * lax.axis_size("angle") + lax.axis_index("angle")
    copies = [
        pltpu.make_async_copy(blocks_ref, blocks, arrived.at[local]),
        pltpu.make_async_copy(table.at[place], info, arrived.at[local + 1]),
    ]
    copies += [
        pltpu.make_async_copy(
            rows_ref.at[angle], padded.at[angle, :, pl.ds(ahead, bins)], arrived.at[angle]
        )
        for angle in range(local)
    ]
    for copy in copies:
        copy.start()
    behind = padded.shape[2] - ahead - bins
    padded[:, :, :ahead] = jnp.zeros((local, slices, ahead), jnp.float32)
    padded[:, :, ahead + bins :] = jnp.zeros((local, slices, behind), jnp.float32)

    decay = width[0]
    steps = (lax.broadcasted_iota(jnp.int32, (1, BAND), 1) + 1).astype(jnp.float32)
    total = 1.0 + 2.0 * jnp.sum(jnp.exp(-steps / decay), axis=1, keepdims=True)
    away = offsets(2 * 256, 256, BAND)
    spread = jnp.abs(away)
    paganin = jnp.where(
        spread <= BAND, jnp.exp(-spread.astype(jnp.float32) / decay) / total, 0.0
    )
    paganin = split(paganin)
    away = offsets(512, LANES, BAND + first_bin)
    spread = jnp.abs(away)
    squared = jnp.maximum(spread * spread, 1).astype(jnp.float32)
    odd = jnp.logical_and(spread <= BAND, (spread & 1) == 1)
    ramp = jnp.where(odd, -1.0 / (math.pi * math.pi * squared), 0.0)
    ramp = split(jnp.where(away == 0, 0.25, ramp))

    for copy in copies:
        copy.wait()
    first = place * local
    mine = lax.axis_index("tile")
    starts = []
    for turn in range(tiles):
        tile = lax.rem(mine - turn + tiles, tiles)
        for angle in range(local):
            start = blocks[tile, first + angle]
            starts.append(start)
            at = (turn * local + angle) * slices
            lanes = pl.ds(pl.multiple_of(start * LANES, LANES), raw_wide)
            raw[at : at + slices, :] = padded[angle, :, lanes]
    pairs = range(0, smooth_blocks * LANES, 256)
    for at, value in zip(pairs, banded(raw[...], paganin, pairs)):
        smooth[:, at : at + 256] = value
    for index, start in enumerate(starts):
        at = slice(index * slices, (index + 1) * slices)
        for j in range(smooth_blocks):
            if 1 <= j <= WIN // LANES:
                continue
            block = start - 1 + j
            inside = jnp.logical_and(block >= 0, block < block_total)
            lanes = slice(j * LANES, (j + 1) * LANES)
            smooth[at, lanes] = jnp.where(inside, smooth[at, lanes], 0.0)
    lanes = range(0, outs * LANES, LANES)
    for j, value in enumerate(banded(smooth[...], ramp, lanes)):
        for turn in range(tiles):
            part = value[turn * height : (turn + 1) * height]
            outputs[turn][:, j * LANES : (j + 1) * LANES] = part.astype(jnp.bfloat16)


def read(info, index):
    return info[index >> LANE_BITS, index & (LANES - 1)]


def hat_kernel(plan, info, hats):
    part, half, tile_rows, angle_total = plan
    chunks, depth, pixels = hats.shape
    count = depth // SLOT
    place = lax.axis_index("segment") * lax.axis_size("angle") + lax.axis_index("angle")
    first_row = (place * ROWS_DEV).astype(jnp.float32) - (tile_rows - 1) / 2.0
    lane = lax.broadcasted_iota(jnp.int32, (8, pixels), 1)
    depth_step = lax.broadcasted_iota(jnp.int32, (8, pixels), 0).astype(jnp.float32)
    y = (lane // CHUNK).astype(jnp.float32) + first_row
    x = (lane % CHUNK).astype(jnp.float32)
    gap = jnp.zeros((SLOT - DEPTH, pixels), jnp.bfloat16)

    def step(index, carry):
        angle = part * count + index
        cosine, sine = read(info, angle), read(info, angle_total + angle)
        at = pl.multiple_of(index * SLOT, SLOT)
        for chunk in range(chunks):
            left = chunk * CHUNK - (TCOLS - 1) / 2.0
            low = read(info, 2 * angle_total + angle * chunks + chunk)
            across = (x + left) * cosine + y * sine + (half - low) - depth_step
            rows = [jnp.maximum(0.0, 1.0 - jnp.abs(across - 8.0 * j)) for j in range(DEPTH // 8)]
            rows = jnp.concatenate(rows, axis=0).astype(jnp.bfloat16)
            hats[chunk, pl.ds(at, DEPTH), :] = rows
            hats[chunk, pl.ds(at + DEPTH, SLOT - DEPTH), :] = gap
        return carry

    lax.fori_loop(0, count, step, 0)


def project_kernel(plan, info, windows, *refs):
    part, hat_count, local, angle_total, last = plan
    hats, before, (out, held, cut) = refs[:hat_count], refs[hat_count:-3], refs[-3:]
    chunks, hat_depth, pixels = hats[0].shape
    depth = hat_count * hat_depth
    sources, tiles, height, wide = windows.shape
    slices = height // local
    count = depth // SLOT
    lane_blocks = wide // LANES
    for source in range(sources):
        for turn in range(tiles):
            piece = windows[source, turn].astype(held.dtype)
            for angle in range(local):
                held[source * local + angle, turn * slices : (turn + 1) * slices, :] = piece[
                    angle * slices : (angle + 1) * slices
                ]
    lane = lax.broadcasted_iota(jnp.int32, (slices * tiles, LANES), 1)

    def step(pair, carry):
        for chunk in range(chunks):
            merged = None
            for spot in range(PER):
                index = pair * PER + spot
                low = read(info, 2 * angle_total + (part * count + index) * chunks + chunk)
                low = low.astype(jnp.int32)
                block = low >> LANE_BITS
                past = low & (LANES - 1)
                after = jnp.minimum(block + 1, lane_blocks - 1)
                near = pl.ds(pl.multiple_of(block * LANES, LANES), LANES)
                far = pl.ds(pl.multiple_of(after * LANES, LANES), LANES)
                value = jnp.where(lane >= past, held[index, :, near], held[index, :, far])
                turn_by = (spot * SLOT + LANES - past) & (LANES - 1)
                value = pltpu.roll(value, turn_by, 1)
                merged = value if spot == 0 else jnp.where(lane < spot * SLOT, merged, value)
            at = pl.ds(pl.multiple_of(pair * LANES, LANES), LANES)
            cut[chunk, :, at] = merged.astype(jnp.bfloat16)
        return carry

    lax.fori_loop(0, count // PER, step, 0, unroll=4)
    sums = []
    for chunk in range(chunks):
        value = before[0][chunk] if before else None
        for index, hat in enumerate(hats):
            lanes = slice(index * hat_depth, (index + 1) * hat_depth)
            more = jnp.dot(cut[chunk, :, lanes], hat[chunk], preferred_element_type=jnp.float32)
            value = more if value is None else value + more
        sums.append(value)
        if not last:
            out[chunk] = value
    if not last:
        return
    mine = lax.axis_index("tile")
    for pair in range(TCOLS // LANES):
        near = sums[pair * (LANES // CHUNK) : (pair + 1) * (LANES // CHUNK)]
        for row in range(ROWS_DEV):
            value = jnp.concatenate(
                [part[:, row * CHUNK : (row + 1) * CHUNK] for part in near], axis=1
            )
            at = row * TCOLS + pair * LANES
            if slices % 8 == 0:
                for turn in range(tiles):
                    tile = lax.rem(mine + turn, tiles)
                    into = pl.ds(pl.multiple_of(tile * slices, slices), slices)
                    out[0, into, at : at + LANES] = value[turn * slices : (turn + 1) * slices]
            else:
                out[0, :, at : at + LANES] = pltpu.roll(value, mine * slices, 0)


def shifted(value, axis, by):
    size = lax.axis_size(axis)
    return lax.ppermute(value, axis, [(i, (i - by) % size) for i in range(size)])


def swapped(value, axis, by):
    return lax.ppermute(value, axis, [(i, i ^ by) for i in range(lax.axis_size(axis))])


def body(sinogram, paganin_width, window_block):
    local, slices, bins = sinogram.shape
    segments, spots, tiles = (lax.axis_size(name) for name in ("segment", "angle", "tile"))
    segment, spot = lax.axis_index("segment"), lax.axis_index("angle")
    groups = segments * spots
    angle_total = local * groups
    tile_rows = ROWS_DEV * groups
    reach = math.hypot((TCOLS - 1) / 2, (tile_rows - 1) / 2)
    first_bin = max(0, int(WIN / 2 - reach - 0.01)) // 16 * 16
    last_bin = min(WIN - 1, int(WIN / 2 + reach + 0.01) + 1)
    outs = -(-(last_bin + 1 - first_bin) // LANES)
    assert first_bin + (outs - 1) * LANES < WIN and first_bin < LANES
    assert spots & (spots - 1) == 0 and spots > 1
    smooth_blocks = -(-(outs + 3) // 2) * 2
    chunks, pixels = TCOLS // CHUNK, ROWS_DEV * CHUNK
    half = WIN / 2.0 - first_bin

    smem = pl.BlockSpec(memory_space=pltpu.SMEM)
    vmem = pl.BlockSpec(memory_space=pltpu.VMEM)
    hat_bytes = angle_total * SLOT * ROWS_DEV * TCOLS * 2
    params = pltpu.CompilerParams(vmem_limit_bytes=hat_bytes + 12 * 1024 * 1024)
    height = local * slices
    block_total = bins // LANES
    bits = [1 << bit for bit in reversed(range(spots.bit_length() - 1))]
    exchanges = [(bits[0],)]
    for first in range(1, len(bits), 2):
        pair = bits[first : first + 2]
        exchanges.append((*pair, sum(pair)) if len(pair) == 2 else tuple(pair))
    reached = [0]
    for masks in exchanges:
        reached = [other ^ mask for mask in (0, *masks) for other in reached]
    order = np.repeat(np.array(reached), local), np.tile(np.arange(local), spots)
    where = np.arange(groups)[:, None]
    by = np.arange(segments)[:, None] + where[:, :, None] // spots
    angles = (where % spots ^ order[0]) * local + order[1]
    angles = by % segments * (spots * local) + angles[:, None]
    theta = math.pi * angles.reshape(groups, angle_total) / angle_total
    cosine, sine = np.cos(theta), np.sin(theta)
    left = np.arange(chunks) * CHUNK - (TCOLS - 1) / 2.0
    edges = np.minimum(cosine[..., None] * left, cosine[..., None] * (left + (CHUNK - 1)))
    top = where * ROWS_DEV - (tile_rows - 1) / 2.0
    rise = np.minimum(sine * top, sine * (top + (ROWS_DEV - 1)))
    lows = np.floor(edges + rise[..., None] + (half - 0.01)).astype(np.int32)
    lows = lows.astype(np.float32).reshape(groups, -1)
    table = np.concatenate([cosine.astype(np.float32), sine.astype(np.float32), lows], axis=1)
    info_rows = -(-table.shape[1] // (8 * LANES)) * 8
    table = np.pad(table, ((0, 0), (0, info_rows * LANES - table.shape[1])))
    table = jnp.asarray(table.reshape(groups, info_rows, LANES))

    *cut, info = pl.pallas_call(
        functools.partial(filter_kernel, (tiles, outs, first_bin)),
        out_shape=[jax.ShapeDtypeStruct((height, outs * LANES), jnp.bfloat16)] * tiles
        + [jax.ShapeDtypeStruct((info_rows, LANES), jnp.float32)],
        in_specs=[smem] + [pl.BlockSpec(memory_space=pltpu.HBM)] * 3,
        out_specs=[vmem] * (tiles + 1),
        scratch_shapes=[
            pltpu.SMEM(window_block.T.shape, jnp.int32),
            pltpu.VMEM(
                (local, slices, (block_total - WIN // LANES + smooth_blocks + 2) * LANES),
                jnp.float32,
            ),
            pltpu.VMEM((height * tiles, (smooth_blocks + 2) * LANES), jnp.float32),
            pltpu.VMEM((height * tiles, smooth_blocks * LANES), jnp.float32),
            pltpu.SemaphoreType.DMA((local + 2,)),
        ],
        compiler_params=params,
        name="filter",
    )(
        paganin_width,
        *(pltpu.with_memory_space_constraint(v, pltpu.HBM) for v in (window_block.T, table, sinogram)),
    )

    depth = spots * local // 2 * SLOT
    def hats_of(part, after):
        ready = lax.optimization_barrier((info, *after))[0]
        return pl.pallas_call(
            functools.partial(hat_kernel, (part, half, tile_rows, angle_total)),
            out_shape=jax.ShapeDtypeStruct((chunks, depth, pixels), jnp.bfloat16),
            in_specs=[smem],
            out_specs=vmem,
            compiler_params=params,
            cost_estimate=pl.CostEstimate(
                flops=chunks * depth * pixels * 16, bytes_accessed=0, transcendentals=0
            ),
            name="hats",
        )(ready)

    hats = []

    def beside(moved, after, count):
        made = []
        for _ in range(min(count, 2 * segments - len(hats))):
            made.append(hats_of(len(hats), after))
            hats.append(None)
        moved, made = lax.optimization_barrier((moved, made))
        hats[len(hats) - len(made) :] = made
        return moved

    def joint(turn, mask):
        def index(spot, tile):
            return (spot ^ mask) * tiles + (tile - turn) % tiles

        pairs = [(at, index(at // tiles, at % tiles)) for at in range(spots * tiles)]
        return lax.ppermute(cut[turn], ("angle", "tile"), pairs)

    near = [(turn, mask) for mask in (0, *exchanges[0]) for turn in range(tiles)][1:]
    moved = beside([joint(*pair) for pair in near], cut, 2)
    pieces = jnp.stack([cut[0], *moved]).reshape(2, tiles, *cut[0].shape)
    for index, masks in enumerate(exchanges[1:]):
        moved = [swapped(pieces, "angle", mask) for mask in masks]
        last = index == len(exchanges) - 2
        moved = beside(moved, (pieces,), 2 * segments if last else 2)
        pieces = jnp.concatenate([pieces, *moved])
    held_type = jnp.bfloat16 if slices % 16 == 0 else jnp.float32
    parts = [pieces] + [shifted(pieces, "segment", by) for by in range(1, segments)]
    sums = ()
    for by, windows in enumerate(parts):
        last = by == segments - 1
        value = pl.pallas_call(
            functools.partial(project_kernel, (by, 2, local, angle_total, last)),
            out_shape=jax.ShapeDtypeStruct(
                (1, slices * tiles, ROWS_DEV * TCOLS)
                if last
                else (chunks, slices * tiles, pixels),
                jnp.float32,
            ),
            in_specs=[smem] + [vmem] * (3 + len(sums)),
            out_specs=vmem,
            scratch_shapes=[
                pltpu.VMEM((spots * local, slices * tiles, outs * LANES), held_type),
                pltpu.VMEM((chunks, slices * tiles, 2 * depth), jnp.bfloat16),
            ],
            compiler_params=params,
            cost_estimate=pl.CostEstimate(
                flops=64 * slices * tiles * chunks * depth * pixels,
                bytes_accessed=0,
                transcendentals=0,
            ),
            name="project",
        )(info, windows, *hats[2 * by : 2 * by + 2], *sums)
        sums = (value,)
    return sums[0]


def solution(mesh):
    in_specs = (P(("segment", "angle"), "tile", None), P(), P())
    out_specs = P("tile", None, ("segment", "angle"))
    return jax.shard_map(body, mesh=mesh, in_specs=in_specs, out_specs=out_specs, check_vma=False)
```

```python
import functools
import math

import jax
import jax.numpy as jnp
import numpy as np
from jax import lax
from jax.experimental import pallas as pl
from jax.experimental.pallas import tpu as pltpu
from jax.sharding import PartitionSpec as P

WIN = 512
BAND = 128
ROWS_DEV = 8
TCOLS = 256
LANES = 128
LANE_BITS = 7
CHUNK = 32
DEPTH = 40
SLOT = 64
PER = LANES // SLOT


def split(value):
    high = value.astype(jnp.bfloat16)
    return high, (value - high.astype(jnp.float32)).astype(jnp.bfloat16)


def banded(value, taps, starts):
    tap_high, tap_low = taps
    dot = functools.partial(jnp.dot, preferred_element_type=jnp.float32)
    cut = [value[:, start : start + tap_high.shape[0]] for start in starts]
    high, low = split(jnp.concatenate(cut, axis=0))
    both = dot(jnp.concatenate([high, low], axis=0), tap_high)
    result = both[: high.shape[0]] + (both[high.shape[0] :] + dot(high, tap_low))
    rows = value.shape[0]
    return [result[index * rows : (index + 1) * rows] for index in range(len(starts))]


def offsets(depth, width, shift):
    return (
        lax.broadcasted_iota(jnp.int32, (depth, width), 0)
        - lax.broadcasted_iota(jnp.int32, (depth, width), 1)
        - shift
    )


def filter_kernel(plan, width, blocks_ref, trig_table, code_table, rows_ref, *refs):
    tiles, outs, first_bin = plan
    outputs, (trig, codes, blocks, padded, raw, smooth, arrived) = (
        refs[:tiles],
        refs[tiles:],
    )
    local, slices, bins = rows_ref.shape
    block_total = bins // LANES
    raw_wide = raw.shape[1]
    smooth_blocks = smooth.shape[1] // LANES
    height = local * slices
    ahead = 2 * LANES

    place = lax.axis_index("segment") * lax.axis_size("angle") + lax.axis_index("angle")
    sources = [(blocks_ref, blocks), (trig_table.at[place], trig), (code_table.at[place], codes)]
    group = math.gcd(slices, 8)
    for angle in range(local):
        for row in range(0, slices, group):
            into = padded.at[angle, pl.ds(row, group), pl.ds(ahead, bins)]
            sources.append((rows_ref.at[angle, pl.ds(row, group)], into))
    copies = [
        pltpu.make_async_copy(source, into, arrived.at[index])
        for index, (source, into) in enumerate(sources)
    ]
    for copy in copies:
        copy.start()
    behind = padded.shape[2] - ahead - bins
    padded[:, :, :ahead] = jnp.zeros((local, slices, ahead), jnp.float32)
    padded[:, :, ahead + bins :] = jnp.zeros((local, slices, behind), jnp.float32)

    decay = width[0]
    steps = (lax.broadcasted_iota(jnp.int32, (1, BAND), 1) + 1).astype(jnp.float32)
    total = 1.0 + 2.0 * jnp.sum(jnp.exp(-steps / decay), axis=1, keepdims=True)
    away = offsets(2 * 256, 256, BAND)
    spread = jnp.abs(away)
    paganin = jnp.where(
        spread <= BAND, jnp.exp(-spread.astype(jnp.float32) / decay) / total, 0.0
    )
    paganin = split(paganin)
    away = offsets(512, LANES, BAND + first_bin)
    spread = jnp.abs(away)
    squared = jnp.maximum(spread * spread, 1).astype(jnp.float32)
    odd = jnp.logical_and(spread <= BAND, (spread & 1) == 1)
    ramp = jnp.where(odd, -1.0 / (math.pi * math.pi * squared), 0.0)
    ramp = split(jnp.where(away == 0, 0.25, ramp))

    for copy in copies:
        copy.wait()
    first = place * local
    mine = lax.axis_index("tile")
    starts = []
    for turn in range(tiles):
        tile = lax.rem(mine - turn + tiles, tiles)
        for angle in range(local):
            start = blocks[tile, first + angle]
            starts.append(start)
            at = (turn * local + angle) * slices
            lanes = pl.ds(pl.multiple_of(start * LANES, LANES), raw_wide)
            raw[at : at + slices, :] = padded[angle, :, lanes]
    pairs = range(0, smooth_blocks * LANES, 256)
    for at, value in zip(pairs, banded(raw[...], paganin, pairs)):
        smooth[:, at : at + 256] = value
    for index, start in enumerate(starts):
        at = slice(index * slices, (index + 1) * slices)
        for j in range(smooth_blocks):
            if 1 <= j <= WIN // LANES:
                continue
            block = start - 1 + j
            inside = jnp.logical_and(block >= 0, block < block_total)
            lanes = slice(j * LANES, (j + 1) * LANES)
            smooth[at, lanes] = jnp.where(inside, smooth[at, lanes], 0.0)
    lanes = range(0, outs * LANES, LANES)
    for j, value in enumerate(banded(smooth[...], ramp, lanes)):
        for turn in range(tiles):
            part = value[turn * height : (turn + 1) * height]
            outputs[turn][:, j * LANES : (j + 1) * LANES] = part.astype(jnp.bfloat16)


def read(table, index):
    return table[index >> LANE_BITS, index & (LANES - 1)]


def hat_kernel(plan, trig, codes, hats):
    part, half, tile_rows, angle_total = plan
    chunks, depth, pixels = hats.shape
    count = depth // SLOT
    place = lax.axis_index("segment") * lax.axis_size("angle") + lax.axis_index("angle")
    first_row = (place * ROWS_DEV).astype(jnp.float32) - (tile_rows - 1) / 2.0
    lane = lax.broadcasted_iota(jnp.int32, (8, pixels), 1)
    depth_step = lax.broadcasted_iota(jnp.int32, (8, pixels), 0).astype(jnp.float32)
    y = (lane // CHUNK).astype(jnp.float32) + first_row
    x = (lane % CHUNK).astype(jnp.float32)
    rest = jnp.zeros((-DEPTH % 16, pixels), jnp.float32)
    gap = jnp.zeros((SLOT - DEPTH - DEPTH % 16, pixels), jnp.bfloat16)

    def step(index, carry):
        angle = part * count + index
        cosine, sine = read(trig, angle), read(trig, angle_total + angle)
        at = pl.multiple_of(index * SLOT, SLOT)
        start = y * sine + x * cosine - depth_step
        for chunk in range(chunks):
            left = chunk * CHUNK - (TCOLS - 1) / 2.0
            code = read(codes, angle * chunks + chunk)
            low = ((code >> LANE_BITS) * SLOT + (code & (LANES - 1))).astype(jnp.float32)
            across = start + (left * cosine + (half - low))
            rows = [jnp.maximum(0.0, 1.0 - jnp.abs(across - 8.0 * j)) for j in range(DEPTH // 8)]
            rows = jnp.concatenate([*rows, rest], axis=0).astype(jnp.bfloat16)
            hats[chunk, pl.ds(at, rows.shape[0]), :] = rows
            hats[chunk, pl.ds(at + rows.shape[0], gap.shape[0]), :] = gap
        return carry

    lax.fori_loop(0, count, step, 0, unroll=2)


def project_kernel(plan, codes, windows, hats, *refs):
    part, local, last = plan
    before, (out, held) = refs[:-2], refs[-2:]
    chunks, depth, pixels = hats.shape
    sources, tiles, height, wide = windows.shape
    slices = height // local
    count = depth // SLOT
    spread = lax.broadcasted_iota(jnp.int32, (height, LANES), 1)
    for source in range(sources):
        for turn in range(tiles):
            piece = windows[source, turn].astype(held.dtype)
            pieces = [piece[:, at : at + LANES] for at in range(0, wide, LANES)]
            halves = [pltpu.roll(value, SLOT, 1) for value in pieces]
            for j in range(held.shape[1]):
                if j % 2 == 0:
                    value = pieces[j // 2]
                else:
                    value = jnp.where(spread < SLOT, halves[j // 2], halves[j // 2 + 1])
                for angle in range(local):
                    held[source * local + angle, j, turn * slices : (turn + 1) * slices, :] = (
                        value[angle * slices : (angle + 1) * slices]
                    )
    lane = lax.broadcasted_iota(jnp.int32, (slices * tiles, LANES), 1)
    sums = []
    for chunk in range(chunks):
        cut = []
        for first in range(0, count, PER):
            merged = None
            for spot in range(PER):
                index = first + spot
                code = read(codes, (part * count + index) * chunks + chunk)
                turn_by = (spot * SLOT + LANES - (code & (LANES - 1))) & (LANES - 1)
                value = pltpu.roll(held[index, code >> LANE_BITS], turn_by, 1)
                merged = value if spot == 0 else jnp.where(lane < spot * SLOT, merged, value)
            cut.append(merged.astype(jnp.bfloat16))
        value = jnp.dot(
            jnp.concatenate(cut, axis=1), hats[chunk], preferred_element_type=jnp.float32
        )
        if before:
            value = value + before[0][chunk]
        sums.append(value)
        if not last:
            out[chunk] = value
        if not last or (chunk + 1) * CHUNK % LANES:
            continue
        mine = lax.axis_index("tile")
        for row in range(ROWS_DEV):
            value = jnp.concatenate(
                [part[:, row * CHUNK : (row + 1) * CHUNK] for part in sums], axis=1
            )
            at = row * TCOLS + (chunk + 1) * CHUNK - LANES
            if slices % 8 == 0:
                for turn in range(tiles):
                    tile = lax.rem(mine + turn, tiles)
                    into = pl.ds(pl.multiple_of(tile * slices, slices), slices)
                    out[0, into, at : at + LANES] = value[turn * slices : (turn + 1) * slices]
            else:
                out[0, :, at : at + LANES] = pltpu.roll(value, mine * slices, 0)
        sums = []


def shifted(value, axis, by):
    size = lax.axis_size(axis)
    return lax.ppermute(value, axis, [(i, (i - by) % size) for i in range(size)])


def swapped(value, axis, by):
    return lax.ppermute(value, axis, [(i, i ^ by) for i in range(lax.axis_size(axis))])


def body(sinogram, paganin_width, window_block):
    local, slices, bins = sinogram.shape
    segments, spots, tiles = (lax.axis_size(name) for name in ("segment", "angle", "tile"))
    segment, spot = lax.axis_index("segment"), lax.axis_index("angle")
    groups = segments * spots
    angle_total = local * groups
    tile_rows = ROWS_DEV * groups
    reach = math.hypot((TCOLS - 1) / 2, (tile_rows - 1) / 2)
    first_bin = max(0, int(WIN / 2 - reach - 0.01)) // 16 * 16
    last_bin = min(WIN - 1, int(WIN / 2 + reach + 0.01) + 1)
    outs = -(-(last_bin + 1 - first_bin) // LANES)
    assert first_bin + (outs - 1) * LANES < WIN and first_bin < LANES
    assert spots & (spots - 1) == 0 and spots > 1
    smooth_blocks = -(-(outs + 3) // 2) * 2
    chunks, pixels = TCOLS // CHUNK, ROWS_DEV * CHUNK
    half = WIN / 2.0 - first_bin

    smem = pl.BlockSpec(memory_space=pltpu.SMEM)
    vmem = pl.BlockSpec(memory_space=pltpu.VMEM)
    hat_bytes = angle_total * SLOT * ROWS_DEV * TCOLS * 2
    params = pltpu.CompilerParams(vmem_limit_bytes=hat_bytes + 12 * 1024 * 1024)
    height = local * slices
    block_total = bins // LANES
    bits = [1 << bit for bit in reversed(range(spots.bit_length() - 1))]
    exchanges = [(bits[0],)]
    for first in range(1, len(bits), 2):
        pair = bits[first : first + 2]
        exchanges.append((*pair, sum(pair)) if len(pair) == 2 else tuple(pair))
    reached = [0]
    for masks in exchanges:
        reached = [other ^ mask for mask in (0, *masks) for other in reached]
    order = np.repeat(np.array(reached), local), np.tile(np.arange(local), spots)
    where = np.arange(groups)[:, None]
    by = np.arange(segments)[:, None] + where[:, :, None] // spots
    angles = (where % spots ^ order[0]) * local + order[1]
    angles = by % segments * (spots * local) + angles[:, None]
    theta = math.pi * angles.reshape(groups, angle_total) / angle_total
    cosine, sine = np.cos(theta), np.sin(theta)
    left = np.arange(chunks) * CHUNK - (TCOLS - 1) / 2.0
    edges = np.minimum(cosine[..., None] * left, cosine[..., None] * (left + (CHUNK - 1)))
    top = where * ROWS_DEV - (tile_rows - 1) / 2.0
    rise = np.minimum(sine * top, sine * (top + (ROWS_DEV - 1)))
    lows = np.floor(edges + rise[..., None] + (half - 0.01)).astype(np.int32)
    blocks = np.minimum(lows // SLOT, PER * (outs - 1))
    codes = (blocks << LANE_BITS) + lows - blocks * SLOT

    def in_rows(values):
        values = values.reshape(groups, -1)
        rows = -(-values.shape[1] // (8 * LANES)) * 8
        values = np.pad(values, ((0, 0), (0, rows * LANES - values.shape[1])))
        return jnp.asarray(values.reshape(groups, rows, LANES))

    trig_table = in_rows(np.concatenate([cosine, sine], axis=1).astype(np.float32))
    code_table = in_rows(codes.astype(np.int32))

    *cut, trig, codes = pl.pallas_call(
        functools.partial(filter_kernel, (tiles, outs, first_bin)),
        out_shape=[jax.ShapeDtypeStruct((height, outs * LANES), jnp.bfloat16)] * tiles
        + [jax.ShapeDtypeStruct(v.shape[1:], v.dtype) for v in (trig_table, code_table)],
        in_specs=[smem] + [pl.BlockSpec(memory_space=pltpu.HBM)] * 4,
        out_specs=[vmem] * (tiles + 2),
        scratch_shapes=[
            pltpu.SMEM(window_block.T.shape, jnp.int32),
            pltpu.VMEM(
                (local, slices, (block_total - WIN // LANES + smooth_blocks + 2) * LANES),
                jnp.float32,
            ),
            pltpu.VMEM((height * tiles, (smooth_blocks + 2) * LANES), jnp.float32),
            pltpu.VMEM((height * tiles, smooth_blocks * LANES), jnp.float32),
            pltpu.SemaphoreType.DMA((local * slices // math.gcd(slices, 8) + 3,)),
        ],
        compiler_params=params,
        name="filter",
    )(
        paganin_width,
        *(
            pltpu.with_memory_space_constraint(value, pltpu.HBM)
            for value in (window_block.T, trig_table, code_table, sinogram)
        ),
    )

    depth = spots * local * SLOT
    def hats_of(part, after):
        ready = lax.optimization_barrier((trig, codes, *after))[:2]
        return pl.pallas_call(
            functools.partial(hat_kernel, (part, half, tile_rows, angle_total)),
            out_shape=jax.ShapeDtypeStruct((chunks, depth, pixels), jnp.bfloat16),
            in_specs=[smem, smem],
            out_specs=vmem,
            compiler_params=params,
            cost_estimate=pl.CostEstimate(
                flops=chunks * depth * pixels * 16, bytes_accessed=0, transcendentals=0
            ),
            name="hats",
        )(*ready)

    hats = []

    def beside(moved, after, count):
        made = []
        for _ in range(min(count, segments - len(hats))):
            made.append(hats_of(len(hats), after))
            hats.append(None)
        moved, made = lax.optimization_barrier((moved, made))
        hats[len(hats) - len(made) :] = made
        return moved

    def joint(turn, mask):
        def index(spot, tile):
            return (spot ^ mask) * tiles + (tile - turn) % tiles

        pairs = [(at, index(at // tiles, at % tiles)) for at in range(spots * tiles)]
        return lax.ppermute(cut[turn], ("angle", "tile"), pairs)

    near = [(turn, mask) for mask in (0, *exchanges[0]) for turn in range(tiles)][1:]
    moved = beside([joint(*pair) for pair in near], cut, 1)
    pieces = jnp.stack([cut[0], *moved]).reshape(2, tiles, *cut[0].shape)
    for index, masks in enumerate(exchanges[1:]):
        moved = [swapped(pieces, "angle", mask) for mask in masks]
        last = index == len(exchanges) - 2
        moved = beside(moved, (pieces,), segments if last else 1)
        pieces = jnp.concatenate([pieces, *moved])
    held_type = jnp.bfloat16 if slices % 16 == 0 else jnp.float32
    parts = [pieces] + [shifted(pieces, "segment", by) for by in range(1, segments)]
    sums = ()
    for by, windows in enumerate(parts):
        last = by == segments - 1
        value = pl.pallas_call(
            functools.partial(project_kernel, (by, local, last)),
            out_shape=jax.ShapeDtypeStruct(
                (1, slices * tiles, ROWS_DEV * TCOLS)
                if last
                else (chunks, slices * tiles, pixels),
                jnp.float32,
            ),
            in_specs=[smem] + [vmem] * (2 + len(sums)),
            out_specs=vmem,
            scratch_shapes=[
                pltpu.VMEM((spots * local, PER * (outs - 1) + 1, slices * tiles, LANES), held_type),
            ],
            compiler_params=params,
            cost_estimate=pl.CostEstimate(
                flops=32 * slices * tiles * chunks * depth * pixels,
                bytes_accessed=0,
                transcendentals=0,
            ),
            name="project",
        )(codes, windows, hats[by], *sums)
        sums = (value,)
    return sums[0]


def solution(mesh):
    in_specs = (P(("segment", "angle"), "tile", None), P(), P())
    out_specs = P("tile", None, ("segment", "angle"))
    return jax.shard_map(body, mesh=mesh, in_specs=in_specs, out_specs=out_specs, check_vma=False)
```

```python
import functools
import math

import jax
import jax.numpy as jnp
import numpy as np
from jax import lax
from jax.experimental import pallas as pl
from jax.experimental.pallas import tpu as pltpu
from jax.sharding import PartitionSpec as P

WIN = 512
BAND = 128
ROWS_DEV = 8
TCOLS = 256
LANES = 128
LANE_BITS = 7
CHUNK = 32
DEPTH = 40
SLOT = 64
PER = LANES // SLOT


def split(value):
    high = value.astype(jnp.bfloat16)
    return high, (value - high.astype(jnp.float32)).astype(jnp.bfloat16)


def banded(value, taps, starts):
    tap_high, tap_low = taps
    dot = functools.partial(jnp.dot, preferred_element_type=jnp.float32)
    cut = [value[:, start : start + tap_high.shape[0]] for start in starts]
    high, low = split(jnp.concatenate(cut, axis=0))
    both = dot(jnp.concatenate([high, low], axis=0), tap_high)
    result = both[: high.shape[0]] + (both[high.shape[0] :] + dot(high, tap_low))
    rows = value.shape[0]
    return [result[index * rows : (index + 1) * rows] for index in range(len(starts))]


def offsets(depth, width, shift):
    return (
        lax.broadcasted_iota(jnp.int32, (depth, width), 0)
        - lax.broadcasted_iota(jnp.int32, (depth, width), 1)
        - shift
    )


def filter_kernel(plan, width, blocks_ref, trig_table, code_table, rows_ref, *refs):
    tiles, outs, first_bin, packing = plan
    full, rows_of_block, groups = packing
    outputs, (trig, codes, blocks, padded, raw, smooth, arrived) = (
        refs[:tiles],
        refs[tiles:],
    )
    local, slices, bins = rows_ref.shape
    block_total = bins // LANES
    raw_wide = raw.shape[1]
    smooth_blocks = smooth.shape[1] // LANES
    height = local * slices
    ahead = 2 * LANES

    place = lax.axis_index("segment") * lax.axis_size("angle") + lax.axis_index("angle")
    sources = [(rows_ref.at[i], padded.at[i, :, pl.ds(ahead, bins)]) for i in range(local)]
    sources = [
        *sources,
        (blocks_ref, blocks),
        (trig_table.at[place], trig),
        (code_table.at[place], codes),
    ]
    copies = [
        pltpu.make_async_copy(source, into, arrived.at[index])
        for index, (source, into) in enumerate(sources)
    ]
    for copy in copies:
        copy.start()
    behind = padded.shape[2] - ahead - bins
    padded[:, :, :ahead] = jnp.zeros((local, slices, ahead), jnp.float32)
    padded[:, :, ahead + bins :] = jnp.zeros((local, slices, behind), jnp.float32)

    away = offsets(512, LANES, BAND + first_bin)
    spread = jnp.abs(away)
    squared = jnp.maximum(spread * spread, 1).astype(jnp.float32)
    odd = jnp.logical_and(spread <= BAND, (spread & 1) == 1)
    ramp = jnp.where(odd, -1.0 / (math.pi * math.pi * squared), 0.0)
    ramp = split(jnp.where(away == 0, 0.25, ramp))
    decay = width[0]
    steps = (lax.broadcasted_iota(jnp.int32, (1, BAND), 1) + 1).astype(jnp.float32)
    total = 1.0 + 2.0 * jnp.sum(jnp.exp(-steps / decay), axis=1, keepdims=True)
    away = offsets(2 * 256, 256, BAND)
    spread = jnp.abs(away)
    paganin = jnp.where(
        spread <= BAND, jnp.exp(-spread.astype(jnp.float32) / decay) / total, 0.0
    )
    paganin = split(paganin)

    for copy in copies:
        copy.wait()
    first = place * local
    mine = lax.axis_index("tile")
    starts = []
    for turn in range(tiles):
        tile = lax.rem(mine - turn + tiles, tiles)
        for angle in range(local):
            start = blocks[tile, first + angle]
            starts.append(start)
            at = (turn * local + angle) * slices
            lanes = pl.ds(pl.multiple_of(start * LANES, LANES), raw_wide)
            raw[at : at + slices, :] = padded[angle, :, lanes]
    pairs = range(0, smooth_blocks * LANES, 256)
    for at, value in zip(pairs, banded(raw[...], paganin, pairs)):
        smooth[:, at : at + 256] = value
    for index, start in enumerate(starts):
        at = slice(index * slices, (index + 1) * slices)
        for j in range(smooth_blocks):
            if 1 <= j <= WIN // LANES:
                continue
            block = start - 1 + j
            inside = jnp.logical_and(block >= 0, block < block_total)
            lanes = slice(j * LANES, (j + 1) * LANES)
            smooth[at, lanes] = jnp.where(inside, smooth[at, lanes], 0.0)
    lanes = range(0, outs * LANES, LANES)
    for j, value in enumerate(banded(smooth[...], ramp, lanes)):
        for turn in range(tiles):
            part = value[turn * height : (turn + 1) * height]
            if j == full:
                part = pack(part, groups)
            if part.shape[0] % 16:
                rest = jnp.zeros((-part.shape[0] % 16, LANES), jnp.float32)
                part = jnp.concatenate([part, rest], axis=0)
            at = j * rows_of_block
            outputs[turn][at : at + part.shape[0], :] = part.astype(jnp.bfloat16)


def pack(value, groups):
    rows, wide = value.shape[0] // groups, LANES // groups
    lane = lax.broadcasted_iota(jnp.int32, (rows, LANES), 1)
    packed = value[:rows]
    for group in range(1, groups):
        more = pltpu.roll(value[group * rows : (group + 1) * rows], group * wide, 1)
        packed = jnp.where(lane < group * wide, packed, more)
    return packed


def unpack(value, groups):
    wide = LANES // groups
    rolled = [pltpu.roll(value, (LANES - group * wide) % LANES, 1) for group in range(groups)]
    return jnp.concatenate(rolled, axis=0)


def read(table, index):
    return table[index >> LANE_BITS, index & (LANES - 1)]


def hat_kernel(plan, trig, codes, hats):
    part, half, tile_rows, angle_total = plan
    chunks, depth, pixels = hats.shape
    count = depth // SLOT
    place = lax.axis_index("segment") * lax.axis_size("angle") + lax.axis_index("angle")
    first_row = (place * ROWS_DEV).astype(jnp.float32) - (tile_rows - 1) / 2.0
    lane = lax.broadcasted_iota(jnp.int32, (8, pixels), 1)
    depth_step = lax.broadcasted_iota(jnp.int32, (8, pixels), 0).astype(jnp.float32)
    y = (lane // CHUNK).astype(jnp.float32) + first_row
    x = (lane % CHUNK).astype(jnp.float32)
    rest = jnp.zeros((-DEPTH % 16, pixels), jnp.float32)
    gap = jnp.zeros((SLOT - DEPTH - DEPTH % 16, pixels), jnp.bfloat16)

    def step(index, carry):
        angle = part * count + index
        cosine, sine = read(trig, angle), read(trig, angle_total + angle)
        at = pl.multiple_of(index * SLOT, SLOT)
        start = y * sine + x * cosine - depth_step
        for chunk in range(chunks):
            left = chunk * CHUNK - (TCOLS - 1) / 2.0
            code = read(codes, angle * chunks + chunk)
            low = ((code >> LANE_BITS) * SLOT + (code & (LANES - 1))).astype(jnp.float32)
            across = start + (left * cosine + (half - low))
            rows = [jnp.maximum(0.0, 1.0 - jnp.abs(across - 8.0 * j)) for j in range(DEPTH // 8)]
            rows = jnp.concatenate([*rows, rest], axis=0).astype(jnp.bfloat16)
            hats[chunk, pl.ds(at, rows.shape[0]), :] = rows
            hats[chunk, pl.ds(at + rows.shape[0], gap.shape[0]), :] = gap
        return carry

    lax.fori_loop(0, count, step, 0, unroll=2)


def project_kernel(plan, codes, windows, hats, *refs):
    part, local, last, tiles, height, packing = plan
    full, rows_of_block, groups = packing
    before, (out, held) = refs[:-2], refs[-2:]
    chunks, depth, pixels = hats.shape
    sources = windows.shape[0]
    tail_first = tiles * full * rows_of_block
    slices = height // local
    count = depth // SLOT
    spread = lax.broadcasted_iota(jnp.int32, (height, LANES), 1)
    for source in range(sources):
        if groups > 1:
            tails = windows[source, tail_first:, :].astype(jnp.float32)
        for turn in range(tiles):
            pieces = []
            for j in range(full):
                rows = pl.ds((turn * full + j) * rows_of_block, rows_of_block)
                pieces.append(windows[source, rows, :].astype(held.dtype)[:height])
            if groups > 1:
                tail = height // groups
                tail = tails[turn * tail : (turn + 1) * tail]
                pieces.append(unpack(tail, groups).astype(held.dtype))
            halves = [pltpu.roll(value, SLOT, 1) for value in pieces]
            for j in range(held.shape[1]):
                if j % 2 == 0:
                    value = pieces[j // 2]
                else:
                    value = jnp.where(spread < SLOT, halves[j // 2], halves[j // 2 + 1])
                for angle in range(local):
                    held[source * local + angle, j, turn * slices : (turn + 1) * slices, :] = (
                        value[angle * slices : (angle + 1) * slices]
                    )
    lane = lax.broadcasted_iota(jnp.int32, (slices * tiles, LANES), 1)
    sums = []
    for chunk in range(chunks):
        cut = []
        for first in range(0, count, PER):
            merged = None
            for spot in range(PER):
                index = first + spot
                code = read(codes, (part * count + index) * chunks + chunk)
                turn_by = (spot * SLOT + LANES - (code & (LANES - 1))) & (LANES - 1)
                value = pltpu.roll(held[index, code >> LANE_BITS], turn_by, 1)
                merged = value if spot == 0 else jnp.where(lane < spot * SLOT, merged, value)
            cut.append(merged.astype(jnp.bfloat16))
        value = jnp.dot(
            jnp.concatenate(cut, axis=1), hats[chunk], preferred_element_type=jnp.float32
        )
        if before:
            value = value + before[0][chunk]
        sums.append(value)
        if not last:
            out[chunk] = value
        if not last or (chunk + 1) * CHUNK % LANES:
            continue
        mine = lax.axis_index("tile")
        for row in range(ROWS_DEV):
            value = jnp.concatenate(
                [part[:, row * CHUNK : (row + 1) * CHUNK] for part in sums], axis=1
            )
            at = row * TCOLS + (chunk + 1) * CHUNK - LANES
            if slices % 8 == 0:
                for turn in range(tiles):
                    tile = lax.rem(mine + turn, tiles)
                    into = pl.ds(pl.multiple_of(tile * slices, slices), slices)
                    out[0, into, at : at + LANES] = value[turn * slices : (turn + 1) * slices]
            else:
                out[0, :, at : at + LANES] = pltpu.roll(value, mine * slices, 0)
        sums = []


def shifted(value, axis, by):
    size = lax.axis_size(axis)
    return lax.ppermute(value, axis, [(i, (i - by) % size) for i in range(size)])


def swapped(value, axis, by):
    return lax.ppermute(value, axis, [(i, i ^ by) for i in range(lax.axis_size(axis))])


def body(sinogram, paganin_width, window_block):
    local, slices, bins = sinogram.shape
    segments, spots, tiles = (lax.axis_size(name) for name in ("segment", "angle", "tile"))
    segment, spot = lax.axis_index("segment"), lax.axis_index("angle")
    groups = segments * spots
    angle_total = local * groups
    tile_rows = ROWS_DEV * groups
    reach = math.hypot((TCOLS - 1) / 2, (tile_rows - 1) / 2)
    first_bin = max(0, int(WIN / 2 - reach - 0.01)) // 16 * 16
    last_bin = min(WIN - 1, int(WIN / 2 + reach + 0.01) + 1)
    outs = -(-(last_bin + 1 - first_bin) // LANES)
    assert first_bin + (outs - 1) * LANES < WIN and first_bin < LANES
    assert spots & (spots - 1) == 0 and spots > 1
    smooth_blocks = -(-(outs + 3) // 2) * 2
    chunks, pixels = TCOLS // CHUNK, ROWS_DEV * CHUNK
    half = WIN / 2.0 - first_bin

    smem = pl.BlockSpec(memory_space=pltpu.SMEM)
    vmem = pl.BlockSpec(memory_space=pltpu.VMEM)
    hat_bytes = angle_total * SLOT * ROWS_DEV * TCOLS * 2
    params = pltpu.CompilerParams(vmem_limit_bytes=hat_bytes + 12 * 1024 * 1024)
    height = local * slices
    block_total = bins // LANES
    used = last_bin + 1 - first_bin - (outs - 1) * LANES
    row_groups = LANES // (1 << (used - 1).bit_length())
    if height % (8 * row_groups):
        row_groups = 1
    full = outs if row_groups == 1 else outs - 1
    rows_of_block = -(-height // 16) * 16
    tail = 0 if row_groups == 1 else height // row_groups
    packing = (full, rows_of_block, row_groups)
    bits = [1 << bit for bit in reversed(range(spots.bit_length() - 1))]
    exchanges = [(bits[0],)]
    for first in range(1, len(bits), 2):
        pair = bits[first : first + 2]
        exchanges.append((*pair, sum(pair)) if len(pair) == 2 else tuple(pair))
    reached = [0]
    for masks in exchanges:
        reached = [other ^ mask for mask in (0, *masks) for other in reached]
    order = np.repeat(np.array(reached), local), np.tile(np.arange(local), spots)
    where = np.arange(groups)[:, None]
    by = np.arange(segments)[:, None] + where[:, :, None] // spots
    angles = (where % spots ^ order[0]) * local + order[1]
    angles = by % segments * (spots * local) + angles[:, None]
    theta = math.pi * angles.reshape(groups, angle_total) / angle_total
    cosine, sine = np.cos(theta), np.sin(theta)
    left = np.arange(chunks) * CHUNK - (TCOLS - 1) / 2.0
    edges = np.minimum(cosine[..., None] * left, cosine[..., None] * (left + (CHUNK - 1)))
    top = where * ROWS_DEV - (tile_rows - 1) / 2.0
    rise = np.minimum(sine * top, sine * (top + (ROWS_DEV - 1)))
    lows = np.floor(edges + rise[..., None] + (half - 0.01)).astype(np.int32)
    blocks = np.minimum(lows // SLOT, PER * (outs - 1))
    codes = (blocks << LANE_BITS) + lows - blocks * SLOT

    def in_rows(values):
        values = values.reshape(groups, -1)
        rows = -(-values.shape[1] // (8 * LANES)) * 8
        values = np.pad(values, ((0, 0), (0, rows * LANES - values.shape[1])))
        return jnp.asarray(values.reshape(groups, rows, LANES))

    trig_table = in_rows(np.concatenate([cosine, sine], axis=1).astype(np.float32))
    code_table = in_rows(codes.astype(np.int32))

    *cut, trig, codes = pl.pallas_call(
        functools.partial(filter_kernel, (tiles, outs, first_bin, packing)),
        out_shape=[
            jax.ShapeDtypeStruct((full * rows_of_block + -(-tail // 16) * 16, LANES), jnp.bfloat16)
        ]
        * tiles
        + [jax.ShapeDtypeStruct(v.shape[1:], v.dtype) for v in (trig_table, code_table)],
        in_specs=[smem] + [pl.BlockSpec(memory_space=pltpu.HBM)] * 4,
        out_specs=[vmem] * (tiles + 2),
        scratch_shapes=[
            pltpu.SMEM(window_block.T.shape, jnp.int32),
            pltpu.VMEM(
                (local, slices, (block_total - WIN // LANES + smooth_blocks + 2) * LANES),
                jnp.float32,
            ),
            pltpu.VMEM((height * tiles, (smooth_blocks + 2) * LANES), jnp.float32),
            pltpu.VMEM((height * tiles, smooth_blocks * LANES), jnp.float32),
            pltpu.SemaphoreType.DMA((local + 3,)),
        ],
        compiler_params=params,
        name="filter",
    )(
        paganin_width,
        *(
            pltpu.with_memory_space_constraint(value, pltpu.HBM)
            for value in (window_block.T, trig_table, code_table, sinogram)
        ),
    )

    depth = spots * local * SLOT
    def hats_of(part, after):
        ready = lax.optimization_barrier((trig, codes, *after))[:2]
        return pl.pallas_call(
            functools.partial(hat_kernel, (part, half, tile_rows, angle_total)),
            out_shape=jax.ShapeDtypeStruct((chunks, depth, pixels), jnp.bfloat16),
            in_specs=[smem, smem],
            out_specs=vmem,
            compiler_params=params,
            cost_estimate=pl.CostEstimate(
                flops=chunks * depth * pixels * 16, bytes_accessed=0, transcendentals=0
            ),
            name="hats",
        )(*ready)

    hats = []

    def beside(moved, after, count):
        made = []
        for _ in range(min(count, segments - len(hats))):
            made.append(hats_of(len(hats), after))
            hats.append(None)
        moved, made = lax.optimization_barrier((moved, made))
        hats[len(hats) - len(made) :] = made
        return moved

    def joint(turn, mask):
        def index(spot, tile):
            return (spot ^ mask) * tiles + (tile - turn) % tiles

        pairs = [(at, index(at // tiles, at % tiles)) for at in range(spots * tiles)]
        return lax.ppermute(cut[turn], ("angle", "tile"), pairs)

    near = [(turn, mask) for mask in (0, *exchanges[0]) for turn in range(tiles)][1:]
    moved = beside([joint(*pair) for pair in near], cut, 1)
    pieces = jnp.stack([cut[0], *moved])
    whole = full * rows_of_block
    if tail:
        main = pieces[:, :whole].reshape(2, tiles * whole, LANES)
        tails = pieces[:, whole : whole + tail].reshape(2, tiles * tail, LANES)
        pieces = jnp.concatenate([main, tails], axis=1)
    else:
        pieces = pieces.reshape(2, tiles * whole, LANES)
    for index, masks in enumerate(exchanges[1:]):
        moved = [swapped(pieces, "angle", mask) for mask in masks]
        last = index == len(exchanges) - 2
        moved = beside(moved, (pieces,), segments if last else 1)
        pieces = jnp.concatenate([pieces, *moved])
    held_type = jnp.bfloat16 if slices % 16 == 0 else jnp.float32
    parts = [pieces] + [shifted(pieces, "segment", by) for by in range(1, segments)]
    sums = ()
    for by, windows in enumerate(parts):
        last = by == segments - 1
        value = pl.pallas_call(
            functools.partial(project_kernel, (by, local, last, tiles, height, packing)),
            out_shape=jax.ShapeDtypeStruct(
                (1, slices * tiles, ROWS_DEV * TCOLS)
                if last
                else (chunks, slices * tiles, pixels),
                jnp.float32,
            ),
            in_specs=[smem] + [vmem] * (2 + len(sums)),
            out_specs=vmem,
            scratch_shapes=[
                pltpu.VMEM((spots * local, PER * (outs - 1) + 1, slices * tiles, LANES), held_type),
            ],
            compiler_params=params,
            cost_estimate=pl.CostEstimate(
                flops=32 * slices * tiles * chunks * depth * pixels,
                bytes_accessed=0,
                transcendentals=0,
            ),
            name="project",
        )(codes, windows, hats[by], *sums)
        sums = (value,)
    return sums[0]


def solution(mesh):
    in_specs = (P(("segment", "angle"), "tile", None), P(), P())
    out_specs = P("tile", None, ("segment", "angle"))
    return jax.shard_map(body, mesh=mesh, in_specs=in_specs, out_specs=out_specs, check_vma=False)
```

```python
import functools
import math

import jax
import jax.numpy as jnp
import numpy as np
from jax import lax
from jax.experimental import pallas as pl
from jax.experimental.pallas import tpu as pltpu
from jax.sharding import PartitionSpec as P

WIN = 512
BAND = 128
ROWS_DEV = 8
TCOLS = 256
LANES = 128
LANE_BITS = 7
CHUNK = 32
DEPTH = 40
SLOT = 64
PER = LANES // SLOT


def split(value):
    high = value.astype(jnp.bfloat16)
    return high, (value - high.astype(jnp.float32)).astype(jnp.bfloat16)


def banded(value, taps, starts):
    tap_high, tap_low = taps
    dot = functools.partial(jnp.dot, preferred_element_type=jnp.float32)
    cut = [value[:, start : start + tap_high.shape[0]] for start in starts]
    high, low = split(jnp.concatenate(cut, axis=0))
    both = dot(jnp.concatenate([high, low], axis=0), tap_high)
    result = both[: high.shape[0]] + (both[high.shape[0] :] + dot(high, tap_low))
    rows = value.shape[0]
    return [result[index * rows : (index + 1) * rows] for index in range(len(starts))]


def offsets(depth, width, shift):
    return (
        lax.broadcasted_iota(jnp.int32, (depth, width), 0)
        - lax.broadcasted_iota(jnp.int32, (depth, width), 1)
        - shift
    )


def filter_kernel(plan, width, blocks_ref, trig_table, code_table, rows_ref, *refs):
    tiles, outs, first_bin, packing = plan
    full, rows_of_block, groups = packing
    outputs, (trig, codes, blocks, padded, raw, smooth, arrived) = (
        refs[:tiles],
        refs[tiles:],
    )
    local, slices, bins = rows_ref.shape
    block_total = bins // LANES
    raw_wide = raw.shape[1]
    smooth_blocks = smooth.shape[1] // LANES
    height = local * slices
    ahead = 2 * LANES

    place = lax.axis_index("segment") * lax.axis_size("angle") + lax.axis_index("angle")
    sources = [(rows_ref.at[i], padded.at[i, :, pl.ds(ahead, bins)]) for i in range(local)]
    sources = [
        *sources,
        (blocks_ref, blocks),
        (trig_table.at[place], trig),
        (code_table.at[place], codes),
    ]
    copies = [
        pltpu.make_async_copy(source, into, arrived.at[index])
        for index, (source, into) in enumerate(sources)
    ]
    for copy in copies:
        copy.start()
    behind = padded.shape[2] - ahead - bins
    padded[:, :, :ahead] = jnp.zeros((local, slices, ahead), jnp.float32)
    padded[:, :, ahead + bins :] = jnp.zeros((local, slices, behind), jnp.float32)

    away = offsets(512, LANES, BAND + first_bin)
    spread = jnp.abs(away)
    squared = jnp.maximum(spread * spread, 1).astype(jnp.float32)
    odd = jnp.logical_and(spread <= BAND, (spread & 1) == 1)
    ramp = jnp.where(odd, -1.0 / (math.pi * math.pi * squared), 0.0)
    ramp = split(jnp.where(away == 0, 0.25, ramp))
    decay = width[0]
    steps = (lax.broadcasted_iota(jnp.int32, (1, BAND), 1) + 1).astype(jnp.float32)
    total = 1.0 + 2.0 * jnp.sum(jnp.exp(-steps / decay), axis=1, keepdims=True)
    away = offsets(2 * 256, 256, BAND)
    spread = jnp.abs(away)
    paganin = jnp.where(
        spread <= BAND, jnp.exp(-spread.astype(jnp.float32) / decay) / total, 0.0
    )
    paganin = split(paganin)

    for copy in copies:
        copy.wait()
    first = place * local
    mine = lax.axis_index("tile")
    starts = []
    for turn in range(tiles):
        tile = lax.rem(mine - turn + tiles, tiles)
        for angle in range(local):
            start = blocks[tile, first + angle]
            starts.append(start)
            at = (turn * local + angle) * slices
            lanes = pl.ds(pl.multiple_of(start * LANES, LANES), raw_wide)
            raw[at : at + slices, :] = padded[angle, :, lanes]
    pairs = range(0, smooth_blocks * LANES, 256)
    for at, value in zip(pairs, banded(raw[...], paganin, pairs)):
        smooth[:, at : at + 256] = value
    for index, start in enumerate(starts):
        at = slice(index * slices, (index + 1) * slices)
        for j in range(smooth_blocks):
            if 1 <= j <= WIN // LANES:
                continue
            block = start - 1 + j
            inside = jnp.logical_and(block >= 0, block < block_total)
            lanes = slice(j * LANES, (j + 1) * LANES)
            smooth[at, lanes] = jnp.where(inside, smooth[at, lanes], 0.0)
    lanes = range(0, outs * LANES, LANES)
    for j, value in enumerate(banded(smooth[...], ramp, lanes)):
        for turn in range(tiles):
            part = value[turn * height : (turn + 1) * height]
            if j == full:
                part = pack(part, groups)
            if part.shape[0] % 16:
                rest = jnp.zeros((-part.shape[0] % 16, LANES), jnp.float32)
                part = jnp.concatenate([part, rest], axis=0)
            at = j * rows_of_block
            outputs[turn][at : at + part.shape[0], :] = part.astype(jnp.bfloat16)


def pack(value, groups):
    rows, wide = value.shape[0] // groups, LANES // groups
    lane = lax.broadcasted_iota(jnp.int32, (rows, LANES), 1)
    packed = value[:rows]
    for group in range(1, groups):
        more = pltpu.roll(value[group * rows : (group + 1) * rows], group * wide, 1)
        packed = jnp.where(lane < group * wide, packed, more)
    return packed


def unpack(value, groups):
    wide = LANES // groups
    rolled = [pltpu.roll(value, (LANES - group * wide) % LANES, 1) for group in range(groups)]
    return jnp.concatenate(rolled, axis=0)


def read(table, index):
    return table[index >> LANE_BITS, index & (LANES - 1)]


def hat_kernel(plan, trig, codes, hats):
    part, half, tile_rows, angle_total = plan
    chunks, depth, pixels = hats.shape
    count = depth // SLOT
    place = lax.axis_index("segment") * lax.axis_size("angle") + lax.axis_index("angle")
    first_row = (place * ROWS_DEV).astype(jnp.float32) - (tile_rows - 1) / 2.0
    lane = lax.broadcasted_iota(jnp.int32, (8, pixels), 1)
    depth_step = lax.broadcasted_iota(jnp.int32, (8, pixels), 0).astype(jnp.float32)
    y = (lane // CHUNK).astype(jnp.float32) + first_row
    x = (lane % CHUNK).astype(jnp.float32)
    rest = jnp.zeros((-DEPTH % 16, pixels), jnp.float32)
    gap = jnp.zeros((SLOT - DEPTH - DEPTH % 16, pixels), jnp.bfloat16)

    def step(index, carry):
        angle = part * count + index
        cosine, sine = read(trig, angle), read(trig, angle_total + angle)
        at = pl.multiple_of(index * SLOT, SLOT)
        start = y * sine + x * cosine - depth_step
        for chunk in range(chunks):
            left = chunk * CHUNK - (TCOLS - 1) / 2.0
            code = read(codes, angle * chunks + chunk)
            low = ((code >> LANE_BITS) * SLOT + (code & (LANES - 1))).astype(jnp.float32)
            across = start + (left * cosine + (half - low))
            rows = [jnp.maximum(0.0, 1.0 - jnp.abs(across - 8.0 * j)) for j in range(DEPTH // 8)]
            rows = jnp.concatenate([*rows, rest], axis=0).astype(jnp.bfloat16)
            hats[chunk, pl.ds(at, rows.shape[0]), :] = rows
            hats[chunk, pl.ds(at + rows.shape[0], gap.shape[0]), :] = gap
        return carry

    lax.fori_loop(0, count, step, 0, unroll=2)


def project_kernel(plan, codes, *refs):
    parts, sources, arrays, segments, local, last, tiles, height, packing = plan
    full, rows_of_block, groups = packing
    windows, refs = refs[:arrays], refs[arrays:]
    windows = [(window, source) for window in windows for source in range(window.shape[0])]
    hats, before, (out, held) = refs[:segments], refs[segments:-2], refs[-2:]
    chunks, depth, pixels = hats[0].shape
    tail_first = tiles * full * rows_of_block
    slices = height // local
    count = sources * local
    angle_count = depth // SLOT
    spread = lax.broadcasted_iota(jnp.int32, (height, LANES), 1)
    for at, (window, source) in enumerate(windows):
        if groups > 1:
            tails = window[source, tail_first:, :].astype(jnp.float32)
        for turn in range(tiles):
            pieces = []
            for j in range(full):
                rows = pl.ds((turn * full + j) * rows_of_block, rows_of_block)
                pieces.append(window[source, rows, :].astype(held.dtype)[:height])
            if groups > 1:
                tail = height // groups
                tail = tails[turn * tail : (turn + 1) * tail]
                pieces.append(unpack(tail, groups).astype(held.dtype))
            halves = [pltpu.roll(value, SLOT, 1) for value in pieces]
            for j in range(held.shape[1]):
                if j % 2 == 0:
                    value = pieces[j // 2]
                else:
                    value = jnp.where(spread < SLOT, halves[j // 2], halves[j // 2 + 1])
                for angle in range(local):
                    held[at * local + angle, j, turn * slices : (turn + 1) * slices, :] = value[
                        angle * slices : (angle + 1) * slices
                    ]
    lane = lax.broadcasted_iota(jnp.int32, (slices * tiles, LANES), 1)
    sums = []
    for chunk in range(chunks):
        value = before[0][chunk] if before else None
        for at, (by, part) in enumerate(parts):
            cut = []
            for first in range(0, count, PER):
                merged = None
                for spot in range(PER):
                    index = first + spot
                    code = read(codes, (by * angle_count + part * count + index) * chunks + chunk)
                    turn_by = (spot * SLOT + LANES - (code & (LANES - 1))) & (LANES - 1)
                    piece = pltpu.roll(held[at * count + index, code >> LANE_BITS], turn_by, 1)
                    merged = piece if spot == 0 else jnp.where(lane < spot * SLOT, merged, piece)
                cut.append(merged.astype(jnp.bfloat16))
            rows = pl.ds(part * count * SLOT, count * SLOT)
            more = jnp.dot(
                jnp.concatenate(cut, axis=1),
                hats[by][chunk, rows, :],
                preferred_element_type=jnp.float32,
            )
            value = more if value is None else value + more
        sums.append(value)
        if not last:
            out[chunk] = value
        if not last or (chunk + 1) * CHUNK % LANES:
            continue
        mine = lax.axis_index("tile")
        for row in range(ROWS_DEV):
            value = jnp.concatenate(
                [part[:, row * CHUNK : (row + 1) * CHUNK] for part in sums], axis=1
            )
            at = row * TCOLS + (chunk + 1) * CHUNK - LANES
            if slices % 8 == 0:
                for turn in range(tiles):
                    tile = lax.rem(mine + turn, tiles)
                    into = pl.ds(pl.multiple_of(tile * slices, slices), slices)
                    out[0, into, at : at + LANES] = value[turn * slices : (turn + 1) * slices]
            else:
                out[0, :, at : at + LANES] = pltpu.roll(value, mine * slices, 0)
        sums = []


def shifted(value, axis, by):
    size = lax.axis_size(axis)
    return lax.ppermute(value, axis, [(i, (i - by) % size) for i in range(size)])


def swapped(value, axis, by):
    return lax.ppermute(value, axis, [(i, i ^ by) for i in range(lax.axis_size(axis))])


def body(sinogram, paganin_width, window_block):
    local, slices, bins = sinogram.shape
    segments, spots, tiles = (lax.axis_size(name) for name in ("segment", "angle", "tile"))
    segment, spot = lax.axis_index("segment"), lax.axis_index("angle")
    groups = segments * spots
    angle_total = local * groups
    tile_rows = ROWS_DEV * groups
    reach = math.hypot((TCOLS - 1) / 2, (tile_rows - 1) / 2)
    first_bin = max(0, int(WIN / 2 - reach - 0.01)) // 16 * 16
    last_bin = min(WIN - 1, int(WIN / 2 + reach + 0.01) + 1)
    outs = -(-(last_bin + 1 - first_bin) // LANES)
    assert first_bin + (outs - 1) * LANES < WIN and first_bin < LANES
    assert spots & (spots - 1) == 0 and spots > 1
    smooth_blocks = -(-(outs + 3) // 2) * 2
    chunks, pixels = TCOLS // CHUNK, ROWS_DEV * CHUNK
    half = WIN / 2.0 - first_bin

    smem = pl.BlockSpec(memory_space=pltpu.SMEM)
    vmem = pl.BlockSpec(memory_space=pltpu.VMEM)
    hat_bytes = angle_total * SLOT * ROWS_DEV * TCOLS * 2
    params = pltpu.CompilerParams(vmem_limit_bytes=hat_bytes + 12 * 1024 * 1024)
    height = local * slices
    block_total = bins // LANES
    used = last_bin + 1 - first_bin - (outs - 1) * LANES
    row_groups = LANES // (1 << (used - 1).bit_length())
    if height % (8 * row_groups):
        row_groups = 1
    full = outs if row_groups == 1 else outs - 1
    rows_of_block = -(-height // 16) * 16
    tail = 0 if row_groups == 1 else height // row_groups
    packing = (full, rows_of_block, row_groups)
    bits = [1 << bit for bit in reversed(range(spots.bit_length() - 1))]
    exchanges = [(bits[0],)]
    for first in range(1, len(bits), 2):
        pair = bits[first : first + 2]
        exchanges.append((*pair, sum(pair)) if len(pair) == 2 else tuple(pair))
    reached = [0]
    for masks in exchanges:
        reached = [other ^ mask for mask in (0, *masks) for other in reached]
    order = np.repeat(np.array(reached), local), np.tile(np.arange(local), spots)
    where = np.arange(groups)[:, None]
    by = np.arange(segments)[:, None] + where[:, :, None] // spots
    angles = (where % spots ^ order[0]) * local + order[1]
    angles = by % segments * (spots * local) + angles[:, None]
    theta = math.pi * angles.reshape(groups, angle_total) / angle_total
    cosine, sine = np.cos(theta), np.sin(theta)
    left = np.arange(chunks) * CHUNK - (TCOLS - 1) / 2.0
    edges = np.minimum(cosine[..., None] * left, cosine[..., None] * (left + (CHUNK - 1)))
    top = where * ROWS_DEV - (tile_rows - 1) / 2.0
    rise = np.minimum(sine * top, sine * (top + (ROWS_DEV - 1)))
    lows = np.floor(edges + rise[..., None] + (half - 0.01)).astype(np.int32)
    blocks = np.minimum(lows // SLOT, PER * (outs - 1))
    codes = (blocks << LANE_BITS) + lows - blocks * SLOT

    def in_rows(values):
        values = values.reshape(groups, -1)
        rows = -(-values.shape[1] // (8 * LANES)) * 8
        values = np.pad(values, ((0, 0), (0, rows * LANES - values.shape[1])))
        return jnp.asarray(values.reshape(groups, rows, LANES))

    trig_table = in_rows(np.concatenate([cosine, sine], axis=1).astype(np.float32))
    code_table = in_rows(codes.astype(np.int32))

    *cut, trig, codes = pl.pallas_call(
        functools.partial(filter_kernel, (tiles, outs, first_bin, packing)),
        out_shape=[
            jax.ShapeDtypeStruct((full * rows_of_block + -(-tail // 16) * 16, LANES), jnp.bfloat16)
        ]
        * tiles
        + [jax.ShapeDtypeStruct(v.shape[1:], v.dtype) for v in (trig_table, code_table)],
        in_specs=[smem] + [pl.BlockSpec(memory_space=pltpu.HBM)] * 4,
        out_specs=[vmem] * (tiles + 2),
        scratch_shapes=[
            pltpu.SMEM(window_block.T.shape, jnp.int32),
            pltpu.VMEM(
                (local, slices, (block_total - WIN // LANES + smooth_blocks + 2) * LANES),
                jnp.float32,
            ),
            pltpu.VMEM((height * tiles, (smooth_blocks + 2) * LANES), jnp.float32),
            pltpu.VMEM((height * tiles, smooth_blocks * LANES), jnp.float32),
            pltpu.SemaphoreType.DMA((local + 3,)),
        ],
        compiler_params=params,
        name="filter",
    )(
        paganin_width,
        *(
            pltpu.with_memory_space_constraint(value, pltpu.HBM)
            for value in (window_block.T, trig_table, code_table, sinogram)
        ),
    )

    depth = spots * local * SLOT
    def hats_of(part, after):
        ready = lax.optimization_barrier((trig, codes, *after))[:2]
        return pl.pallas_call(
            functools.partial(hat_kernel, (part, half, tile_rows, angle_total)),
            out_shape=jax.ShapeDtypeStruct((chunks, depth, pixels), jnp.bfloat16),
            in_specs=[smem, smem],
            out_specs=vmem,
            compiler_params=params,
            cost_estimate=pl.CostEstimate(
                flops=chunks * depth * pixels * 16, bytes_accessed=0, transcendentals=0
            ),
            name="hats",
        )(*ready)

    hats = []

    def beside(moved, after, count):
        made = []
        for _ in range(min(count, segments - len(hats))):
            made.append(hats_of(len(hats), after))
            hats.append(None)
        moved, made = lax.optimization_barrier((moved, made))
        hats[len(hats) - len(made) :] = made
        return moved

    def joint(turn, mask):
        def index(spot, tile):
            return (spot ^ mask) * tiles + (tile - turn) % tiles

        pairs = [(at, index(at // tiles, at % tiles)) for at in range(spots * tiles)]
        return lax.ppermute(cut[turn], ("angle", "tile"), pairs)

    near = [(turn, mask) for mask in (0, *exchanges[0]) for turn in range(tiles)][1:]
    moved = beside([joint(*pair) for pair in near], cut, 1)
    pieces = jnp.stack([cut[0], *moved])
    whole = full * rows_of_block
    if tail:
        main = pieces[:, :whole].reshape(2, tiles * whole, LANES)
        tails = pieces[:, whole : whole + tail].reshape(2, tiles * tail, LANES)
        pieces = jnp.concatenate([main, tails], axis=1)
    else:
        pieces = pieces.reshape(2, tiles * whole, LANES)
    for masks in exchanges[1:-1]:
        moved = beside([swapped(pieces, "angle", mask) for mask in masks], (pieces,), 1)
        pieces = jnp.concatenate([pieces, *moved])
    held_type = jnp.bfloat16 if slices % 16 == 0 else jnp.float32
    sources = pieces.shape[0]

    def project(parts, windows, sums, last=False):
        return pl.pallas_call(
            functools.partial(
                project_kernel,
                (parts, sources, len(windows), segments, local, last, tiles, height, packing),
            ),
            out_shape=jax.ShapeDtypeStruct(
                (1, slices * tiles, ROWS_DEV * TCOLS)
                if last
                else (chunks, slices * tiles, pixels),
                jnp.float32,
            ),
            in_specs=[smem] + [vmem] * (len(windows) + segments + len(sums)),
            out_specs=vmem,
            scratch_shapes=[
                pltpu.VMEM(
                    (
                        len(parts) * sources * local,
                        PER * (outs - 1) + 1,
                        slices * tiles,
                        LANES,
                    ),
                    held_type,
                ),
            ],
            compiler_params=params,
            cost_estimate=pl.CostEstimate(
                flops=32 * slices * tiles * chunks * depth * pixels,
                bytes_accessed=0,
                transcendentals=0,
            ),
            name="project",
        )(codes, *windows, *hats, *sums)

    others = range(1, segments)
    early = [pieces] + [shifted(pieces, "segment", by) for by in others]
    moved = [swapped(pieces, "angle", mask) for mask in exchanges[-1]]
    hats += [hats_of(part, (pieces,)) for part in range(len(hats), segments)]
    count = len(moved)
    if count > 1:
        early, moved[-1] = lax.optimization_barrier((early, moved[-1]))
    sums = project([(by, 0) for by in range(segments)], early, ())
    if count > 1:
        moved[:-1], sums = lax.optimization_barrier((moved[:-1], sums))
    else:
        moved, sums = lax.optimization_barrier((moved, sums))
    ahead = [shifted(moved[-1], "segment", by) for by in others]
    final = [(by, part) for by in others for part in range(1, count)]
    if final:
        rest = jnp.concatenate(moved[:-1])
        late = [shifted(rest, "segment", by) for by in others]
    own = [(0, part + 1) for part in range(count)]
    first = [(by, count) for by in others]
    if final:
        sums = project(own + first, [*moved, *ahead], (sums,))
        return project(final, late, (sums,), True)
    sums = project(own, moved, (sums,))
    return project(first, ahead, (sums,), True)


def solution(mesh):
    in_specs = (P(("segment", "angle"), "tile", None), P(), P())
    out_specs = P("tile", None, ("segment", "angle"))
    return jax.shard_map(body, mesh=mesh, in_specs=in_specs, out_specs=out_specs, check_vma=False)
```

```python
import functools
import math

import jax
import jax.numpy as jnp
import numpy as np
from jax import lax
from jax.experimental import pallas as pl
from jax.experimental.pallas import tpu as pltpu
from jax.sharding import PartitionSpec as P

WIN = 512
BAND = 128
ROWS_DEV = 8
TCOLS = 256
LANES = 128
LANE_BITS = 7
CHUNK = 32
DEPTH = 40
SLOT = 64
PER = LANES // SLOT


def split(value):
    high = value.astype(jnp.bfloat16)
    return high, (value - high.astype(jnp.float32)).astype(jnp.bfloat16)


def banded(value, taps, starts):
    tap_high, tap_low = taps
    dot = functools.partial(jnp.dot, preferred_element_type=jnp.float32)
    cut = [value[:, start : start + tap_high.shape[0]] for start in starts]
    high, low = split(jnp.concatenate(cut, axis=0))
    both = dot(jnp.concatenate([high, low], axis=0), tap_high)
    result = both[: high.shape[0]] + (both[high.shape[0] :] + dot(high, tap_low))
    rows = value.shape[0]
    return [result[index * rows : (index + 1) * rows] for index in range(len(starts))]


def offsets(depth, width, shift):
    return (
        lax.broadcasted_iota(jnp.int32, (depth, width), 0)
        - lax.broadcasted_iota(jnp.int32, (depth, width), 1)
        - shift
    )


def filter_kernel(plan, width, blocks_ref, trig_table, code_table, rows_ref, *refs):
    tiles, outs, first_bin, packing = plan
    full, rows_of_block, groups = packing
    outputs, (trig, codes, blocks, padded, raw, smooth, arrived) = (
        refs[:tiles],
        refs[tiles:],
    )
    local, slices, bins = rows_ref.shape
    block_total = bins // LANES
    raw_wide = raw.shape[1]
    smooth_blocks = smooth.shape[1] // LANES
    height = local * slices
    ahead = 2 * LANES

    place = lax.axis_index("segment") * lax.axis_size("angle") + lax.axis_index("angle")
    sources = [(rows_ref.at[i], padded.at[i, :, pl.ds(ahead, bins)]) for i in range(local)]
    sources = [
        *sources,
        (blocks_ref, blocks),
        (trig_table.at[place], trig),
        (code_table.at[place], codes),
    ]
    copies = [
        pltpu.make_async_copy(source, into, arrived.at[index])
        for index, (source, into) in enumerate(sources)
    ]
    for copy in copies:
        copy.start()
    behind = padded.shape[2] - ahead - bins
    padded[:, :, :ahead] = jnp.zeros((local, slices, ahead), jnp.float32)
    padded[:, :, ahead + bins :] = jnp.zeros((local, slices, behind), jnp.float32)

    away = offsets(512, LANES, BAND + first_bin)
    spread = jnp.abs(away)
    squared = jnp.maximum(spread * spread, 1).astype(jnp.float32)
    odd = jnp.logical_and(spread <= BAND, (spread & 1) == 1)
    ramp = jnp.where(odd, -1.0 / (math.pi * math.pi * squared), 0.0)
    ramp = split(jnp.where(away == 0, 0.25, ramp))
    decay = width[0]
    steps = (lax.broadcasted_iota(jnp.int32, (1, BAND), 1) + 1).astype(jnp.float32)
    total = 1.0 + 2.0 * jnp.sum(jnp.exp(-steps / decay), axis=1, keepdims=True)
    away = offsets(2 * 256, 256, BAND)
    spread = jnp.abs(away)
    paganin = jnp.where(
        spread <= BAND, jnp.exp(-spread.astype(jnp.float32) / decay) / total, 0.0
    )
    paganin = split(paganin)

    for copy in copies:
        copy.wait()
    first = place * local
    mine = lax.axis_index("tile")
    starts = []
    for turn in range(tiles):
        tile = lax.rem(mine - turn + tiles, tiles)
        for angle in range(local):
            start = blocks[tile, first + angle]
            starts.append(start)
            at = (turn * local + angle) * slices
            lanes = pl.ds(pl.multiple_of(start * LANES, LANES), raw_wide)
            raw[at : at + slices, :] = padded[angle, :, lanes]
    pairs = range(0, smooth_blocks * LANES, 256)
    for at, value in zip(pairs, banded(raw[...], paganin, pairs)):
        smooth[:, at : at + 256] = value
    for index, start in enumerate(starts):
        at = slice(index * slices, (index + 1) * slices)
        for j in range(smooth_blocks):
            if 1 <= j <= WIN // LANES:
                continue
            block = start - 1 + j
            inside = jnp.logical_and(block >= 0, block < block_total)
            lanes = slice(j * LANES, (j + 1) * LANES)
            smooth[at, lanes] = jnp.where(inside, smooth[at, lanes], 0.0)
    lanes = range(0, outs * LANES, LANES)
    for j, value in enumerate(banded(smooth[...], ramp, lanes)):
        for turn in range(tiles):
            part = value[turn * height : (turn + 1) * height]
            if j == full:
                part = pack(part, groups)
            if part.shape[0] % 16:
                rest = jnp.zeros((-part.shape[0] % 16, LANES), jnp.float32)
                part = jnp.concatenate([part, rest], axis=0)
            at = j * rows_of_block
            outputs[turn][at : at + part.shape[0], :] = part.astype(jnp.bfloat16)


def pack(value, groups):
    rows, wide = value.shape[0] // groups, LANES // groups
    lane = lax.broadcasted_iota(jnp.int32, (rows, LANES), 1)
    packed = value[:rows]
    for group in range(1, groups):
        more = pltpu.roll(value[group * rows : (group + 1) * rows], group * wide, 1)
        packed = jnp.where(lane < group * wide, packed, more)
    return packed


def unpack(value, groups):
    wide = LANES // groups
    rolled = [pltpu.roll(value, (LANES - group * wide) % LANES, 1) for group in range(groups)]
    return jnp.concatenate(rolled, axis=0)


def read(table, index):
    return table[index >> LANE_BITS, index & (LANES - 1)]


def hat_kernel(plan, trig, codes, hats):
    part, half, tile_rows, angle_total = plan
    chunks, depth, pixels = hats.shape
    count = depth // SLOT
    place = lax.axis_index("segment") * lax.axis_size("angle") + lax.axis_index("angle")
    first_row = (place * ROWS_DEV).astype(jnp.float32) - (tile_rows - 1) / 2.0
    lane = lax.broadcasted_iota(jnp.int32, (8, pixels), 1)
    depth_step = lax.broadcasted_iota(jnp.int32, (8, pixels), 0).astype(jnp.float32)
    y = (lane // CHUNK).astype(jnp.float32) + first_row
    x = (lane % CHUNK).astype(jnp.float32)
    rest = jnp.zeros((-DEPTH % 16, pixels), jnp.float32)
    gap = jnp.zeros((SLOT - DEPTH - DEPTH % 16, pixels), jnp.bfloat16)

    def step(index, carry):
        angle = part * count + index
        cosine, sine = read(trig, angle), read(trig, angle_total + angle)
        at = pl.multiple_of(index * SLOT, SLOT)
        start = y * sine + x * cosine - depth_step
        for chunk in range(chunks):
            left = chunk * CHUNK - (TCOLS - 1) / 2.0
            code = read(codes, angle * chunks + chunk)
            low = ((code >> LANE_BITS) * SLOT + (code & (LANES - 1))).astype(jnp.float32)
            across = start + (left * cosine + (half - low))
            rows = [jnp.maximum(0.0, 1.0 - jnp.abs(across - 8.0 * j)) for j in range(DEPTH // 8)]
            rows = jnp.concatenate([*rows, rest], axis=0).astype(jnp.bfloat16)
            hats[chunk, pl.ds(at, rows.shape[0]), :] = rows
            hats[chunk, pl.ds(at + rows.shape[0], gap.shape[0]), :] = gap
        return carry

    lax.fori_loop(0, count, step, 0, unroll=2)


def project_kernel(plan, codes, *refs):
    parts, sources, arrays, segments, local, last, tiles, height, packing = plan
    full, rows_of_block, groups = packing
    windows, refs = refs[:arrays], refs[arrays:]
    windows = [(window, source) for window in windows for source in range(window.shape[0])]
    hats, before, (out, held) = refs[:segments], refs[segments:-2], refs[-2:]
    chunks, depth, pixels = hats[0].shape
    tail_first = tiles * full * rows_of_block
    slices = height // local
    count = sources * local
    angle_count = depth // SLOT
    spread = lax.broadcasted_iota(jnp.int32, (height, LANES), 1)
    for at, (window, source) in enumerate(windows):
        if groups > 1:
            tails = window[source, tail_first:, :].astype(jnp.float32)
        for turn in range(tiles):
            pieces = []
            for j in range(full):
                rows = pl.ds((turn * full + j) * rows_of_block, rows_of_block)
                pieces.append(window[source, rows, :].astype(held.dtype)[:height])
            if groups > 1:
                tail = height // groups
                tail = tails[turn * tail : (turn + 1) * tail]
                pieces.append(unpack(tail, groups).astype(held.dtype))
            halves = [pltpu.roll(value, SLOT, 1) for value in pieces]
            for j in range(held.shape[1]):
                if j % 2 == 0:
                    value = pieces[j // 2]
                else:
                    value = jnp.where(spread < SLOT, halves[j // 2], halves[j // 2 + 1])
                for angle in range(local):
                    held[at * local + angle, j, turn * slices : (turn + 1) * slices, :] = value[
                        angle * slices : (angle + 1) * slices
                    ]
    lane = lax.broadcasted_iota(jnp.int32, (slices * tiles, LANES), 1)
    sums = []
    for chunk in range(chunks):
        value = before[0][chunk] if before else None
        for at, (by, part) in enumerate(parts):
            cut = []
            for first in range(0, count, PER):
                merged = None
                for spot in range(PER):
                    index = first + spot
                    code = read(codes, (by * angle_count + part * count + index) * chunks + chunk)
                    turn_by = (spot * SLOT + LANES - (code & (LANES - 1))) & (LANES - 1)
                    piece = pltpu.roll(held[at * count + index, code >> LANE_BITS], turn_by, 1)
                    merged = piece if spot == 0 else jnp.where(lane < spot * SLOT, merged, piece)
                cut.append(merged.astype(jnp.bfloat16))
            rows = pl.ds(part * count * SLOT, count * SLOT)
            more = jnp.dot(
                jnp.concatenate(cut, axis=1),
                hats[by][chunk, rows, :],
                preferred_element_type=jnp.float32,
            )
            value = more if value is None else value + more
        sums.append(value)
        if not last:
            out[chunk] = value
        if not last or (chunk + 1) * CHUNK % LANES:
            continue
        mine = lax.axis_index("tile")
        for row in range(ROWS_DEV):
            value = jnp.concatenate(
                [part[:, row * CHUNK : (row + 1) * CHUNK] for part in sums], axis=1
            )
            at = row * TCOLS + (chunk + 1) * CHUNK - LANES
            if slices % 8 == 0:
                for turn in range(tiles):
                    tile = lax.rem(mine + turn, tiles)
                    into = pl.ds(pl.multiple_of(tile * slices, slices), slices)
                    out[0, into, at : at + LANES] = value[turn * slices : (turn + 1) * slices]
            else:
                out[0, :, at : at + LANES] = pltpu.roll(value, mine * slices, 0)
        sums = []


def shifted(value, axis, by):
    size = lax.axis_size(axis)
    return lax.ppermute(value, axis, [(i, (i - by) % size) for i in range(size)])


def swapped(value, axis, by):
    return lax.ppermute(value, axis, [(i, i ^ by) for i in range(lax.axis_size(axis))])


def body(sinogram, paganin_width, window_block):
    local, slices, bins = sinogram.shape
    segments, spots, tiles = (lax.axis_size(name) for name in ("segment", "angle", "tile"))
    segment, spot = lax.axis_index("segment"), lax.axis_index("angle")
    groups = segments * spots
    angle_total = local * groups
    tile_rows = ROWS_DEV * groups
    reach = math.hypot((TCOLS - 1) / 2, (tile_rows - 1) / 2)
    first_bin = max(0, int(WIN / 2 - reach - 0.01)) // 16 * 16
    last_bin = min(WIN - 1, int(WIN / 2 + reach + 0.01) + 1)
    outs = -(-(last_bin + 1 - first_bin) // LANES)
    assert first_bin + (outs - 1) * LANES < WIN and first_bin < LANES
    assert spots & (spots - 1) == 0 and spots > 1
    smooth_blocks = -(-(outs + 3) // 2) * 2
    chunks, pixels = TCOLS // CHUNK, ROWS_DEV * CHUNK
    half = WIN / 2.0 - first_bin

    smem = pl.BlockSpec(memory_space=pltpu.SMEM)
    vmem = pl.BlockSpec(memory_space=pltpu.VMEM)
    hat_bytes = angle_total * SLOT * ROWS_DEV * TCOLS * 2
    params = pltpu.CompilerParams(vmem_limit_bytes=hat_bytes + 12 * 1024 * 1024)
    height = local * slices
    block_total = bins // LANES
    used = last_bin + 1 - first_bin - (outs - 1) * LANES
    row_groups = LANES // (1 << (used - 1).bit_length())
    if height % (8 * row_groups):
        row_groups = 1
    full = outs if row_groups == 1 else outs - 1
    rows_of_block = -(-height // 16) * 16
    tail = 0 if row_groups == 1 else height // row_groups
    packing = (full, rows_of_block, row_groups)
    bits = [1 << bit for bit in reversed(range(spots.bit_length() - 1))]
    exchanges = [(bits[0],)]
    for first in range(1, len(bits), 2):
        pair = bits[first : first + 2]
        exchanges.append((*pair, sum(pair)) if len(pair) == 2 else tuple(pair))
    reached = [0]
    for masks in exchanges:
        reached = [other ^ mask for mask in (0, *masks) for other in reached]
    order = np.repeat(np.array(reached), local), np.tile(np.arange(local), spots)
    where = np.arange(groups)[:, None]
    by = np.arange(segments)[:, None] + where[:, :, None] // spots
    angles = (where % spots ^ order[0]) * local + order[1]
    angles = by % segments * (spots * local) + angles[:, None]
    theta = math.pi * angles.reshape(groups, angle_total) / angle_total
    cosine, sine = np.cos(theta), np.sin(theta)
    left = np.arange(chunks) * CHUNK - (TCOLS - 1) / 2.0
    edges = np.minimum(cosine[..., None] * left, cosine[..., None] * (left + (CHUNK - 1)))
    top = where * ROWS_DEV - (tile_rows - 1) / 2.0
    rise = np.minimum(sine * top, sine * (top + (ROWS_DEV - 1)))
    lows = np.floor(edges + rise[..., None] + (half - 0.01)).astype(np.int32)
    blocks = np.minimum(lows // SLOT, PER * (outs - 1))
    codes = (blocks << LANE_BITS) + lows - blocks * SLOT

    def in_rows(values):
        values = values.reshape(groups, -1)
        rows = -(-values.shape[1] // (8 * LANES)) * 8
        values = np.pad(values, ((0, 0), (0, rows * LANES - values.shape[1])))
        return jnp.asarray(values.reshape(groups, rows, LANES))

    trig_table = in_rows(np.concatenate([cosine, sine], axis=1).astype(np.float32))
    code_table = in_rows(codes.astype(np.int32))

    *cut, trig, codes = pl.pallas_call(
        functools.partial(filter_kernel, (tiles, outs, first_bin, packing)),
        out_shape=[
            jax.ShapeDtypeStruct((full * rows_of_block + -(-tail // 16) * 16, LANES), jnp.bfloat16)
        ]
        * tiles
        + [pltpu.SMEM(v.shape[1:], v.dtype) for v in (trig_table, code_table)],
        in_specs=[smem] + [pl.BlockSpec(memory_space=pltpu.HBM)] * 4,
        out_specs=[vmem] * tiles + [smem] * 2,
        scratch_shapes=[
            pltpu.SMEM(window_block.T.shape, jnp.int32),
            pltpu.VMEM(
                (local, slices, (block_total - WIN // LANES + smooth_blocks + 2) * LANES),
                jnp.float32,
            ),
            pltpu.VMEM((height * tiles, (smooth_blocks + 2) * LANES), jnp.float32),
            pltpu.VMEM((height * tiles, smooth_blocks * LANES), jnp.float32),
            pltpu.SemaphoreType.DMA((local + 3,)),
        ],
        compiler_params=params,
        name="filter",
    )(
        paganin_width,
        *(
            pltpu.with_memory_space_constraint(value, pltpu.HBM)
            for value in (window_block.T, trig_table, code_table, sinogram)
        ),
    )

    depth = spots * local * SLOT
    def hats_of(part, after):
        ready = lax.optimization_barrier((trig, codes, *after))[:2]
        return pl.pallas_call(
            functools.partial(hat_kernel, (part, half, tile_rows, angle_total)),
            out_shape=jax.ShapeDtypeStruct((chunks, depth, pixels), jnp.bfloat16),
            in_specs=[smem, smem],
            out_specs=vmem,
            compiler_params=params,
            cost_estimate=pl.CostEstimate(
                flops=chunks * depth * pixels * 16, bytes_accessed=0, transcendentals=0
            ),
            name="hats",
        )(*ready)

    hats = []

    def beside(moved, after, count):
        made = []
        for _ in range(min(count, segments - len(hats))):
            made.append(hats_of(len(hats), after))
            hats.append(None)
        moved, made = lax.optimization_barrier((moved, made))
        hats[len(hats) - len(made) :] = made
        return moved

    def joint(turn, mask):
        def index(spot, tile):
            return (spot ^ mask) * tiles + (tile - turn) % tiles

        pairs = [(at, index(at // tiles, at % tiles)) for at in range(spots * tiles)]
        return lax.ppermute(cut[turn], ("angle", "tile"), pairs)

    near = [(turn, mask) for mask in (0, *exchanges[0]) for turn in range(tiles)][1:]
    moved = beside([joint(*pair) for pair in near], cut, 1)
    pieces = jnp.stack([cut[0], *moved])
    whole = full * rows_of_block
    if tail:
        main = pieces[:, :whole].reshape(2, tiles * whole, LANES)
        tails = pieces[:, whole : whole + tail].reshape(2, tiles * tail, LANES)
        pieces = jnp.concatenate([main, tails], axis=1)
    else:
        pieces = pieces.reshape(2, tiles * whole, LANES)
    for masks in exchanges[1:-1]:
        moved = beside([swapped(pieces, "angle", mask) for mask in masks], (pieces,), 1)
        pieces = jnp.concatenate([pieces, *moved])
    held_type = jnp.bfloat16 if slices % 16 == 0 else jnp.float32
    sources = pieces.shape[0]

    def project(parts, windows, sums, last=False):
        return pl.pallas_call(
            functools.partial(
                project_kernel,
                (parts, sources, len(windows), segments, local, last, tiles, height, packing),
            ),
            out_shape=jax.ShapeDtypeStruct(
                (1, slices * tiles, ROWS_DEV * TCOLS)
                if last
                else (chunks, slices * tiles, pixels),
                jnp.float32,
            ),
            in_specs=[smem] + [vmem] * (len(windows) + segments + len(sums)),
            out_specs=vmem,
            scratch_shapes=[
                pltpu.VMEM(
                    (
                        len(parts) * sources * local,
                        PER * (outs - 1) + 1,
                        slices * tiles,
                        LANES,
                    ),
                    held_type,
                ),
            ],
            compiler_params=params,
            cost_estimate=pl.CostEstimate(
                flops=32 * slices * tiles * chunks * depth * pixels,
                bytes_accessed=0,
                transcendentals=0,
            ),
            name="project",
        )(codes, *windows, *hats, *sums)

    others = range(1, segments)
    early = [pieces] + [shifted(pieces, "segment", by) for by in others]
    moved = [swapped(pieces, "angle", mask) for mask in exchanges[-1]]
    hats += [hats_of(part, (pieces,)) for part in range(len(hats), segments)]
    count = len(moved)
    if count > 1:
        early, moved[-1] = lax.optimization_barrier((early, moved[-1]))
    sums = project([(by, 0) for by in range(segments)], early, ())
    if count > 1:
        moved[:-1], sums = lax.optimization_barrier((moved[:-1], sums))
    else:
        moved, sums = lax.optimization_barrier((moved, sums))
    ahead = [shifted(moved[-1], "segment", by) for by in others]
    final = [(by, part) for by in others for part in range(1, count)]
    if final:
        rest = jnp.concatenate(moved[:-1])
        late = [shifted(rest, "segment", by) for by in others]
    own = [(0, part + 1) for part in range(count)]
    first = [(by, count) for by in others]
    if final:
        sums = project(own + first, [*moved, *ahead], (sums,))
        return project(final, late, (sums,), True)
    sums = project(own, moved, (sums,))
    return project(first, ahead, (sums,), True)


def solution(mesh):
    in_specs = (P(("segment", "angle"), "tile", None), P(), P())
    out_specs = P("tile", None, ("segment", "angle"))
    return jax.shard_map(body, mesh=mesh, in_specs=in_specs, out_specs=out_specs, check_vma=False)
```

```python
import functools
import math

import jax
import jax.numpy as jnp
import numpy as np
from jax import lax
from jax.experimental import pallas as pl
from jax.experimental.pallas import tpu as pltpu
from jax.sharding import PartitionSpec as P

WIN = 512
BAND = 128
ROWS_DEV = 8
TCOLS = 256
LANES = 128
LANE_BITS = 7
CHUNK = 32
DEPTH = 40
SLOT = 64
PER = LANES // SLOT


def split(value):
    high = value.astype(jnp.bfloat16)
    return high, (value - high.astype(jnp.float32)).astype(jnp.bfloat16)


def banded(value, taps, starts):
    tap_high, tap_low = taps
    dot = functools.partial(jnp.dot, preferred_element_type=jnp.float32)
    cut = [value[:, start : start + tap_high.shape[0]] for start in starts]
    high, low = split(jnp.concatenate(cut, axis=0))
    both = dot(jnp.concatenate([high, low], axis=0), tap_high)
    result = both[: high.shape[0]] + (both[high.shape[0] :] + dot(high, tap_low))
    rows = value.shape[0]
    return [result[index * rows : (index + 1) * rows] for index in range(len(starts))]


def offsets(depth, width, shift):
    return (
        lax.broadcasted_iota(jnp.int32, (depth, width), 0)
        - lax.broadcasted_iota(jnp.int32, (depth, width), 1)
        - shift
    )


def filter_kernel(plan, width, blocks_ref, trig_table, code_table, ramp_ref, rows_ref, *refs):
    tiles, outs, packing = plan
    full, rows_of_block, groups = packing
    outputs, (trig, codes, blocks, ramp, padded, raw, smooth, arrived) = (
        refs[:tiles],
        refs[tiles:],
    )
    local, slices, bins = rows_ref.shape
    block_total = bins // LANES
    raw_wide = raw.shape[1]
    smooth_blocks = smooth.shape[1] // LANES
    height = local * slices
    ahead = 2 * LANES

    place = lax.axis_index("segment") * lax.axis_size("angle") + lax.axis_index("angle")
    sources = [(rows_ref.at[i], padded.at[i, :, pl.ds(ahead, bins)]) for i in range(local)]
    sources = [
        *sources,
        (blocks_ref, blocks),
        (ramp_ref, ramp),
        (trig_table.at[place], trig),
        (code_table.at[place], codes),
    ]
    copies = [
        pltpu.make_async_copy(source, into, arrived.at[index])
        for index, (source, into) in enumerate(sources)
    ]
    for copy in copies:
        copy.start()
    behind = padded.shape[2] - ahead - bins
    padded[:, :, :ahead] = jnp.zeros((local, slices, ahead), jnp.float32)
    padded[:, :, ahead + bins :] = jnp.zeros((local, slices, behind), jnp.float32)

    rate = 1.0 / width[0]
    steps = (lax.broadcasted_iota(jnp.int32, (1, BAND), 1) + 1).astype(jnp.float32)
    total = 1.0 + 2.0 * jnp.sum(jnp.exp(-steps * rate), axis=1, keepdims=True)
    share = 1.0 / total
    near = []
    for shift in (LANES, 0, -LANES):
        spread = jnp.abs(offsets(LANES, LANES, shift))
        taps = jnp.exp(-spread.astype(jnp.float32) * rate) * share
        near.append(split(jnp.where(spread <= BAND, taps, 0.0)))
    none = jnp.zeros((LANES, LANES), jnp.bfloat16)
    paganin = [
        jnp.concatenate(
            [
                jnp.concatenate([*(taps[part] for taps in near), none], axis=0),
                jnp.concatenate([none, *(taps[part] for taps in near)], axis=0),
            ],
            axis=1,
        )
        for part in range(2)
    ]

    for copy in copies:
        copy.wait()
    first = place * local
    mine = lax.axis_index("tile")
    starts = []
    for turn in range(tiles):
        tile = lax.rem(mine - turn + tiles, tiles)
        for angle in range(local):
            start = blocks[tile, first + angle]
            starts.append(start)
            at = (turn * local + angle) * slices
            lanes = pl.ds(pl.multiple_of(start * LANES, LANES), raw_wide)
            raw[at : at + slices, :] = padded[angle, :, lanes]
    pairs = range(0, smooth_blocks * LANES, 256)
    for at, value in zip(pairs, banded(raw[...], paganin, pairs)):
        smooth[:, at : at + 256] = value
    for index, start in enumerate(starts):
        at = slice(index * slices, (index + 1) * slices)
        for j in range(smooth_blocks):
            if 1 <= j <= WIN // LANES:
                continue
            block = start - 1 + j
            inside = jnp.logical_and(block >= 0, block < block_total)
            lanes = slice(j * LANES, (j + 1) * LANES)
            smooth[at, lanes] = jnp.where(inside, smooth[at, lanes], 0.0)
    lanes = range(0, outs * LANES, LANES)
    for j, value in enumerate(banded(smooth[...], (ramp[0], ramp[1]), lanes)):
        for turn in range(tiles):
            part = value[turn * height : (turn + 1) * height]
            if j == full:
                part = pack(part, groups)
            if part.shape[0] % 16:
                rest = jnp.zeros((-part.shape[0] % 16, LANES), jnp.float32)
                part = jnp.concatenate([part, rest], axis=0)
            at = j * rows_of_block
            outputs[turn][at : at + part.shape[0], :] = part.astype(jnp.bfloat16)


def pack(value, groups):
    rows, wide = value.shape[0] // groups, LANES // groups
    lane = lax.broadcasted_iota(jnp.int32, (rows, LANES), 1)
    packed = value[:rows]
    for group in range(1, groups):
        more = pltpu.roll(value[group * rows : (group + 1) * rows], group * wide, 1)
        packed = jnp.where(lane < group * wide, packed, more)
    return packed


def unpack(value, groups):
    wide = LANES // groups
    rolled = [pltpu.roll(value, (LANES - group * wide) % LANES, 1) for group in range(groups)]
    return jnp.concatenate(rolled, axis=0)


def read(table, index):
    return table[index >> LANE_BITS, index & (LANES - 1)]


def hat_kernel(plan, trig, codes, hats):
    part, half, tile_rows, angle_total = plan
    chunks, depth, pixels = hats.shape
    count = depth // SLOT
    place = lax.axis_index("segment") * lax.axis_size("angle") + lax.axis_index("angle")
    first_row = (place * ROWS_DEV).astype(jnp.float32) - (tile_rows - 1) / 2.0
    lane = lax.broadcasted_iota(jnp.int32, (8, pixels), 1)
    depth_step = lax.broadcasted_iota(jnp.int32, (8, pixels), 0).astype(jnp.float32)
    y = (lane // CHUNK).astype(jnp.float32) + first_row
    x = (lane % CHUNK).astype(jnp.float32)
    rest = jnp.zeros((-DEPTH % 16, pixels), jnp.float32)
    gap = jnp.zeros((SLOT - DEPTH - DEPTH % 16, pixels), jnp.bfloat16)

    def step(index, carry):
        angle = part * count + index
        cosine, sine = read(trig, angle), read(trig, angle_total + angle)
        at = pl.multiple_of(index * SLOT, SLOT)
        start = y * sine + x * cosine - depth_step
        for chunk in range(chunks):
            left = chunk * CHUNK - (TCOLS - 1) / 2.0
            code = read(codes, angle * chunks + chunk)
            low = ((code >> LANE_BITS) * SLOT + (code & (LANES - 1))).astype(jnp.float32)
            across = start + (left * cosine + (half - low))
            rows = [jnp.maximum(0.0, 1.0 - jnp.abs(across - 8.0 * j)) for j in range(DEPTH // 8)]
            rows = jnp.concatenate([*rows, rest], axis=0).astype(jnp.bfloat16)
            hats[chunk, pl.ds(at, rows.shape[0]), :] = rows
            hats[chunk, pl.ds(at + rows.shape[0], gap.shape[0]), :] = gap
        return carry

    lax.fori_loop(0, count, step, 0, unroll=2)


def project_kernel(plan, codes, *refs):
    parts, sources, arrays, segments, local, last, tiles, height, packing = plan
    full, rows_of_block, groups = packing
    windows, refs = refs[:arrays], refs[arrays:]
    windows = [(window, source) for window in windows for source in range(window.shape[0])]
    hats, before, (out, held) = refs[:segments], refs[segments:-2], refs[-2:]
    chunks, depth, pixels = hats[0].shape
    tail_first = tiles * full * rows_of_block
    slices = height // local
    count = sources * local
    angle_count = depth // SLOT
    spread = lax.broadcasted_iota(jnp.int32, (height, LANES), 1)
    for at, (window, source) in enumerate(windows):
        if groups > 1:
            tails = window[source, tail_first:, :].astype(jnp.float32)
        for turn in range(tiles):
            pieces = []
            for j in range(full):
                rows = pl.ds((turn * full + j) * rows_of_block, rows_of_block)
                pieces.append(window[source, rows, :].astype(held.dtype)[:height])
            if groups > 1:
                tail = height // groups
                tail = tails[turn * tail : (turn + 1) * tail]
                pieces.append(unpack(tail, groups).astype(held.dtype))
            halves = [pltpu.roll(value, SLOT, 1) for value in pieces]
            for j in range(held.shape[1]):
                if j % 2 == 0:
                    value = pieces[j // 2]
                else:
                    value = jnp.where(spread < SLOT, halves[j // 2], halves[j // 2 + 1])
                for angle in range(local):
                    held[at * local + angle, j, turn * slices : (turn + 1) * slices, :] = value[
                        angle * slices : (angle + 1) * slices
                    ]
    lane = lax.broadcasted_iota(jnp.int32, (slices * tiles, LANES), 1)
    sums = []
    for chunk in range(chunks):
        value = before[0][chunk] if before else None
        for at, (by, part) in enumerate(parts):
            cut = []
            for first in range(0, count, PER):
                merged = None
                for spot in range(PER):
                    index = first + spot
                    code = read(codes, (by * angle_count + part * count + index) * chunks + chunk)
                    turn_by = (spot * SLOT + LANES - (code & (LANES - 1))) & (LANES - 1)
                    piece = pltpu.roll(held[at * count + index, code >> LANE_BITS], turn_by, 1)
                    merged = piece if spot == 0 else jnp.where(lane < spot * SLOT, merged, piece)
                cut.append(merged.astype(jnp.bfloat16))
            rows = pl.ds(part * count * SLOT, count * SLOT)
            more = jnp.dot(
                jnp.concatenate(cut, axis=1),
                hats[by][chunk, rows, :],
                preferred_element_type=jnp.float32,
            )
            value = more if value is None else value + more
        sums.append(value)
        if not last:
            out[chunk] = value
        if not last or (chunk + 1) * CHUNK % LANES:
            continue
        mine = lax.axis_index("tile")
        for row in range(ROWS_DEV):
            value = jnp.concatenate(
                [part[:, row * CHUNK : (row + 1) * CHUNK] for part in sums], axis=1
            )
            at = row * TCOLS + (chunk + 1) * CHUNK - LANES
            if slices % 8 == 0:
                for turn in range(tiles):
                    tile = lax.rem(mine + turn, tiles)
                    into = pl.ds(pl.multiple_of(tile * slices, slices), slices)
                    out[0, into, at : at + LANES] = value[turn * slices : (turn + 1) * slices]
            else:
                out[0, :, at : at + LANES] = pltpu.roll(value, mine * slices, 0)
        sums = []


def shifted(value, axis, by):
    size = lax.axis_size(axis)
    return lax.ppermute(value, axis, [(i, (i - by) % size) for i in range(size)])


def swapped(value, axis, by):
    return lax.ppermute(value, axis, [(i, i ^ by) for i in range(lax.axis_size(axis))])


def body(sinogram, paganin_width, window_block):
    local, slices, bins = sinogram.shape
    segments, spots, tiles = (lax.axis_size(name) for name in ("segment", "angle", "tile"))
    segment, spot = lax.axis_index("segment"), lax.axis_index("angle")
    groups = segments * spots
    angle_total = local * groups
    tile_rows = ROWS_DEV * groups
    reach = math.hypot((TCOLS - 1) / 2, (tile_rows - 1) / 2)
    first_bin = max(0, int(WIN / 2 - reach - 0.01)) // 16 * 16
    last_bin = min(WIN - 1, int(WIN / 2 + reach + 0.01) + 1)
    outs = -(-(last_bin + 1 - first_bin) // LANES)
    assert first_bin + (outs - 1) * LANES < WIN and first_bin < LANES
    assert spots & (spots - 1) == 0 and spots > 1
    smooth_blocks = -(-(outs + 3) // 2) * 2
    chunks, pixels = TCOLS // CHUNK, ROWS_DEV * CHUNK
    half = WIN / 2.0 - first_bin

    smem = pl.BlockSpec(memory_space=pltpu.SMEM)
    vmem = pl.BlockSpec(memory_space=pltpu.VMEM)
    hat_bytes = angle_total * SLOT * ROWS_DEV * TCOLS * 2
    params = pltpu.CompilerParams(vmem_limit_bytes=hat_bytes + 12 * 1024 * 1024)
    height = local * slices
    block_total = bins // LANES
    used = last_bin + 1 - first_bin - (outs - 1) * LANES
    row_groups = LANES // (1 << (used - 1).bit_length())
    if height % (8 * row_groups):
        row_groups = 1
    full = outs if row_groups == 1 else outs - 1
    rows_of_block = -(-height // 16) * 16
    tail = 0 if row_groups == 1 else height // row_groups
    packing = (full, rows_of_block, row_groups)
    bits = [1 << bit for bit in reversed(range(spots.bit_length() - 1))]
    exchanges = [(bits[0],)]
    for first in range(1, len(bits), 2):
        pair = bits[first : first + 2]
        exchanges.append((*pair, sum(pair)) if len(pair) == 2 else tuple(pair))
    reached = [0]
    for masks in exchanges:
        reached = [other ^ mask for mask in (0, *masks) for other in reached]
    order = np.repeat(np.array(reached), local), np.tile(np.arange(local), spots)
    where = np.arange(groups)[:, None]
    by = np.arange(segments)[:, None] + where[:, :, None] // spots
    angles = (where % spots ^ order[0]) * local + order[1]
    angles = by % segments * (spots * local) + angles[:, None]
    theta = math.pi * angles.reshape(groups, angle_total) / angle_total
    cosine, sine = np.cos(theta), np.sin(theta)
    left = np.arange(chunks) * CHUNK - (TCOLS - 1) / 2.0
    edges = np.minimum(cosine[..., None] * left, cosine[..., None] * (left + (CHUNK - 1)))
    top = where * ROWS_DEV - (tile_rows - 1) / 2.0
    rise = np.minimum(sine * top, sine * (top + (ROWS_DEV - 1)))
    lows = np.floor(edges + rise[..., None] + (half - 0.01)).astype(np.int32)
    blocks = np.minimum(lows // SLOT, PER * (outs - 1))
    codes = (blocks << LANE_BITS) + lows - blocks * SLOT

    def in_rows(values):
        values = values.reshape(groups, -1)
        rows = -(-values.shape[1] // (8 * LANES)) * 8
        values = np.pad(values, ((0, 0), (0, rows * LANES - values.shape[1])))
        return jnp.asarray(values.reshape(groups, rows, LANES))

    trig_table = in_rows(np.concatenate([cosine, sine], axis=1).astype(np.float32))
    code_table = in_rows(codes.astype(np.int32))

    away = np.arange(4 * LANES)[:, None] - np.arange(LANES) - BAND - first_bin
    odd = (np.abs(away) <= BAND) & (away % 2 == 1)
    ramp = np.where(odd, -1.0 / (math.pi**2 * np.maximum(away**2, 1)), 0.0)
    ramp = np.where(away == 0, 0.25, ramp)
    high = ramp.astype(jnp.bfloat16)
    low = (ramp - high.astype(np.float64)).astype(jnp.bfloat16)
    ramp_table = jnp.asarray(np.stack([high, low]))

    *cut, trig, codes = pl.pallas_call(
        functools.partial(filter_kernel, (tiles, outs, packing)),
        out_shape=[
            jax.ShapeDtypeStruct((full * rows_of_block + -(-tail // 16) * 16, LANES), jnp.bfloat16)
        ]
        * tiles
        + [pltpu.SMEM(v.shape[1:], v.dtype) for v in (trig_table, code_table)],
        in_specs=[smem] + [pl.BlockSpec(memory_space=pltpu.HBM)] * 5,
        out_specs=[vmem] * tiles + [smem] * 2,
        scratch_shapes=[
            pltpu.SMEM(window_block.T.shape, jnp.int32),
            pltpu.VMEM(ramp_table.shape, ramp_table.dtype),
            pltpu.VMEM(
                (local, slices, (block_total - WIN // LANES + smooth_blocks + 2) * LANES),
                jnp.float32,
            ),
            pltpu.VMEM((height * tiles, (smooth_blocks + 2) * LANES), jnp.float32),
            pltpu.VMEM((height * tiles, smooth_blocks * LANES), jnp.float32),
            pltpu.SemaphoreType.DMA((local + 4,)),
        ],
        compiler_params=params,
        name="filter",
    )(
        paganin_width,
        *(
            pltpu.with_memory_space_constraint(value, pltpu.HBM)
            for value in (window_block.T, trig_table, code_table, ramp_table, sinogram)
        ),
    )

    depth = spots * local * SLOT
    def hats_of(part, after):
        ready = lax.optimization_barrier((trig, codes, *after))[:2]
        return pl.pallas_call(
            functools.partial(hat_kernel, (part, half, tile_rows, angle_total)),
            out_shape=jax.ShapeDtypeStruct((chunks, depth, pixels), jnp.bfloat16),
            in_specs=[smem, smem],
            out_specs=vmem,
            compiler_params=params,
            cost_estimate=pl.CostEstimate(
                flops=chunks * depth * pixels * 16, bytes_accessed=0, transcendentals=0
            ),
            name="hats",
        )(*ready)

    hats = []

    def beside(moved, after, count):
        made = []
        for _ in range(min(count, segments - len(hats))):
            made.append(hats_of(len(hats), after))
            hats.append(None)
        moved, made = lax.optimization_barrier((moved, made))
        hats[len(hats) - len(made) :] = made
        return moved

    def joint(turn, mask):
        def index(spot, tile):
            return (spot ^ mask) * tiles + (tile - turn) % tiles

        pairs = [(at, index(at // tiles, at % tiles)) for at in range(spots * tiles)]
        return lax.ppermute(cut[turn], ("angle", "tile"), pairs)

    near = [(turn, mask) for mask in (0, *exchanges[0]) for turn in range(tiles)][1:]
    moved = beside([joint(*pair) for pair in near], cut, 1)
    pieces = jnp.stack([cut[0], *moved])
    whole = full * rows_of_block
    if tail:
        main = pieces[:, :whole].reshape(2, tiles * whole, LANES)
        tails = pieces[:, whole : whole + tail].reshape(2, tiles * tail, LANES)
        pieces = jnp.concatenate([main, tails], axis=1)
    else:
        pieces = pieces.reshape(2, tiles * whole, LANES)
    for masks in exchanges[1:-1]:
        moved = beside([swapped(pieces, "angle", mask) for mask in masks], (pieces,), 1)
        pieces = jnp.concatenate([pieces, *moved])
    held_type = jnp.bfloat16 if slices % 16 == 0 else jnp.float32
    sources = pieces.shape[0]

    def project(parts, windows, sums, last=False):
        return pl.pallas_call(
            functools.partial(
                project_kernel,
                (parts, sources, len(windows), segments, local, last, tiles, height, packing),
            ),
            out_shape=jax.ShapeDtypeStruct(
                (1, slices * tiles, ROWS_DEV * TCOLS)
                if last
                else (chunks, slices * tiles, pixels),
                jnp.float32,
            ),
            in_specs=[smem] + [vmem] * (len(windows) + segments + len(sums)),
            out_specs=vmem,
            scratch_shapes=[
                pltpu.VMEM(
                    (
                        len(parts) * sources * local,
                        PER * (outs - 1) + 1,
                        slices * tiles,
                        LANES,
                    ),
                    held_type,
                ),
            ],
            compiler_params=params,
            cost_estimate=pl.CostEstimate(
                flops=32 * slices * tiles * chunks * depth * pixels,
                bytes_accessed=0,
                transcendentals=0,
            ),
            name="project",
        )(codes, *windows, *hats, *sums)

    others = range(1, segments)
    early = [pieces] + [shifted(pieces, "segment", by) for by in others]
    moved = [swapped(pieces, "angle", mask) for mask in exchanges[-1]]
    hats += [hats_of(part, (pieces,)) for part in range(len(hats), segments)]
    count = len(moved)
    if count > 1:
        early, moved[-1] = lax.optimization_barrier((early, moved[-1]))
    sums = project([(by, 0) for by in range(segments)], early, ())
    if count > 1:
        moved[:-1], sums = lax.optimization_barrier((moved[:-1], sums))
    else:
        moved, sums = lax.optimization_barrier((moved, sums))
    ahead = [shifted(moved[-1], "segment", by) for by in others]
    final = [(by, part) for by in others for part in range(1, count)]
    if final:
        rest = jnp.concatenate(moved[:-1])
        late = [shifted(rest, "segment", by) for by in others]
    own = [(0, part + 1) for part in range(count)]
    first = [(by, count) for by in others]
    if final:
        sums = project(own + first, [*moved, *ahead], (sums,))
        return project(final, late, (sums,), True)
    sums = project(own, moved, (sums,))
    return project(first, ahead, (sums,), True)


def solution(mesh):
    in_specs = (P(("segment", "angle"), "tile", None), P(), P())
    out_specs = P("tile", None, ("segment", "angle"))
    return jax.shard_map(body, mesh=mesh, in_specs=in_specs, out_specs=out_specs, check_vma=False)
```

```python
import functools
import math

import jax
import jax.numpy as jnp
import numpy as np
from jax import lax
from jax.experimental import pallas as pl
from jax.experimental.pallas import tpu as pltpu
from jax.sharding import PartitionSpec as P

WIN = 512
BAND = 128
ROWS_DEV = 8
TCOLS = 256
LANES = 128
LANE_BITS = 7
CHUNK = 32
DEPTH = 40
SLOT = 64
PER = LANES // SLOT


def split(value):
    high = value.astype(jnp.bfloat16)
    return high, (value - high.astype(jnp.float32)).astype(jnp.bfloat16)


def banded(value, taps, starts):
    tap_high, tap_low = taps
    dot = functools.partial(jnp.dot, preferred_element_type=jnp.float32)
    cut = [value[:, start : start + tap_high.shape[0]] for start in starts]
    high, low = split(jnp.concatenate(cut, axis=0))
    both = dot(jnp.concatenate([high, low], axis=0), tap_high)
    result = both[: high.shape[0]] + (both[high.shape[0] :] + dot(high, tap_low))
    rows = value.shape[0]
    return [result[index * rows : (index + 1) * rows] for index in range(len(starts))]


def offsets(depth, width, shift):
    return (
        lax.broadcasted_iota(jnp.int32, (depth, width), 0)
        - lax.broadcasted_iota(jnp.int32, (depth, width), 1)
        - shift
    )


def filter_kernel(plan, width, blocks_ref, trig_table, code_table, rows_ref, *refs):
    tiles, outs, first_bin, packing = plan
    full, rows_of_block, groups = packing
    outputs, (trig, codes, blocks, padded, raw, smooth, arrived) = (
        refs[:tiles],
        refs[tiles:],
    )
    local, slices, bins = rows_ref.shape
    block_total = bins // LANES
    raw_wide = raw.shape[1]
    smooth_blocks = smooth.shape[1] // LANES
    height = local * slices
    ahead = 2 * LANES

    place = lax.axis_index("segment") * lax.axis_size("angle") + lax.axis_index("angle")
    sources = [(rows_ref.at[i], padded.at[i, :, pl.ds(ahead, bins)]) for i in range(local)]
    sources = [
        *sources,
        (blocks_ref, blocks),
        (trig_table.at[place], trig),
        (code_table.at[place], codes),
    ]
    copies = [
        pltpu.make_async_copy(source, into, arrived.at[index])
        for index, (source, into) in enumerate(sources)
    ]
    for copy in copies:
        copy.start()
    behind = padded.shape[2] - ahead - bins
    padded[:, :, :ahead] = jnp.zeros((local, slices, ahead), jnp.float32)
    padded[:, :, ahead + bins :] = jnp.zeros((local, slices, behind), jnp.float32)

    away = offsets(512, LANES, BAND + first_bin)
    spread = jnp.abs(away)
    squared = jnp.maximum(spread * spread, 1).astype(jnp.float32)
    odd = jnp.logical_and(spread <= BAND, (spread & 1) == 1)
    ramp = jnp.where(odd, -1.0 / (math.pi * math.pi * squared), 0.0)
    ramp = split(jnp.where(away == 0, 0.25, ramp))
    decay = width[0]
    steps = (lax.broadcasted_iota(jnp.int32, (1, BAND), 1) + 1).astype(jnp.float32)
    total = 1.0 + 2.0 * jnp.sum(jnp.exp(-steps / decay), axis=1, keepdims=True)
    away = offsets(2 * 256, 256, BAND)
    spread = jnp.abs(away)
    paganin = jnp.where(
        spread <= BAND, jnp.exp(-spread.astype(jnp.float32) / decay) / total, 0.0
    )
    paganin = split(paganin)

    for copy in copies:
        copy.wait()
    first = place * local
    mine = lax.axis_index("tile")
    starts = []
    for turn in range(tiles):
        tile = lax.rem(mine - turn + tiles, tiles)
        for angle in range(local):
            start = blocks[tile, first + angle]
            starts.append(start)
            at = (turn * local + angle) * slices
            lanes = pl.ds(pl.multiple_of(start * LANES, LANES), raw_wide)
            raw[at : at + slices, :] = padded[angle, :, lanes]
    pairs = range(0, smooth_blocks * LANES, 256)
    for at, value in zip(pairs, banded(raw[...], paganin, pairs)):
        smooth[:, at : at + 256] = value
    for index, start in enumerate(starts):
        at = slice(index * slices, (index + 1) * slices)
        for j in range(smooth_blocks):
            if 1 <= j <= WIN // LANES:
                continue
            block = start - 1 + j
            inside = jnp.logical_and(block >= 0, block < block_total)
            lanes = slice(j * LANES, (j + 1) * LANES)
            smooth[at, lanes] = jnp.where(inside, smooth[at, lanes], 0.0)
    lanes = range(0, outs * LANES, LANES)
    for j, value in enumerate(banded(smooth[...], ramp, lanes)):
        for turn in range(tiles):
            part = value[turn * height : (turn + 1) * height]
            if j == full:
                part = pack(part, groups)
            if part.shape[0] % 16:
                rest = jnp.zeros((-part.shape[0] % 16, LANES), jnp.float32)
                part = jnp.concatenate([part, rest], axis=0)
            at = j * rows_of_block
            outputs[turn][at : at + part.shape[0], :] = part.astype(jnp.bfloat16)


def pack(value, groups):
    rows, wide = value.shape[0] // groups, LANES // groups
    lane = lax.broadcasted_iota(jnp.int32, (rows, LANES), 1)
    packed = value[:rows]
    for group in range(1, groups):
        more = pltpu.roll(value[group * rows : (group + 1) * rows], group * wide, 1)
        packed = jnp.where(lane < group * wide, packed, more)
    return packed


def unpack(value, groups):
    wide = LANES // groups
    rolled = [pltpu.roll(value, (LANES - group * wide) % LANES, 1) for group in range(groups)]
    return jnp.concatenate(rolled, axis=0)


def read(table, index):
    return table[index >> LANE_BITS, index & (LANES - 1)]


def hat_kernel(plan, trig, codes, hats):
    part, half, tile_rows, angle_total = plan
    chunks, depth, pixels = hats.shape
    count = depth // SLOT
    place = lax.axis_index("segment") * lax.axis_size("angle") + lax.axis_index("angle")
    first_row = (place * ROWS_DEV).astype(jnp.float32) - (tile_rows - 1) / 2.0
    lane = lax.broadcasted_iota(jnp.int32, (8, pixels), 1)
    depth_step = lax.broadcasted_iota(jnp.int32, (8, pixels), 0).astype(jnp.float32)
    y = (lane // CHUNK).astype(jnp.float32) + first_row
    x = (lane % CHUNK).astype(jnp.float32)
    rest = jnp.zeros((-DEPTH % 16, pixels), jnp.float32)
    gap = jnp.zeros((SLOT - DEPTH - DEPTH % 16, pixels), jnp.bfloat16)

    def step(index, carry):
        angle = part * count + index
        cosine, sine = read(trig, angle), read(trig, angle_total + angle)
        at = pl.multiple_of(index * SLOT, SLOT)
        start = y * sine + x * cosine - depth_step
        for chunk in range(chunks):
            left = chunk * CHUNK - (TCOLS - 1) / 2.0
            code = read(codes, angle * chunks + chunk)
            low = ((code >> LANE_BITS) * SLOT + (code & (LANES - 1))).astype(jnp.float32)
            across = start + (left * cosine + (half - low))
            rows = [jnp.maximum(0.0, 1.0 - jnp.abs(across - 8.0 * j)) for j in range(DEPTH // 8)]
            rows = jnp.concatenate([*rows, rest], axis=0).astype(jnp.bfloat16)
            hats[chunk, pl.ds(at, rows.shape[0]), :] = rows
            hats[chunk, pl.ds(at + rows.shape[0], gap.shape[0]), :] = gap
        return carry

    lax.fori_loop(0, count, step, 0, unroll=2)


def project_kernel(plan, codes, *refs):
    parts, sources, arrays, segments, local, last, tiles, height, packing = plan
    full, rows_of_block, groups = packing
    windows, refs = refs[:arrays], refs[arrays:]
    windows = [(window, source) for window in windows for source in range(window.shape[0])]
    scratch = 3 if last else 1
    hats, before = refs[:segments], refs[segments : -1 - scratch]
    out, held = refs[-1 - scratch], refs[-scratch]
    if last:
        ready, sent = refs[-2:]
        copies = []
    chunks, depth, pixels = hats[0].shape
    tail_first = tiles * full * rows_of_block
    slices = height // local
    count = sources * local
    angle_count = depth // SLOT
    spread = lax.broadcasted_iota(jnp.int32, (height, LANES), 1)
    for at, (window, source) in enumerate(windows):
        if groups > 1:
            tails = window[source, tail_first:, :].astype(jnp.float32)
        for turn in range(tiles):
            pieces = []
            for j in range(full):
                rows = pl.ds((turn * full + j) * rows_of_block, rows_of_block)
                pieces.append(window[source, rows, :].astype(held.dtype)[:height])
            if groups > 1:
                tail = height // groups
                tail = tails[turn * tail : (turn + 1) * tail]
                pieces.append(unpack(tail, groups).astype(held.dtype))
            halves = [pltpu.roll(value, SLOT, 1) for value in pieces]
            for j in range(held.shape[1]):
                if j % 2 == 0:
                    value = pieces[j // 2]
                else:
                    value = jnp.where(spread < SLOT, halves[j // 2], halves[j // 2 + 1])
                for angle in range(local):
                    held[at * local + angle, j, turn * slices : (turn + 1) * slices, :] = value[
                        angle * slices : (angle + 1) * slices
                    ]
    lane = lax.broadcasted_iota(jnp.int32, (slices * tiles, LANES), 1)
    sums = []
    for chunk in range(chunks):
        value = before[0][chunk] if before else None
        for at, (by, part) in enumerate(parts):
            cut = []
            for first in range(0, count, PER):
                merged = None
                for spot in range(PER):
                    index = first + spot
                    code = read(codes, (by * angle_count + part * count + index) * chunks + chunk)
                    turn_by = (spot * SLOT + LANES - (code & (LANES - 1))) & (LANES - 1)
                    piece = pltpu.roll(held[at * count + index, code >> LANE_BITS], turn_by, 1)
                    merged = piece if spot == 0 else jnp.where(lane < spot * SLOT, merged, piece)
                cut.append(merged.astype(jnp.bfloat16))
            rows = pl.ds(part * count * SLOT, count * SLOT)
            more = jnp.dot(
                jnp.concatenate(cut, axis=1),
                hats[by][chunk, rows, :],
                preferred_element_type=jnp.float32,
            )
            value = more if value is None else value + more
        sums.append(value)
        if not last:
            out[chunk] = value
        if not last or (chunk + 1) * CHUNK % LANES:
            continue
        mine = lax.axis_index("tile")
        for row in range(ROWS_DEV):
            value = jnp.concatenate(
                [part[:, row * CHUNK : (row + 1) * CHUNK] for part in sums], axis=1
            )
            at = row * TCOLS + (chunk + 1) * CHUNK - LANES
            if slices % 8 == 0:
                for turn in range(tiles):
                    tile = lax.rem(mine + turn, tiles)
                    into = pl.ds(pl.multiple_of(tile * slices, slices), slices)
                    ready[into, at : at + LANES] = value[turn * slices : (turn + 1) * slices]
            else:
                ready[:, at : at + LANES] = pltpu.roll(value, mine * slices, 0)
            lanes = pl.ds(at, LANES)
            copies.append(
                pltpu.make_async_copy(
                    ready.at[:, lanes], out.at[0, :, lanes], sent.at[len(copies)]
                )
            )
            copies[-1].start()
        sums = []
    if last:
        for copy in copies:
            copy.wait()


def shifted(value, axis, by):
    size = lax.axis_size(axis)
    return lax.ppermute(value, axis, [(i, (i - by) % size) for i in range(size)])


def swapped(value, axis, by):
    return lax.ppermute(value, axis, [(i, i ^ by) for i in range(lax.axis_size(axis))])


def body(sinogram, paganin_width, window_block):
    local, slices, bins = sinogram.shape
    segments, spots, tiles = (lax.axis_size(name) for name in ("segment", "angle", "tile"))
    segment, spot = lax.axis_index("segment"), lax.axis_index("angle")
    groups = segments * spots
    angle_total = local * groups
    tile_rows = ROWS_DEV * groups
    reach = math.hypot((TCOLS - 1) / 2, (tile_rows - 1) / 2)
    first_bin = max(0, int(WIN / 2 - reach - 0.01)) // 16 * 16
    last_bin = min(WIN - 1, int(WIN / 2 + reach + 0.01) + 1)
    outs = -(-(last_bin + 1 - first_bin) // LANES)
    assert first_bin + (outs - 1) * LANES < WIN and first_bin < LANES
    assert spots & (spots - 1) == 0 and spots > 1
    smooth_blocks = -(-(outs + 3) // 2) * 2
    chunks, pixels = TCOLS // CHUNK, ROWS_DEV * CHUNK
    half = WIN / 2.0 - first_bin

    smem = pl.BlockSpec(memory_space=pltpu.SMEM)
    vmem = pl.BlockSpec(memory_space=pltpu.VMEM)
    hat_bytes = angle_total * SLOT * ROWS_DEV * TCOLS * 2
    params = pltpu.CompilerParams(vmem_limit_bytes=hat_bytes + 12 * 1024 * 1024)
    height = local * slices
    block_total = bins // LANES
    used = last_bin + 1 - first_bin - (outs - 1) * LANES
    row_groups = LANES // (1 << (used - 1).bit_length())
    if height % (8 * row_groups):
        row_groups = 1
    full = outs if row_groups == 1 else outs - 1
    rows_of_block = -(-height // 16) * 16
    tail = 0 if row_groups == 1 else height // row_groups
    packing = (full, rows_of_block, row_groups)
    bits = [1 << bit for bit in reversed(range(spots.bit_length() - 1))]
    exchanges = [(bits[0],)]
    for first in range(1, len(bits), 2):
        pair = bits[first : first + 2]
        exchanges.append((*pair, sum(pair)) if len(pair) == 2 else tuple(pair))
    reached = [0]
    for masks in exchanges:
        reached = [other ^ mask for mask in (0, *masks) for other in reached]
    order = np.repeat(np.array(reached), local), np.tile(np.arange(local), spots)
    where = np.arange(groups)[:, None]
    by = np.arange(segments)[:, None] + where[:, :, None] // spots
    angles = (where % spots ^ order[0]) * local + order[1]
    angles = by % segments * (spots * local) + angles[:, None]
    theta = math.pi * angles.reshape(groups, angle_total) / angle_total
    cosine, sine = np.cos(theta), np.sin(theta)
    left = np.arange(chunks) * CHUNK - (TCOLS - 1) / 2.0
    edges = np.minimum(cosine[..., None] * left, cosine[..., None] * (left + (CHUNK - 1)))
    top = where * ROWS_DEV - (tile_rows - 1) / 2.0
    rise = np.minimum(sine * top, sine * (top + (ROWS_DEV - 1)))
    lows = np.floor(edges + rise[..., None] + (half - 0.01)).astype(np.int32)
    blocks = np.minimum(lows // SLOT, PER * (outs - 1))
    codes = (blocks << LANE_BITS) + lows - blocks * SLOT

    def in_rows(values):
        values = values.reshape(groups, -1)
        rows = -(-values.shape[1] // (8 * LANES)) * 8
        values = np.pad(values, ((0, 0), (0, rows * LANES - values.shape[1])))
        return jnp.asarray(values.reshape(groups, rows, LANES))

    trig_table = in_rows(np.concatenate([cosine, sine], axis=1).astype(np.float32))
    code_table = in_rows(codes.astype(np.int32))

    *cut, trig, codes = pl.pallas_call(
        functools.partial(filter_kernel, (tiles, outs, first_bin, packing)),
        out_shape=[
            jax.ShapeDtypeStruct((full * rows_of_block + -(-tail // 16) * 16, LANES), jnp.bfloat16)
        ]
        * tiles
        + [pltpu.SMEM(v.shape[1:], v.dtype) for v in (trig_table, code_table)],
        in_specs=[smem] + [pl.BlockSpec(memory_space=pltpu.HBM)] * 4,
        out_specs=[vmem] * tiles + [smem] * 2,
        scratch_shapes=[
            pltpu.SMEM(window_block.T.shape, jnp.int32),
            pltpu.VMEM(
                (local, slices, (block_total - WIN // LANES + smooth_blocks + 2) * LANES),
                jnp.float32,
            ),
            pltpu.VMEM((height * tiles, (smooth_blocks + 2) * LANES), jnp.float32),
            pltpu.VMEM((height * tiles, smooth_blocks * LANES), jnp.float32),
            pltpu.SemaphoreType.DMA((local + 3,)),
        ],
        compiler_params=params,
        name="filter",
    )(
        paganin_width,
        *(
            pltpu.with_memory_space_constraint(value, pltpu.HBM)
            for value in (window_block.T, trig_table, code_table, sinogram)
        ),
    )

    depth = spots * local * SLOT
    def hats_of(part, after):
        ready = lax.optimization_barrier((trig, codes, *after))[:2]
        return pl.pallas_call(
            functools.partial(hat_kernel, (part, half, tile_rows, angle_total)),
            out_shape=jax.ShapeDtypeStruct((chunks, depth, pixels), jnp.bfloat16),
            in_specs=[smem, smem],
            out_specs=vmem,
            compiler_params=params,
            cost_estimate=pl.CostEstimate(
                flops=chunks * depth * pixels * 16, bytes_accessed=0, transcendentals=0
            ),
            name="hats",
        )(*ready)

    hats = []

    def beside(moved, after, count):
        made = []
        for _ in range(min(count, segments - len(hats))):
            made.append(hats_of(len(hats), after))
            hats.append(None)
        moved, made = lax.optimization_barrier((moved, made))
        hats[len(hats) - len(made) :] = made
        return moved

    def joint(turn, mask):
        def index(spot, tile):
            return (spot ^ mask) * tiles + (tile - turn) % tiles

        pairs = [(at, index(at // tiles, at % tiles)) for at in range(spots * tiles)]
        return lax.ppermute(cut[turn], ("angle", "tile"), pairs)

    near = [(turn, mask) for mask in (0, *exchanges[0]) for turn in range(tiles)][1:]
    moved = beside([joint(*pair) for pair in near], cut, 1)
    pieces = jnp.stack([cut[0], *moved])
    whole = full * rows_of_block
    if tail:
        main = pieces[:, :whole].reshape(2, tiles * whole, LANES)
        tails = pieces[:, whole : whole + tail].reshape(2, tiles * tail, LANES)
        pieces = jnp.concatenate([main, tails], axis=1)
    else:
        pieces = pieces.reshape(2, tiles * whole, LANES)
    for masks in exchanges[1:-1]:
        moved = beside([swapped(pieces, "angle", mask) for mask in masks], (pieces,), 1)
        pieces = jnp.concatenate([pieces, *moved])
    held_type = jnp.bfloat16 if slices % 16 == 0 else jnp.float32
    sources = pieces.shape[0]

    sending = [
        pltpu.VMEM((slices * tiles, ROWS_DEV * TCOLS), jnp.float32),
        pltpu.SemaphoreType.DMA((ROWS_DEV * TCOLS // LANES,)),
    ]

    def project(parts, windows, sums, last=False):
        return pl.pallas_call(
            functools.partial(
                project_kernel,
                (parts, sources, len(windows), segments, local, last, tiles, height, packing),
            ),
            out_shape=jax.ShapeDtypeStruct(
                (1, slices * tiles, ROWS_DEV * TCOLS)
                if last
                else (chunks, slices * tiles, pixels),
                jnp.float32,
            ),
            in_specs=[smem] + [vmem] * (len(windows) + segments + len(sums)),
            out_specs=pl.BlockSpec(memory_space=pltpu.HBM) if last else vmem,
            scratch_shapes=[
                pltpu.VMEM(
                    (
                        len(parts) * sources * local,
                        PER * (outs - 1) + 1,
                        slices * tiles,
                        LANES,
                    ),
                    held_type,
                ),
                *(sending if last else []),
            ],
            compiler_params=params,
            cost_estimate=pl.CostEstimate(
                flops=32 * slices * tiles * chunks * depth * pixels,
                bytes_accessed=0,
                transcendentals=0,
            ),
            name="project",
        )(codes, *windows, *hats, *sums)

    others = range(1, segments)
    early = [pieces] + [shifted(pieces, "segment", by) for by in others]
    moved = [swapped(pieces, "angle", mask) for mask in exchanges[-1]]
    hats += [hats_of(part, (pieces,)) for part in range(len(hats), segments)]
    count = len(moved)
    if count > 1:
        early, moved[-1] = lax.optimization_barrier((early, moved[-1]))
    sums = project([(by, 0) for by in range(segments)], early, ())
    if count > 1:
        moved[:-1], sums = lax.optimization_barrier((moved[:-1], sums))
    else:
        moved, sums = lax.optimization_barrier((moved, sums))
    ahead = [shifted(moved[-1], "segment", by) for by in others]
    final = [(by, part) for by in others for part in range(1, count)]
    if final:
        rest = jnp.concatenate(moved[:-1])
        late = [shifted(rest, "segment", by) for by in others]
    own = [(0, part + 1) for part in range(count)]
    first = [(by, count) for by in others]
    if final:
        sums = project(own + first, [*moved, *ahead], (sums,))
        return project(final, late, (sums,), True)
    sums = project(own, moved, (sums,))
    return project(first, ahead, (sums,), True)


def solution(mesh):
    in_specs = (P(("segment", "angle"), "tile", None), P(), P())
    out_specs = P("tile", None, ("segment", "angle"))
    return jax.shard_map(body, mesh=mesh, in_specs=in_specs, out_specs=out_specs, check_vma=False)
```

```python
import functools
import math

import jax
import jax.numpy as jnp
import numpy as np
from jax import lax
from jax.experimental import pallas as pl
from jax.experimental.pallas import tpu as pltpu
from jax.sharding import PartitionSpec as P

WIN = 512
BAND = 128
ROWS_DEV = 8
TCOLS = 256
LANES = 128
LANE_BITS = 7
CHUNK = 32
DEPTH = 40
SLOT = 64
PER = LANES // SLOT


def split(value):
    high = value.astype(jnp.bfloat16)
    return high, (value - high.astype(jnp.float32)).astype(jnp.bfloat16)


def banded(blocks, taps, starts):
    tap_high, tap_low = taps
    count = tap_high.shape[0] // LANES
    dot = functools.partial(jnp.dot, preferred_element_type=jnp.float32)
    parts = [split(block) for block in blocks]
    high, low = (
        jnp.concatenate(
            [
                jnp.concatenate([part[which] for part in parts[at : at + count]], axis=1)
                for at in starts
            ],
            axis=0,
        )
        for which in range(2)
    )
    both = dot(jnp.concatenate([high, low], axis=0), tap_high)
    result = both[: high.shape[0]] + (both[high.shape[0] :] + dot(high, tap_low))
    rows = blocks[0].shape[0]
    return [result[index * rows : (index + 1) * rows] for index in range(len(starts))]


def offsets(depth, width, shift):
    return (
        lax.broadcasted_iota(jnp.int32, (depth, width), 0)
        - lax.broadcasted_iota(jnp.int32, (depth, width), 1)
        - shift
    )


def filter_kernel(plan, width, blocks_ref, trig_table, code_table, rows_ref, *refs):
    tiles, outs, first_bin, smooth_blocks, packing = plan
    full, rows_of_block, groups = packing
    outputs, (trig, codes, blocks, padded, arrived) = (
        refs[:tiles],
        refs[tiles:],
    )
    local, slices, bins = rows_ref.shape
    block_total = bins // LANES
    raw_wide = (smooth_blocks + 2) * LANES
    height = local * slices
    ahead = 2 * LANES

    place = lax.axis_index("segment") * lax.axis_size("angle") + lax.axis_index("angle")
    sources = [(rows_ref.at[i], padded.at[i, :, pl.ds(ahead, bins)]) for i in range(local)]
    sources = [
        *sources,
        (blocks_ref, blocks),
        (trig_table.at[place], trig),
        (code_table.at[place], codes),
    ]
    copies = [
        pltpu.make_async_copy(source, into, arrived.at[index])
        for index, (source, into) in enumerate(sources)
    ]
    for copy in copies:
        copy.start()
    behind = padded.shape[2] - ahead - bins
    padded[:, :, :ahead] = jnp.zeros((local, slices, ahead), jnp.float32)
    padded[:, :, ahead + bins :] = jnp.zeros((local, slices, behind), jnp.float32)

    away = offsets(512, LANES, BAND + first_bin)
    spread = jnp.abs(away)
    squared = jnp.maximum(spread * spread, 1).astype(jnp.float32)
    odd = jnp.logical_and(spread <= BAND, (spread & 1) == 1)
    ramp = jnp.where(odd, -1.0 / (math.pi * math.pi * squared), 0.0)
    ramp = split(jnp.where(away == 0, 0.25, ramp))
    decay = width[0]
    steps = (lax.broadcasted_iota(jnp.int32, (1, BAND), 1) + 1).astype(jnp.float32)
    total = 1.0 + 2.0 * jnp.sum(jnp.exp(-steps / decay), axis=1, keepdims=True)
    away = offsets(2 * 256, 256, BAND)
    spread = jnp.abs(away)
    paganin = jnp.where(
        spread <= BAND, jnp.exp(-spread.astype(jnp.float32) / decay) / total, 0.0
    )
    paganin = split(paganin)

    for copy in copies:
        copy.wait()
    first = place * local
    mine = lax.axis_index("tile")
    starts, raw = [], []
    for turn in range(tiles):
        tile = lax.rem(mine - turn + tiles, tiles)
        for angle in range(local):
            start = blocks[tile, first + angle]
            starts.append(start)
            lanes = pl.ds(pl.multiple_of(start * LANES, LANES), raw_wide)
            raw.append(padded[angle, :, lanes])
    raw = jnp.concatenate(raw, axis=0)
    raw = [raw[:, at : at + LANES] for at in range(0, raw_wide, LANES)]
    smooth = []
    for pair in banded(raw, paganin, range(0, smooth_blocks, 2)):
        smooth += [pair[:, :LANES], pair[:, LANES:]]
    for j in range(smooth_blocks):
        if 1 <= j <= WIN // LANES:
            continue
        kept = []
        for index, start in enumerate(starts):
            block = start - 1 + j
            inside = jnp.logical_and(block >= 0, block < block_total)
            value = smooth[j][index * slices : (index + 1) * slices]
            kept.append(jnp.where(inside, value, 0.0))
        smooth[j] = jnp.concatenate(kept, axis=0)
    for j, value in enumerate(banded(smooth, ramp, range(outs))):
        for turn in range(tiles):
            part = value[turn * height : (turn + 1) * height]
            if j == full:
                part = pack(part, groups)
            if part.shape[0] % 16:
                rest = jnp.zeros((-part.shape[0] % 16, LANES), jnp.float32)
                part = jnp.concatenate([part, rest], axis=0)
            at = j * rows_of_block
            outputs[turn][at : at + part.shape[0], :] = part.astype(jnp.bfloat16)


def pack(value, groups):
    rows, wide = value.shape[0] // groups, LANES // groups
    lane = lax.broadcasted_iota(jnp.int32, (rows, LANES), 1)
    packed = value[:rows]
    for group in range(1, groups):
        more = pltpu.roll(value[group * rows : (group + 1) * rows], group * wide, 1)
        packed = jnp.where(lane < group * wide, packed, more)
    return packed


def unpack(value, groups):
    wide = LANES // groups
    rolled = [pltpu.roll(value, (LANES - group * wide) % LANES, 1) for group in range(groups)]
    return jnp.concatenate(rolled, axis=0)


def read(table, index):
    return table[index >> LANE_BITS, index & (LANES - 1)]


def hat_kernel(plan, trig, codes, hats):
    part, half, tile_rows, angle_total = plan
    chunks, depth, pixels = hats.shape
    count = depth // SLOT
    place = lax.axis_index("segment") * lax.axis_size("angle") + lax.axis_index("angle")
    first_row = (place * ROWS_DEV).astype(jnp.float32) - (tile_rows - 1) / 2.0
    lane = lax.broadcasted_iota(jnp.int32, (8, pixels), 1)
    depth_step = lax.broadcasted_iota(jnp.int32, (8, pixels), 0).astype(jnp.float32)
    y = (lane // CHUNK).astype(jnp.float32) + first_row
    x = (lane % CHUNK).astype(jnp.float32)
    rest = jnp.zeros((-DEPTH % 16, pixels), jnp.float32)
    gap = jnp.zeros((SLOT - DEPTH - DEPTH % 16, pixels), jnp.bfloat16)

    def step(index, carry):
        angle = part * count + index
        cosine, sine = read(trig, angle), read(trig, angle_total + angle)
        at = pl.multiple_of(index * SLOT, SLOT)
        start = y * sine + x * cosine - depth_step
        for chunk in range(chunks):
            left = chunk * CHUNK - (TCOLS - 1) / 2.0
            code = read(codes, angle * chunks + chunk)
            low = ((code >> LANE_BITS) * SLOT + (code & (LANES - 1))).astype(jnp.float32)
            across = start + (left * cosine + (half - low))
            rows = [jnp.maximum(0.0, 1.0 - jnp.abs(across - 8.0 * j)) for j in range(DEPTH // 8)]
            rows = jnp.concatenate([*rows, rest], axis=0).astype(jnp.bfloat16)
            hats[chunk, pl.ds(at, rows.shape[0]), :] = rows
            hats[chunk, pl.ds(at + rows.shape[0], gap.shape[0]), :] = gap
        return carry

    lax.fori_loop(0, count, step, 0, unroll=2)


def project_kernel(plan, codes, *refs):
    parts, sources, arrays, segments, local, last, tiles, height, packing = plan
    full, rows_of_block, groups = packing
    windows, refs = refs[:arrays], refs[arrays:]
    windows = [(window, source) for window in windows for source in range(window.shape[0])]
    scratch = 3 if last else 1
    hats, before = refs[:segments], refs[segments : -1 - scratch]
    out, held = refs[-1 - scratch], refs[-scratch]
    if last:
        ready, sent = refs[-2:]
        copies = []
    chunks, depth, pixels = hats[0].shape
    tail_first = tiles * full * rows_of_block
    slices = height // local
    count = sources * local
    angle_count = depth // SLOT
    spread = lax.broadcasted_iota(jnp.int32, (height, LANES), 1)
    for at, (window, source) in enumerate(windows):
        if groups > 1:
            tails = window[source, tail_first:, :].astype(jnp.float32)
        for turn in range(tiles):
            pieces = []
            for j in range(full):
                rows = pl.ds((turn * full + j) * rows_of_block, rows_of_block)
                pieces.append(window[source, rows, :].astype(held.dtype)[:height])
            if groups > 1:
                tail = height // groups
                tail = tails[turn * tail : (turn + 1) * tail]
                pieces.append(unpack(tail, groups).astype(held.dtype))
            halves = [pltpu.roll(value, SLOT, 1) for value in pieces]
            for j in range(held.shape[1]):
                if j % 2 == 0:
                    value = pieces[j // 2]
                else:
                    value = jnp.where(spread < SLOT, halves[j // 2], halves[j // 2 + 1])
                for angle in range(local):
                    held[at * local + angle, j, turn * slices : (turn + 1) * slices, :] = value[
                        angle * slices : (angle + 1) * slices
                    ]
    lane = lax.broadcasted_iota(jnp.int32, (slices * tiles, LANES), 1)
    sums = []
    for chunk in range(chunks):
        value = before[0][chunk] if before else None
        for at, (by, part) in enumerate(parts):
            cut = []
            for first in range(0, count, PER):
                merged = None
                for spot in range(PER):
                    index = first + spot
                    code = read(codes, (by * angle_count + part * count + index) * chunks + chunk)
                    turn_by = (spot * SLOT + LANES - (code & (LANES - 1))) & (LANES - 1)
                    piece = pltpu.roll(held[at * count + index, code >> LANE_BITS], turn_by, 1)
                    merged = piece if spot == 0 else jnp.where(lane < spot * SLOT, merged, piece)
                cut.append(merged.astype(jnp.bfloat16))
            rows = pl.ds(part * count * SLOT, count * SLOT)
            more = jnp.dot(
                jnp.concatenate(cut, axis=1),
                hats[by][chunk, rows, :],
                preferred_element_type=jnp.float32,
            )
            value = more if value is None else value + more
        sums.append(value)
        if not last:
            out[chunk] = value
        if not last or (chunk + 1) * CHUNK % LANES:
            continue
        mine = lax.axis_index("tile")
        for row in range(ROWS_DEV):
            value = jnp.concatenate(
                [part[:, row * CHUNK : (row + 1) * CHUNK] for part in sums], axis=1
            )
            at = row * TCOLS + (chunk + 1) * CHUNK - LANES
            if slices % 8 == 0:
                for turn in range(tiles):
                    tile = lax.rem(mine + turn, tiles)
                    into = pl.ds(pl.multiple_of(tile * slices, slices), slices)
                    ready[into, at : at + LANES] = value[turn * slices : (turn + 1) * slices]
            else:
                ready[:, at : at + LANES] = pltpu.roll(value, mine * slices, 0)
            lanes = pl.ds(at, LANES)
            copies.append(
                pltpu.make_async_copy(
                    ready.at[:, lanes], out.at[0, :, lanes], sent.at[len(copies)]
                )
            )
            copies[-1].start()
        sums = []
    if last:
        for copy in copies:
            copy.wait()


def shifted(value, axis, by):
    size = lax.axis_size(axis)
    return lax.ppermute(value, axis, [(i, (i - by) % size) for i in range(size)])


def swapped(value, axis, by):
    return lax.ppermute(value, axis, [(i, i ^ by) for i in range(lax.axis_size(axis))])


def body(sinogram, paganin_width, window_block):
    local, slices, bins = sinogram.shape
    segments, spots, tiles = (lax.axis_size(name) for name in ("segment", "angle", "tile"))
    segment, spot = lax.axis_index("segment"), lax.axis_index("angle")
    groups = segments * spots
    angle_total = local * groups
    tile_rows = ROWS_DEV * groups
    reach = math.hypot((TCOLS - 1) / 2, (tile_rows - 1) / 2)
    first_bin = max(0, int(WIN / 2 - reach - 0.01)) // 16 * 16
    last_bin = min(WIN - 1, int(WIN / 2 + reach + 0.01) + 1)
    outs = -(-(last_bin + 1 - first_bin) // LANES)
    assert first_bin + (outs - 1) * LANES < WIN and first_bin < LANES
    assert spots & (spots - 1) == 0 and spots > 1
    smooth_blocks = -(-(outs + 3) // 2) * 2
    chunks, pixels = TCOLS // CHUNK, ROWS_DEV * CHUNK
    half = WIN / 2.0 - first_bin

    smem = pl.BlockSpec(memory_space=pltpu.SMEM)
    vmem = pl.BlockSpec(memory_space=pltpu.VMEM)
    hat_bytes = angle_total * SLOT * ROWS_DEV * TCOLS * 2
    params = pltpu.CompilerParams(vmem_limit_bytes=hat_bytes + 12 * 1024 * 1024)
    height = local * slices
    block_total = bins // LANES
    used = last_bin + 1 - first_bin - (outs - 1) * LANES
    row_groups = LANES // (1 << (used - 1).bit_length())
    if height % (8 * row_groups):
        row_groups = 1
    full = outs if row_groups == 1 else outs - 1
    rows_of_block = -(-height // 16) * 16
    tail = 0 if row_groups == 1 else height // row_groups
    packing = (full, rows_of_block, row_groups)
    bits = [1 << bit for bit in reversed(range(spots.bit_length() - 1))]
    exchanges = [(bits[0],)]
    for first in range(1, len(bits), 2):
        pair = bits[first : first + 2]
        exchanges.append((*pair, sum(pair)) if len(pair) == 2 else tuple(pair))
    reached = [0]
    for masks in exchanges:
        reached = [other ^ mask for mask in (0, *masks) for other in reached]
    order = np.repeat(np.array(reached), local), np.tile(np.arange(local), spots)
    where = np.arange(groups)[:, None]
    by = np.arange(segments)[:, None] + where[:, :, None] // spots
    angles = (where % spots ^ order[0]) * local + order[1]
    angles = by % segments * (spots * local) + angles[:, None]
    theta = math.pi * angles.reshape(groups, angle_total) / angle_total
    cosine, sine = np.cos(theta), np.sin(theta)
    left = np.arange(chunks) * CHUNK - (TCOLS - 1) / 2.0
    edges = np.minimum(cosine[..., None] * left, cosine[..., None] * (left + (CHUNK - 1)))
    top = where * ROWS_DEV - (tile_rows - 1) / 2.0
    rise = np.minimum(sine * top, sine * (top + (ROWS_DEV - 1)))
    lows = np.floor(edges + rise[..., None] + (half - 0.01)).astype(np.int32)
    blocks = np.minimum(lows // SLOT, PER * (outs - 1))
    codes = (blocks << LANE_BITS) + lows - blocks * SLOT

    def in_rows(values):
        values = values.reshape(groups, -1)
        rows = -(-values.shape[1] // (8 * LANES)) * 8
        values = np.pad(values, ((0, 0), (0, rows * LANES - values.shape[1])))
        return jnp.asarray(values.reshape(groups, rows, LANES))

    trig_table = in_rows(np.concatenate([cosine, sine], axis=1).astype(np.float32))
    code_table = in_rows(codes.astype(np.int32))

    *cut, trig, codes = pl.pallas_call(
        functools.partial(filter_kernel, (tiles, outs, first_bin, smooth_blocks, packing)),
        out_shape=[
            jax.ShapeDtypeStruct((full * rows_of_block + -(-tail // 16) * 16, LANES), jnp.bfloat16)
        ]
        * tiles
        + [pltpu.SMEM(v.shape[1:], v.dtype) for v in (trig_table, code_table)],
        in_specs=[smem] + [pl.BlockSpec(memory_space=pltpu.HBM)] * 4,
        out_specs=[vmem] * tiles + [smem] * 2,
        scratch_shapes=[
            pltpu.SMEM(window_block.T.shape, jnp.int32),
            pltpu.VMEM(
                (local, slices, (block_total - WIN // LANES + smooth_blocks + 2) * LANES),
                jnp.float32,
            ),
            pltpu.SemaphoreType.DMA((local + 3,)),
        ],
        compiler_params=params,
        name="filter",
    )(
        paganin_width,
        *(
            pltpu.with_memory_space_constraint(value, pltpu.HBM)
            for value in (window_block.T, trig_table, code_table, sinogram)
        ),
    )

    depth = spots * local * SLOT
    def hats_of(part, after):
        ready = lax.optimization_barrier((trig, codes, *after))[:2]
        return pl.pallas_call(
            functools.partial(hat_kernel, (part, half, tile_rows, angle_total)),
            out_shape=jax.ShapeDtypeStruct((chunks, depth, pixels), jnp.bfloat16),
            in_specs=[smem, smem],
            out_specs=vmem,
            compiler_params=params,
            cost_estimate=pl.CostEstimate(
                flops=chunks * depth * pixels * 16, bytes_accessed=0, transcendentals=0
            ),
            name="hats",
        )(*ready)

    hats = []

    def beside(moved, after, count):
        made = []
        for _ in range(min(count, segments - len(hats))):
            made.append(hats_of(len(hats), after))
            hats.append(None)
        moved, made = lax.optimization_barrier((moved, made))
        hats[len(hats) - len(made) :] = made
        return moved

    def joint(turn, mask):
        def index(spot, tile):
            return (spot ^ mask) * tiles + (tile - turn) % tiles

        pairs = [(at, index(at // tiles, at % tiles)) for at in range(spots * tiles)]
        return lax.ppermute(cut[turn], ("angle", "tile"), pairs)

    near = [(turn, mask) for mask in (0, *exchanges[0]) for turn in range(tiles)][1:]
    moved = beside([joint(*pair) for pair in near], cut, 1)
    pieces = jnp.stack([cut[0], *moved])
    whole = full * rows_of_block
    if tail:
        main = pieces[:, :whole].reshape(2, tiles * whole, LANES)
        tails = pieces[:, whole : whole + tail].reshape(2, tiles * tail, LANES)
        pieces = jnp.concatenate([main, tails], axis=1)
    else:
        pieces = pieces.reshape(2, tiles * whole, LANES)
    for masks in exchanges[1:-1]:
        moved = beside([swapped(pieces, "angle", mask) for mask in masks], (pieces,), 1)
        pieces = jnp.concatenate([pieces, *moved])
    held_type = jnp.bfloat16 if slices % 16 == 0 else jnp.float32
    sources = pieces.shape[0]

    sending = [
        pltpu.VMEM((slices * tiles, ROWS_DEV * TCOLS), jnp.float32),
        pltpu.SemaphoreType.DMA((ROWS_DEV * TCOLS // LANES,)),
    ]

    def project(parts, windows, sums, last=False):
        return pl.pallas_call(
            functools.partial(
                project_kernel,
                (parts, sources, len(windows), segments, local, last, tiles, height, packing),
            ),
            out_shape=jax.ShapeDtypeStruct(
                (1, slices * tiles, ROWS_DEV * TCOLS)
                if last
                else (chunks, slices * tiles, pixels),
                jnp.float32,
            ),
            in_specs=[smem] + [vmem] * (len(windows) + segments + len(sums)),
            out_specs=pl.BlockSpec(memory_space=pltpu.HBM) if last else vmem,
            scratch_shapes=[
                pltpu.VMEM(
                    (
                        len(parts) * sources * local,
                        PER * (outs - 1) + 1,
                        slices * tiles,
                        LANES,
                    ),
                    held_type,
                ),
                *(sending if last else []),
            ],
            compiler_params=params,
            cost_estimate=pl.CostEstimate(
                flops=32 * slices * tiles * chunks * depth * pixels,
                bytes_accessed=0,
                transcendentals=0,
            ),
            name="project",
        )(codes, *windows, *hats, *sums)

    others = range(1, segments)
    early = [pieces] + [shifted(pieces, "segment", by) for by in others]
    moved = [swapped(pieces, "angle", mask) for mask in exchanges[-1]]
    hats += [hats_of(part, (pieces,)) for part in range(len(hats), segments)]
    count = len(moved)
    if count > 1:
        early, moved[-1] = lax.optimization_barrier((early, moved[-1]))
    sums = project([(by, 0) for by in range(segments)], early, ())
    if count > 1:
        moved[:-1], sums = lax.optimization_barrier((moved[:-1], sums))
    else:
        moved, sums = lax.optimization_barrier((moved, sums))
    ahead = [shifted(moved[-1], "segment", by) for by in others]
    final = [(by, part) for by in others for part in range(1, count)]
    if final:
        rest = jnp.concatenate(moved[:-1])
        late = [shifted(rest, "segment", by) for by in others]
    own = [(0, part + 1) for part in range(count)]
    first = [(by, count) for by in others]
    if final:
        sums = project(own + first, [*moved, *ahead], (sums,))
        return project(final, late, (sums,), True)
    sums = project(own, moved, (sums,))
    return project(first, ahead, (sums,), True)


def solution(mesh):
    in_specs = (P(("segment", "angle"), "tile", None), P(), P())
    out_specs = P("tile", None, ("segment", "angle"))
    return jax.shard_map(body, mesh=mesh, in_specs=in_specs, out_specs=out_specs, check_vma=False)
```

```python
import functools
import math

import jax
import jax.numpy as jnp
import numpy as np
from jax import lax
from jax.experimental import pallas as pl
from jax.experimental.pallas import tpu as pltpu
from jax.sharding import PartitionSpec as P

WIN = 512
BAND = 128
ROWS_DEV = 8
TCOLS = 256
LANES = 128
LANE_BITS = 7
CHUNK = 32
DEPTH = 40
SLOT = 64
PER = LANES // SLOT


def split(value):
    high = value.astype(jnp.bfloat16)
    return high, (value - high.astype(jnp.float32)).astype(jnp.bfloat16)


def banded(blocks, taps, starts):
    tap_high, tap_low = taps
    count = tap_high.shape[0] // LANES
    dot = functools.partial(jnp.dot, preferred_element_type=jnp.float32)
    parts = [split(block) for block in blocks]
    high, low = (
        jnp.concatenate(
            [
                jnp.concatenate([part[which] for part in parts[at : at + count]], axis=1)
                for at in starts
            ],
            axis=0,
        )
        for which in range(2)
    )
    both = dot(jnp.concatenate([high, low], axis=0), tap_high)
    result = both[: high.shape[0]] + (both[high.shape[0] :] + dot(high, tap_low))
    rows = blocks[0].shape[0]
    return [result[index * rows : (index + 1) * rows] for index in range(len(starts))]


def offsets(depth, width, shift):
    return (
        lax.broadcasted_iota(jnp.int32, (depth, width), 0)
        - lax.broadcasted_iota(jnp.int32, (depth, width), 1)
        - shift
    )


def filter_kernel(plan, width, blocks_ref, trig_table, code_table, rows_ref, *refs):
    tiles, outs, first_bin, smooth_blocks, packing = plan
    full, rows_of_block, groups = packing
    outputs, (trig, codes, blocks, padded, arrived) = (
        refs[:tiles],
        refs[tiles:],
    )
    local, slices, bins = rows_ref.shape
    block_total = bins // LANES
    raw_wide = (smooth_blocks + 2) * LANES
    height = local * slices
    ahead = 2 * LANES

    place = lax.axis_index("segment") * lax.axis_size("angle") + lax.axis_index("angle")
    sources = [(rows_ref.at[i], padded.at[i, :, pl.ds(ahead, bins)]) for i in range(local)]
    sources = [
        *sources,
        (blocks_ref, blocks),
        (trig_table.at[place], trig),
        (code_table.at[place], codes),
    ]
    copies = [
        pltpu.make_async_copy(source, into, arrived.at[index])
        for index, (source, into) in enumerate(sources)
    ]
    for copy in copies:
        copy.start()
    behind = padded.shape[2] - ahead - bins
    padded[:, :, :ahead] = jnp.zeros((local, slices, ahead), jnp.float32)
    padded[:, :, ahead + bins :] = jnp.zeros((local, slices, behind), jnp.float32)

    away = offsets(512, LANES, BAND + first_bin)
    spread = jnp.abs(away)
    squared = jnp.maximum(spread * spread, 1).astype(jnp.float32)
    odd = jnp.logical_and(spread <= BAND, (spread & 1) == 1)
    ramp = jnp.where(odd, -1.0 / (math.pi * math.pi * squared), 0.0)
    ramp = split(jnp.where(away == 0, 0.25, ramp))
    decay = width[0]
    steps = (lax.broadcasted_iota(jnp.int32, (1, BAND), 1) + 1).astype(jnp.float32)
    total = 1.0 + 2.0 * jnp.sum(jnp.exp(-steps / decay), axis=1, keepdims=True)
    away = offsets(2 * 256, 256, BAND)
    spread = jnp.abs(away)
    paganin = jnp.where(
        spread <= BAND, jnp.exp(-spread.astype(jnp.float32) / decay) / total, 0.0
    )
    paganin = split(paganin)

    for copy in copies:
        copy.wait()
    first = place * local
    mine = lax.axis_index("tile")
    starts, raw = [], []
    for turn in range(tiles):
        tile = lax.rem(mine - turn + tiles, tiles)
        for angle in range(local):
            start = blocks[tile, first + angle]
            starts.append(start)
            lanes = pl.ds(pl.multiple_of(start * LANES, LANES), raw_wide)
            raw.append(padded[angle, :, lanes])
    raw = jnp.concatenate(raw, axis=0)
    raw = [raw[:, at : at + LANES] for at in range(0, raw_wide, LANES)]
    smooth = []
    for pair in banded(raw, paganin, range(0, smooth_blocks, 2)):
        smooth += [pair[:, :LANES], pair[:, LANES:]]
    for j in range(smooth_blocks):
        if 1 <= j <= WIN // LANES:
            continue
        kept = []
        for index, start in enumerate(starts):
            block = start - 1 + j
            inside = jnp.logical_and(block >= 0, block < block_total)
            value = smooth[j][index * slices : (index + 1) * slices]
            kept.append(jnp.where(inside, value, 0.0))
        smooth[j] = jnp.concatenate(kept, axis=0)
    for j, value in enumerate(banded(smooth, ramp, range(outs))):
        for turn in range(tiles):
            part = value[turn * height : (turn + 1) * height]
            if j == full:
                part = pack(part, groups)
            if part.shape[0] % 16:
                rest = jnp.zeros((-part.shape[0] % 16, LANES), jnp.float32)
                part = jnp.concatenate([part, rest], axis=0)
            at = j * rows_of_block
            outputs[turn][at : at + part.shape[0], :] = part.astype(jnp.bfloat16)


def pack(value, groups):
    rows, wide = value.shape[0] // groups, LANES // groups
    lane = lax.broadcasted_iota(jnp.int32, (rows, LANES), 1)
    packed = value[:rows]
    for group in range(1, groups):
        more = pltpu.roll(value[group * rows : (group + 1) * rows], group * wide, 1)
        packed = jnp.where(lane < group * wide, packed, more)
    return packed


def unpack(value, groups):
    wide = LANES // groups
    rolled = [pltpu.roll(value, (LANES - group * wide) % LANES, 1) for group in range(groups)]
    return jnp.concatenate(rolled, axis=0)


def read(table, index):
    return table[index >> LANE_BITS, index & (LANES - 1)]


def hat_kernel(plan, trig, codes, hats):
    part, half, tile_rows, angle_total = plan
    chunks, depth, pixels = hats.shape
    count = depth // SLOT
    place = lax.axis_index("segment") * lax.axis_size("angle") + lax.axis_index("angle")
    first_row = (place * ROWS_DEV).astype(jnp.float32) - (tile_rows - 1) / 2.0
    lane = lax.broadcasted_iota(jnp.int32, (8, pixels), 1)
    depth_step = lax.broadcasted_iota(jnp.int32, (8, pixels), 0).astype(jnp.float32)
    y = (lane // CHUNK).astype(jnp.float32) + first_row
    x = (lane % CHUNK).astype(jnp.float32)
    rest = jnp.zeros((-DEPTH % 16, pixels), jnp.float32)
    gap = jnp.zeros((SLOT - DEPTH - DEPTH % 16, pixels), jnp.bfloat16)

    def step(index, carry):
        angle = part * count + index
        cosine, sine = read(trig, angle), read(trig, angle_total + angle)
        at = pl.multiple_of(index * SLOT, SLOT)
        start = y * sine + x * cosine - depth_step
        for chunk in range(chunks):
            left = chunk * CHUNK - (TCOLS - 1) / 2.0
            code = read(codes, angle * chunks + chunk)
            low = ((code >> LANE_BITS) * SLOT + (code & (LANES - 1))).astype(jnp.float32)
            across = start + (left * cosine + (half - low))
            rows = [jnp.maximum(0.0, 1.0 - jnp.abs(across - 8.0 * j)) for j in range(DEPTH // 8)]
            rows = jnp.concatenate([*rows, rest], axis=0).astype(jnp.bfloat16)
            hats[chunk, pl.ds(at, rows.shape[0]), :] = rows
            hats[chunk, pl.ds(at + rows.shape[0], gap.shape[0]), :] = gap
        return carry

    lax.fori_loop(0, count, step, 0, unroll=2)


def by_rows(sums):
    sides = len(sums)
    lane = lax.broadcasted_iota(jnp.int32, (sums[0].shape[0], LANES), 1)
    rows = []
    for first in range(0, sums[0].shape[1], LANES):
        turned = [
            value[:, first : first + LANES]
            if side == 0
            else pltpu.roll(value[:, first : first + LANES], side * CHUNK, 1)
            for side, value in enumerate(sums)
        ]
        for row in range(sides):
            merged = turned[-row % sides]
            for place in range(1, sides):
                more = turned[(place - row) % sides]
                merged = jnp.where(lane < place * CHUNK, merged, more)
            rows.append(pltpu.roll(merged, LANES - row * CHUNK, 1) if row else merged)
    return rows


def project_kernel(plan, codes, *refs):
    parts, sources, arrays, segments, local, last, tiles, height, packing = plan
    full, rows_of_block, groups = packing
    windows, refs = refs[:arrays], refs[arrays:]
    windows = [(window, source) for window in windows for source in range(window.shape[0])]
    scratch = 3 if last else 1
    hats, before = refs[:segments], refs[segments : -1 - scratch]
    out, held = refs[-1 - scratch], refs[-scratch]
    if last:
        ready, sent = refs[-2:]
        copies = []
    chunks, depth, pixels = hats[0].shape
    tail_first = tiles * full * rows_of_block
    slices = height // local
    count = sources * local
    angle_count = depth // SLOT
    spread = lax.broadcasted_iota(jnp.int32, (height, LANES), 1)
    for at, (window, source) in enumerate(windows):
        if groups > 1:
            tails = window[source, tail_first:, :].astype(jnp.float32)
        for turn in range(tiles):
            pieces = []
            for j in range(full):
                rows = pl.ds((turn * full + j) * rows_of_block, rows_of_block)
                pieces.append(window[source, rows, :].astype(held.dtype)[:height])
            if groups > 1:
                tail = height // groups
                tail = tails[turn * tail : (turn + 1) * tail]
                pieces.append(unpack(tail, groups).astype(held.dtype))
            halves = [pltpu.roll(value, SLOT, 1) for value in pieces]
            for j in range(held.shape[1]):
                if j % 2 == 0:
                    value = pieces[j // 2]
                else:
                    value = jnp.where(spread < SLOT, halves[j // 2], halves[j // 2 + 1])
                for angle in range(local):
                    held[at * local + angle, j, turn * slices : (turn + 1) * slices, :] = value[
                        angle * slices : (angle + 1) * slices
                    ]
    lane = lax.broadcasted_iota(jnp.int32, (slices * tiles, LANES), 1)
    sums = []
    for chunk in range(chunks):
        value = before[0][chunk] if before else None
        for at, (by, part) in enumerate(parts):
            cut = []
            for first in range(0, count, PER):
                merged = None
                for spot in range(PER):
                    index = first + spot
                    code = read(codes, (by * angle_count + part * count + index) * chunks + chunk)
                    turn_by = (spot * SLOT + LANES - (code & (LANES - 1))) & (LANES - 1)
                    piece = pltpu.roll(held[at * count + index, code >> LANE_BITS], turn_by, 1)
                    merged = piece if spot == 0 else jnp.where(lane < spot * SLOT, merged, piece)
                cut.append(merged.astype(jnp.bfloat16))
            rows = pl.ds(part * count * SLOT, count * SLOT)
            more = jnp.dot(
                jnp.concatenate(cut, axis=1),
                hats[by][chunk, rows, :],
                preferred_element_type=jnp.float32,
            )
            value = more if value is None else value + more
        sums.append(value)
        if not last:
            out[chunk] = value
        if not last or (chunk + 1) * CHUNK % LANES:
            continue
        mine = lax.axis_index("tile")
        for row, value in enumerate(by_rows(sums)):
            at = row * TCOLS + (chunk + 1) * CHUNK - LANES
            if slices % 8 == 0:
                for turn in range(tiles):
                    tile = lax.rem(mine + turn, tiles)
                    into = pl.ds(pl.multiple_of(tile * slices, slices), slices)
                    ready[into, at : at + LANES] = value[turn * slices : (turn + 1) * slices]
            else:
                ready[:, at : at + LANES] = pltpu.roll(value, mine * slices, 0)
            lanes = pl.ds(at, LANES)
            copies.append(
                pltpu.make_async_copy(
                    ready.at[:, lanes], out.at[0, :, lanes], sent.at[len(copies)]
                )
            )
            copies[-1].start()
        sums = []
    if last:
        for copy in copies:
            copy.wait()


def shifted(value, axis, by):
    size = lax.axis_size(axis)
    return lax.ppermute(value, axis, [(i, (i - by) % size) for i in range(size)])


def swapped(value, axis, by):
    return lax.ppermute(value, axis, [(i, i ^ by) for i in range(lax.axis_size(axis))])


def body(sinogram, paganin_width, window_block):
    local, slices, bins = sinogram.shape
    segments, spots, tiles = (lax.axis_size(name) for name in ("segment", "angle", "tile"))
    segment, spot = lax.axis_index("segment"), lax.axis_index("angle")
    groups = segments * spots
    angle_total = local * groups
    tile_rows = ROWS_DEV * groups
    reach = math.hypot((TCOLS - 1) / 2, (tile_rows - 1) / 2)
    first_bin = max(0, int(WIN / 2 - reach - 0.01)) // 16 * 16
    last_bin = min(WIN - 1, int(WIN / 2 + reach + 0.01) + 1)
    outs = -(-(last_bin + 1 - first_bin) // LANES)
    assert first_bin + (outs - 1) * LANES < WIN and first_bin < LANES
    assert spots & (spots - 1) == 0 and spots > 1
    smooth_blocks = -(-(outs + 3) // 2) * 2
    chunks, pixels = TCOLS // CHUNK, ROWS_DEV * CHUNK
    half = WIN / 2.0 - first_bin

    smem = pl.BlockSpec(memory_space=pltpu.SMEM)
    vmem = pl.BlockSpec(memory_space=pltpu.VMEM)
    hat_bytes = angle_total * SLOT * ROWS_DEV * TCOLS * 2
    params = pltpu.CompilerParams(vmem_limit_bytes=hat_bytes + 12 * 1024 * 1024)
    height = local * slices
    block_total = bins // LANES
    used = last_bin + 1 - first_bin - (outs - 1) * LANES
    row_groups = LANES // (1 << (used - 1).bit_length())
    if height % (8 * row_groups):
        row_groups = 1
    full = outs if row_groups == 1 else outs - 1
    rows_of_block = -(-height // 16) * 16
    tail = 0 if row_groups == 1 else height // row_groups
    packing = (full, rows_of_block, row_groups)
    bits = [1 << bit for bit in reversed(range(spots.bit_length() - 1))]
    exchanges = [(bits[0],)]
    for first in range(1, len(bits), 2):
        pair = bits[first : first + 2]
        exchanges.append((*pair, sum(pair)) if len(pair) == 2 else tuple(pair))
    reached = [0]
    for masks in exchanges:
        reached = [other ^ mask for mask in (0, *masks) for other in reached]
    order = np.repeat(np.array(reached), local), np.tile(np.arange(local), spots)
    where = np.arange(groups)[:, None]
    by = np.arange(segments)[:, None] + where[:, :, None] // spots
    angles = (where % spots ^ order[0]) * local + order[1]
    angles = by % segments * (spots * local) + angles[:, None]
    theta = math.pi * angles.reshape(groups, angle_total) / angle_total
    cosine, sine = np.cos(theta), np.sin(theta)
    left = np.arange(chunks) * CHUNK - (TCOLS - 1) / 2.0
    edges = np.minimum(cosine[..., None] * left, cosine[..., None] * (left + (CHUNK - 1)))
    top = where * ROWS_DEV - (tile_rows - 1) / 2.0
    rise = np.minimum(sine * top, sine * (top + (ROWS_DEV - 1)))
    lows = np.floor(edges + rise[..., None] + (half - 0.01)).astype(np.int32)
    blocks = np.minimum(lows // SLOT, PER * (outs - 1))
    codes = (blocks << LANE_BITS) + lows - blocks * SLOT

    def in_rows(values):
        values = values.reshape(groups, -1)
        rows = -(-values.shape[1] // (8 * LANES)) * 8
        values = np.pad(values, ((0, 0), (0, rows * LANES - values.shape[1])))
        return jnp.asarray(values.reshape(groups, rows, LANES))

    trig_table = in_rows(np.concatenate([cosine, sine], axis=1).astype(np.float32))
    code_table = in_rows(codes.astype(np.int32))

    *cut, trig, codes = pl.pallas_call(
        functools.partial(filter_kernel, (tiles, outs, first_bin, smooth_blocks, packing)),
        out_shape=[
            jax.ShapeDtypeStruct((full * rows_of_block + -(-tail // 16) * 16, LANES), jnp.bfloat16)
        ]
        * tiles
        + [pltpu.SMEM(v.shape[1:], v.dtype) for v in (trig_table, code_table)],
        in_specs=[smem] + [pl.BlockSpec(memory_space=pltpu.HBM)] * 4,
        out_specs=[vmem] * tiles + [smem] * 2,
        scratch_shapes=[
            pltpu.SMEM(window_block.T.shape, jnp.int32),
            pltpu.VMEM(
                (local, slices, (block_total - WIN // LANES + smooth_blocks + 2) * LANES),
                jnp.float32,
            ),
            pltpu.SemaphoreType.DMA((local + 3,)),
        ],
        compiler_params=params,
        name="filter",
    )(
        paganin_width,
        *(
            pltpu.with_memory_space_constraint(value, pltpu.HBM)
            for value in (window_block.T, trig_table, code_table, sinogram)
        ),
    )

    depth = spots * local * SLOT
    def hats_of(part, after):
        ready = lax.optimization_barrier((trig, codes, *after))[:2]
        return pl.pallas_call(
            functools.partial(hat_kernel, (part, half, tile_rows, angle_total)),
            out_shape=jax.ShapeDtypeStruct((chunks, depth, pixels), jnp.bfloat16),
            in_specs=[smem, smem],
            out_specs=vmem,
            compiler_params=params,
            cost_estimate=pl.CostEstimate(
                flops=chunks * depth * pixels * 16, bytes_accessed=0, transcendentals=0
            ),
            name="hats",
        )(*ready)

    hats = []

    def beside(moved, after, count):
        made = []
        for _ in range(min(count, segments - len(hats))):
            made.append(hats_of(len(hats), after))
            hats.append(None)
        moved, made = lax.optimization_barrier((moved, made))
        hats[len(hats) - len(made) :] = made
        return moved

    def joint(turn, mask):
        def index(spot, tile):
            return (spot ^ mask) * tiles + (tile - turn) % tiles

        pairs = [(at, index(at // tiles, at % tiles)) for at in range(spots * tiles)]
        return lax.ppermute(cut[turn], ("angle", "tile"), pairs)

    near = [(turn, mask) for mask in (0, *exchanges[0]) for turn in range(tiles)][1:]
    moved = beside([joint(*pair) for pair in near], cut, 1)
    pieces = jnp.stack([cut[0], *moved])
    whole = full * rows_of_block
    if tail:
        main = pieces[:, :whole].reshape(2, tiles * whole, LANES)
        tails = pieces[:, whole : whole + tail].reshape(2, tiles * tail, LANES)
        pieces = jnp.concatenate([main, tails], axis=1)
    else:
        pieces = pieces.reshape(2, tiles * whole, LANES)
    for masks in exchanges[1:-1]:
        moved = beside([swapped(pieces, "angle", mask) for mask in masks], (pieces,), 1)
        pieces = jnp.concatenate([pieces, *moved])
    held_type = jnp.bfloat16 if slices % 16 == 0 else jnp.float32
    sources = pieces.shape[0]

    sending = [
        pltpu.VMEM((slices * tiles, ROWS_DEV * TCOLS), jnp.float32),
        pltpu.SemaphoreType.DMA((ROWS_DEV * TCOLS // LANES,)),
    ]

    def project(parts, windows, sums, last=False):
        return pl.pallas_call(
            functools.partial(
                project_kernel,
                (parts, sources, len(windows), segments, local, last, tiles, height, packing),
            ),
            out_shape=jax.ShapeDtypeStruct(
                (1, slices * tiles, ROWS_DEV * TCOLS)
                if last
                else (chunks, slices * tiles, pixels),
                jnp.float32,
            ),
            in_specs=[smem] + [vmem] * (len(windows) + segments + len(sums)),
            out_specs=pl.BlockSpec(memory_space=pltpu.HBM) if last else vmem,
            scratch_shapes=[
                pltpu.VMEM(
                    (
                        len(parts) * sources * local,
                        PER * (outs - 1) + 1,
                        slices * tiles,
                        LANES,
                    ),
                    held_type,
                ),
                *(sending if last else []),
            ],
            compiler_params=params,
            cost_estimate=pl.CostEstimate(
                flops=32 * slices * tiles * chunks * depth * pixels,
                bytes_accessed=0,
                transcendentals=0,
            ),
            name="project",
        )(codes, *windows, *hats, *sums)

    others = range(1, segments)
    early = [pieces] + [shifted(pieces, "segment", by) for by in others]
    moved = [swapped(pieces, "angle", mask) for mask in exchanges[-1]]
    hats += [hats_of(part, (pieces,)) for part in range(len(hats), segments)]
    count = len(moved)
    if count > 1:
        early, moved[-1] = lax.optimization_barrier((early, moved[-1]))
    sums = project([(by, 0) for by in range(segments)], early, ())
    if count > 1:
        moved[:-1], sums = lax.optimization_barrier((moved[:-1], sums))
    else:
        moved, sums = lax.optimization_barrier((moved, sums))
    ahead = [shifted(moved[-1], "segment", by) for by in others]
    final = [(by, part) for by in others for part in range(1, count)]
    if final:
        rest = jnp.concatenate(moved[:-1])
        late = [shifted(rest, "segment", by) for by in others]
    own = [(0, part + 1) for part in range(count)]
    first = [(by, count) for by in others]
    if final:
        sums = project(own + first, [*moved, *ahead], (sums,))
        return project(final, late, (sums,), True)
    sums = project(own, moved, (sums,))
    return project(first, ahead, (sums,), True)


def solution(mesh):
    in_specs = (P(("segment", "angle"), "tile", None), P(), P())
    out_specs = P("tile", None, ("segment", "angle"))
    return jax.shard_map(body, mesh=mesh, in_specs=in_specs, out_specs=out_specs, check_vma=False)
```

```python
import functools
import math

import jax
import jax.numpy as jnp
import numpy as np
from jax import lax
from jax.experimental import pallas as pl
from jax.experimental.pallas import tpu as pltpu
from jax.sharding import PartitionSpec as P

WIN = 512
BAND = 128
ROWS_DEV = 8
TCOLS = 256
LANES = 128
LANE_BITS = 7
CHUNK = 32
DEPTH = 40
SLOT = 64
PER = LANES // SLOT


def split(value):
    high = value.astype(jnp.bfloat16)
    return high, (value - high.astype(jnp.float32)).astype(jnp.bfloat16)


def banded(blocks, taps, starts):
    tap_high, tap_low = taps
    count = tap_high.shape[0] // LANES
    dot = functools.partial(jnp.dot, preferred_element_type=jnp.float32)
    parts = [split(block) for block in blocks]
    high, low = (
        jnp.concatenate(
            [
                jnp.concatenate([part[which] for part in parts[at : at + count]], axis=1)
                for at in starts
            ],
            axis=0,
        )
        for which in range(2)
    )
    both = dot(jnp.concatenate([high, low], axis=0), tap_high)
    result = both[: high.shape[0]] + (both[high.shape[0] :] + dot(high, tap_low))
    rows = blocks[0].shape[0]
    return [result[index * rows : (index + 1) * rows] for index in range(len(starts))]


def offsets(depth, width, shift):
    return (
        lax.broadcasted_iota(jnp.int32, (depth, width), 0)
        - lax.broadcasted_iota(jnp.int32, (depth, width), 1)
        - shift
    )


def filter_kernel(plan, width, blocks_ref, trig_table, code_table, rows_ref, *refs):
    tiles, outs, first_bin, smooth_blocks, packing = plan
    full, rows_of_block, groups = packing
    outputs, (trig, codes, blocks, padded, arrived) = (
        refs[:tiles],
        refs[tiles:],
    )
    local, slices, bins = rows_ref.shape
    block_total = bins // LANES
    raw_wide = (smooth_blocks + 2) * LANES
    height = local * slices
    ahead = 2 * LANES

    place = lax.axis_index("segment") * lax.axis_size("angle") + lax.axis_index("angle")
    sources = [(rows_ref.at[i], padded.at[i, :, pl.ds(ahead, bins)]) for i in range(local)]
    sources = [
        *sources,
        (blocks_ref, blocks),
        (trig_table.at[place], trig),
        (code_table.at[place], codes),
    ]
    copies = [
        pltpu.make_async_copy(source, into, arrived.at[index])
        for index, (source, into) in enumerate(sources)
    ]
    for copy in copies:
        copy.start()
    behind = padded.shape[2] - ahead - bins
    padded[:, :, :ahead] = jnp.zeros((local, slices, ahead), jnp.float32)
    padded[:, :, ahead + bins :] = jnp.zeros((local, slices, behind), jnp.float32)

    away = offsets(512, LANES, BAND + first_bin)
    spread = jnp.abs(away)
    squared = jnp.maximum(spread * spread, 1).astype(jnp.float32)
    odd = jnp.logical_and(spread <= BAND, (spread & 1) == 1)
    ramp = jnp.where(odd, -1.0 / (math.pi * math.pi * squared), 0.0)
    ramp = split(jnp.where(away == 0, 0.25, ramp))
    decay = width[0]
    steps = (lax.broadcasted_iota(jnp.int32, (1, BAND), 1) + 1).astype(jnp.float32)
    total = 1.0 + 2.0 * jnp.sum(jnp.exp(-steps / decay), axis=1, keepdims=True)
    away = offsets(2 * 256, 256, BAND)
    spread = jnp.abs(away)
    paganin = jnp.where(
        spread <= BAND, jnp.exp(-spread.astype(jnp.float32) / decay) / total, 0.0
    )
    paganin = split(paganin)

    for copy in copies:
        copy.wait()
    first = place * local
    mine = lax.axis_index("tile")
    starts, raw = [], []
    for turn in range(tiles):
        tile = lax.rem(mine - turn + tiles, tiles)
        for angle in range(local):
            start = blocks[tile, first + angle]
            starts.append(start)
            lanes = pl.ds(pl.multiple_of(start * LANES, LANES), raw_wide)
            raw.append(padded[angle, :, lanes])
    raw = jnp.concatenate(raw, axis=0)
    raw = [raw[:, at : at + LANES] for at in range(0, raw_wide, LANES)]
    smooth = []
    for pair in banded(raw, paganin, range(0, smooth_blocks, 2)):
        smooth += [pair[:, :LANES], pair[:, LANES:]]
    for j in range(smooth_blocks):
        if 1 <= j <= WIN // LANES:
            continue
        kept = []
        for index, start in enumerate(starts):
            block = start - 1 + j
            inside = jnp.logical_and(block >= 0, block < block_total)
            value = smooth[j][index * slices : (index + 1) * slices]
            kept.append(jnp.where(inside, value, 0.0))
        smooth[j] = jnp.concatenate(kept, axis=0)
    for j, value in enumerate(banded(smooth, ramp, range(outs))):
        for turn in range(tiles):
            part = value[turn * height : (turn + 1) * height]
            if j == full:
                part = pack(part, groups)
            if part.shape[0] % 16:
                rest = jnp.zeros((-part.shape[0] % 16, LANES), jnp.float32)
                part = jnp.concatenate([part, rest], axis=0)
            at = j * rows_of_block
            outputs[turn][at : at + part.shape[0], :] = part.astype(jnp.bfloat16)


def pack(value, groups):
    rows, wide = value.shape[0] // groups, LANES // groups
    lane = lax.broadcasted_iota(jnp.int32, (rows, LANES), 1)
    packed = value[:rows]
    for group in range(1, groups):
        more = pltpu.roll(value[group * rows : (group + 1) * rows], group * wide, 1)
        packed = jnp.where(lane < group * wide, packed, more)
    return packed


def unpack(value, groups):
    wide = LANES // groups
    rolled = [pltpu.roll(value, (LANES - group * wide) % LANES, 1) for group in range(groups)]
    return jnp.concatenate(rolled, axis=0)


def read(table, index):
    return table[index >> LANE_BITS, index & (LANES - 1)]


def hat_kernel(plan, trig, codes, hats):
    part, half, tile_rows, angle_total = plan
    chunks, depth, pixels = hats.shape
    count = depth // SLOT
    place = lax.axis_index("segment") * lax.axis_size("angle") + lax.axis_index("angle")
    first_row = (place * ROWS_DEV).astype(jnp.float32) - (tile_rows - 1) / 2.0
    lane = lax.broadcasted_iota(jnp.int32, (8, pixels), 1)
    depth_step = lax.broadcasted_iota(jnp.int32, (8, pixels), 0).astype(jnp.float32)
    y = (lane // CHUNK).astype(jnp.float32) + first_row
    x = (lane % CHUNK).astype(jnp.float32)
    rest = jnp.zeros((-DEPTH % 16, pixels), jnp.float32)
    gap = jnp.zeros((SLOT - DEPTH - DEPTH % 16, pixels), jnp.bfloat16)

    def step(index, carry):
        angle = part * count + index
        cosine, sine = read(trig, angle), read(trig, angle_total + angle)
        at = pl.multiple_of(index * SLOT, SLOT)
        start = y * sine + x * cosine - depth_step
        for chunk in range(chunks):
            left = chunk * CHUNK - (TCOLS - 1) / 2.0
            code = read(codes, angle * chunks + chunk)
            low = ((code >> LANE_BITS) * SLOT + (code & (LANES - 1))).astype(jnp.float32)
            across = start + (left * cosine + (half - low))
            rows = [jnp.maximum(0.0, 1.0 - jnp.abs(across - 8.0 * j)) for j in range(DEPTH // 8)]
            rows = jnp.concatenate([*rows, rest], axis=0).astype(jnp.bfloat16)
            hats[chunk, pl.ds(at, rows.shape[0]), :] = rows
            hats[chunk, pl.ds(at + rows.shape[0], gap.shape[0]), :] = gap
        return carry

    lax.fori_loop(0, count, step, 0, unroll=2)


def project_kernel(plan, codes, *refs):
    parts, sources, arrays, segments, local, last, tiles, height, packing = plan
    full, rows_of_block, groups = packing
    windows, refs = refs[:arrays], refs[arrays:]
    windows = [(window, source) for window in windows for source in range(window.shape[0])]
    scratch = 3 if last else 1
    hats, before = refs[:segments], refs[segments : -1 - scratch]
    out, held = refs[-1 - scratch], refs[-scratch]
    if last:
        ready, sent = refs[-2:]
        copies = []
    chunks, depth, pixels = hats[0].shape
    tail_first = tiles * full * rows_of_block
    slices = height // local
    count = sources * local
    angle_count = depth // SLOT
    spread = lax.broadcasted_iota(jnp.int32, (height, LANES), 1)
    for at, (window, source) in enumerate(windows):
        if groups > 1:
            tails = window[source, tail_first:, :].astype(jnp.float32)
        for turn in range(tiles):
            pieces = []
            for j in range(full):
                rows = pl.ds((turn * full + j) * rows_of_block, rows_of_block)
                pieces.append(window[source, rows, :].astype(held.dtype)[:height])
            if groups > 1:
                tail = height // groups
                tail = tails[turn * tail : (turn + 1) * tail]
                pieces.append(unpack(tail, groups).astype(held.dtype))
            halves = [pltpu.roll(value, SLOT, 1) for value in pieces]
            for j in range(held.shape[1]):
                if j % 2 == 0:
                    value = pieces[j // 2]
                else:
                    value = jnp.where(spread < SLOT, halves[j // 2], halves[j // 2 + 1])
                for angle in range(local):
                    held[at * local + angle, j, turn * slices : (turn + 1) * slices, :] = value[
                        angle * slices : (angle + 1) * slices
                    ]
    lane = lax.broadcasted_iota(jnp.int32, (slices * tiles, LANES), 1)
    sums = []
    for chunk in range(chunks):
        value = before[0][chunk] if before else None
        for at, (by, part) in enumerate(parts):
            cut = []
            for first in range(0, count, PER):
                merged = None
                for spot in range(PER):
                    index = first + spot
                    code = read(codes, (by * angle_count + part * count + index) * chunks + chunk)
                    turn_by = (spot * SLOT + LANES - (code & (LANES - 1))) & (LANES - 1)
                    piece = pltpu.roll(held[at * count + index, code >> LANE_BITS], turn_by, 1)
                    merged = piece if spot == 0 else jnp.where(lane < spot * SLOT, merged, piece)
                cut.append(merged.astype(jnp.bfloat16))
            rows = pl.ds(part * count * SLOT, count * SLOT)
            more = jnp.dot(
                jnp.concatenate(cut, axis=1),
                hats[by][chunk, rows, :],
                preferred_element_type=jnp.float32,
            )
            value = more if value is None else value + more
        sums.append(value)
        if not last:
            out[chunk] = value
        if not last or (chunk + 1) * CHUNK % LANES:
            continue
        mine = lax.axis_index("tile")
        for row in range(ROWS_DEV):
            value = jnp.concatenate(
                [part[:, row * CHUNK : (row + 1) * CHUNK] for part in sums], axis=1
            )
            at = row * TCOLS + (chunk + 1) * CHUNK - LANES
            if slices % 8 == 0:
                for turn in range(tiles):
                    tile = lax.rem(mine + turn, tiles)
                    into = pl.ds(pl.multiple_of(tile * slices, slices), slices)
                    ready[into, at : at + LANES] = value[turn * slices : (turn + 1) * slices]
            else:
                ready[:, at : at + LANES] = pltpu.roll(value, mine * slices, 0)
            lanes = pl.ds(at, LANES)
            copies.append(
                pltpu.make_async_copy(
                    ready.at[:, lanes], out.at[0, :, lanes], sent.at[len(copies)]
                )
            )
            copies[-1].start()
        sums = []
    if last:
        for copy in copies:
            copy.wait()


def shifted(value, axis, by):
    size = lax.axis_size(axis)
    return lax.ppermute(value, axis, [(i, (i - by) % size) for i in range(size)])


def swapped(value, axis, by):
    return lax.ppermute(value, axis, [(i, i ^ by) for i in range(lax.axis_size(axis))])


def body(sinogram, paganin_width, window_block):
    local, slices, bins = sinogram.shape
    segments, spots, tiles = (lax.axis_size(name) for name in ("segment", "angle", "tile"))
    segment, spot = lax.axis_index("segment"), lax.axis_index("angle")
    groups = segments * spots
    angle_total = local * groups
    tile_rows = ROWS_DEV * groups
    reach = math.hypot((TCOLS - 1) / 2, (tile_rows - 1) / 2)
    first_bin = max(0, int(WIN / 2 - reach - 0.01)) // 16 * 16
    last_bin = min(WIN - 1, int(WIN / 2 + reach + 0.01) + 1)
    outs = -(-(last_bin + 1 - first_bin) // LANES)
    assert first_bin + (outs - 1) * LANES < WIN and first_bin < LANES
    assert spots & (spots - 1) == 0 and spots > 1
    smooth_blocks = -(-(outs + 3) // 2) * 2
    chunks, pixels = TCOLS // CHUNK, ROWS_DEV * CHUNK
    half = WIN / 2.0 - first_bin

    smem = pl.BlockSpec(memory_space=pltpu.SMEM)
    vmem = pl.BlockSpec(memory_space=pltpu.VMEM)
    hat_bytes = angle_total * SLOT * ROWS_DEV * TCOLS * 2
    params = pltpu.CompilerParams(vmem_limit_bytes=hat_bytes + 12 * 1024 * 1024)
    height = local * slices
    block_total = bins // LANES
    used = last_bin + 1 - first_bin - (outs - 1) * LANES
    row_groups = LANES // (1 << (used - 1).bit_length())
    if height % (8 * row_groups):
        row_groups = 1
    full = outs if row_groups == 1 else outs - 1
    rows_of_block = -(-height // 16) * 16
    tail = 0 if row_groups == 1 else height // row_groups
    packing = (full, rows_of_block, row_groups)
    bits = [1 << bit for bit in reversed(range(spots.bit_length() - 1))]
    exchanges = [(bits[0],)]
    for first in range(1, len(bits), 2):
        pair = bits[first : first + 2]
        exchanges.append((*pair, sum(pair)) if len(pair) == 2 else tuple(pair))
    reached = [0]
    for masks in exchanges:
        reached = [other ^ mask for mask in (0, *masks) for other in reached]
    order = np.repeat(np.array(reached), local), np.tile(np.arange(local), spots)
    where = np.arange(groups)[:, None]
    by = np.arange(segments)[:, None] + where[:, :, None] // spots
    angles = (where % spots ^ order[0]) * local + order[1]
    angles = by % segments * (spots * local) + angles[:, None]
    theta = math.pi * angles.reshape(groups, angle_total) / angle_total
    cosine, sine = np.cos(theta), np.sin(theta)
    left = np.arange(chunks) * CHUNK - (TCOLS - 1) / 2.0
    edges = np.minimum(cosine[..., None] * left, cosine[..., None] * (left + (CHUNK - 1)))
    top = where * ROWS_DEV - (tile_rows - 1) / 2.0
    rise = np.minimum(sine * top, sine * (top + (ROWS_DEV - 1)))
    lows = np.floor(edges + rise[..., None] + (half - 0.01)).astype(np.int32)
    blocks = np.minimum(lows // SLOT, PER * (outs - 1))
    codes = (blocks << LANE_BITS) + lows - blocks * SLOT

    def in_rows(values):
        values = values.reshape(groups, -1)
        rows = -(-values.shape[1] // (8 * LANES)) * 8
        values = np.pad(values, ((0, 0), (0, rows * LANES - values.shape[1])))
        return jnp.asarray(values.reshape(groups, rows, LANES))

    trig_table = in_rows(np.concatenate([cosine, sine], axis=1).astype(np.float32))
    code_table = in_rows(codes.astype(np.int32))

    *cut, trig, codes = pl.pallas_call(
        functools.partial(filter_kernel, (tiles, outs, first_bin, smooth_blocks, packing)),
        out_shape=[
            jax.ShapeDtypeStruct((full * rows_of_block + -(-tail // 16) * 16, LANES), jnp.bfloat16)
        ]
        * tiles
        + [pltpu.SMEM(v.shape[1:], v.dtype) for v in (trig_table, code_table)],
        in_specs=[smem] + [pl.BlockSpec(memory_space=pltpu.HBM)] * 4,
        out_specs=[vmem] * tiles + [smem] * 2,
        scratch_shapes=[
            pltpu.SMEM(window_block.T.shape, jnp.int32),
            pltpu.VMEM(
                (local, slices, (block_total - WIN // LANES + smooth_blocks + 2) * LANES),
                jnp.float32,
            ),
            pltpu.SemaphoreType.DMA((local + 3,)),
        ],
        compiler_params=params,
        name="filter",
    )(
        paganin_width,
        *(
            pltpu.with_memory_space_constraint(value, pltpu.HBM)
            for value in (window_block.T, trig_table, code_table, sinogram)
        ),
    )

    depth = spots * local * SLOT
    def hats_of(part, after):
        ready = lax.optimization_barrier((trig, codes, *after))[:2]
        return pl.pallas_call(
            functools.partial(hat_kernel, (part, half, tile_rows, angle_total)),
            out_shape=jax.ShapeDtypeStruct((chunks, depth, pixels), jnp.bfloat16),
            in_specs=[smem, smem],
            out_specs=vmem,
            compiler_params=params,
            cost_estimate=pl.CostEstimate(
                flops=chunks * depth * pixels * 16, bytes_accessed=0, transcendentals=0
            ),
            name="hats",
        )(*ready)

    hats = []

    def beside(moved, after, count):
        made = []
        for _ in range(min(count, segments - len(hats))):
            made.append(hats_of(len(hats), after))
            hats.append(None)
        moved, made = lax.optimization_barrier((moved, made))
        hats[len(hats) - len(made) :] = made
        return moved

    def joint(turn, mask):
        def index(spot, tile):
            return (spot ^ mask) * tiles + (tile - turn) % tiles

        pairs = [(at, index(at // tiles, at % tiles)) for at in range(spots * tiles)]
        return lax.ppermute(cut[turn], ("angle", "tile"), pairs)

    near = [(turn, mask) for mask in (0, *exchanges[0]) for turn in range(tiles)][1:]
    moved = beside([joint(*pair) for pair in near], cut, 1)
    pieces = jnp.stack([cut[0], *moved])
    whole = full * rows_of_block
    if tail:
        main = pieces[:, :whole].reshape(2, tiles * whole, LANES)
        tails = pieces[:, whole : whole + tail].reshape(2, tiles * tail, LANES)
        pieces = jnp.concatenate([main, tails], axis=1)
    else:
        pieces = pieces.reshape(2, tiles * whole, LANES)
    for masks in exchanges[1:-1]:
        moved = beside([swapped(pieces, "angle", mask) for mask in masks], (pieces,), 1)
        pieces = jnp.concatenate([pieces, *moved])
    held_type = jnp.bfloat16 if slices % 16 == 0 else jnp.float32
    sources = pieces.shape[0]

    sending = [
        pltpu.VMEM((slices * tiles, ROWS_DEV * TCOLS), jnp.float32),
        pltpu.SemaphoreType.DMA((ROWS_DEV * TCOLS // LANES,)),
    ]

    def project(parts, windows, sums, last=False):
        return pl.pallas_call(
            functools.partial(
                project_kernel,
                (parts, sources, len(windows), segments, local, last, tiles, height, packing),
            ),
            out_shape=jax.ShapeDtypeStruct(
                (1, slices * tiles, ROWS_DEV * TCOLS)
                if last
                else (chunks, slices * tiles, pixels),
                jnp.float32,
            ),
            in_specs=[smem] + [vmem] * (len(windows) + segments + len(sums)),
            out_specs=pl.BlockSpec(memory_space=pltpu.HBM) if last else vmem,
            scratch_shapes=[
                pltpu.VMEM(
                    (
                        len(parts) * sources * local,
                        PER * (outs - 1) + 1,
                        slices * tiles,
                        LANES,
                    ),
                    held_type,
                ),
                *(sending if last else []),
            ],
            compiler_params=params,
            cost_estimate=pl.CostEstimate(
                flops=32 * slices * tiles * chunks * depth * pixels,
                bytes_accessed=0,
                transcendentals=0,
            ),
            name="project",
        )(codes, *windows, *hats, *sums)

    others = range(1, segments)
    moved = [swapped(pieces, "angle", mask) for mask in reversed(exchanges[-1])][::-1]
    hats += [hats_of(part, (pieces,)) for part in range(len(hats), segments)]
    count = len(moved)
    if count > 1:
        pieces, moved[-1] = lax.optimization_barrier((pieces, moved[-1]))
    sums = project([(0, 0)], [pieces], ())
    if count > 1:
        moved[:-1], sums = lax.optimization_barrier((moved[:-1], sums))
    else:
        moved, sums = lax.optimization_barrier((moved, sums))
    ahead = jnp.concatenate([pieces, moved[-1]])
    ahead = [shifted(ahead, "segment", by) for by in others]
    final = [(by, part) for by in others for part in range(1, count)]
    if final:
        rest = jnp.concatenate(moved[:-1])
        late = [shifted(rest, "segment", by) for by in others]
    own = [(0, part + 1) for part in range(count)]
    first = [(by, part) for by in others for part in (0, count)]
    if final:
        sums = project(own + first, [*moved, *ahead], (sums,))
        return project(final, late, (sums,), True)
    sums = project(own, moved, (sums,))
    return project(first, ahead, (sums,), True)


def solution(mesh):
    in_specs = (P(("segment", "angle"), "tile", None), P(), P())
    out_specs = P("tile", None, ("segment", "angle"))
    return jax.shard_map(body, mesh=mesh, in_specs=in_specs, out_specs=out_specs, check_vma=False)
```

```python
import functools
import math

import jax
import jax.numpy as jnp
import numpy as np
from jax import lax
from jax.experimental import pallas as pl
from jax.experimental.pallas import tpu as pltpu
from jax.sharding import PartitionSpec as P

WIN = 512
BAND = 128
ROWS_DEV = 8
TCOLS = 256
LANES = 128
LANE_BITS = 7
CHUNK = 32
DEPTH = 40
SLOT = 64
PER = LANES // SLOT


def split(value):
    high = value.astype(jnp.bfloat16)
    return high, (value - high.astype(jnp.float32)).astype(jnp.bfloat16)


def banded(blocks, taps, starts):
    tap_high, tap_low = taps
    count = tap_high.shape[0] // LANES
    dot = functools.partial(jnp.dot, preferred_element_type=jnp.float32)
    parts = [split(block) for block in blocks]
    high, low = (
        jnp.concatenate(
            [
                jnp.concatenate([part[which] for part in parts[at : at + count]], axis=1)
                for at in starts
            ],
            axis=0,
        )
        for which in range(2)
    )
    both = dot(jnp.concatenate([high, low], axis=0), tap_high)
    result = both[: high.shape[0]] + (both[high.shape[0] :] + dot(high, tap_low))
    rows = blocks[0].shape[0]
    return [result[index * rows : (index + 1) * rows] for index in range(len(starts))]


def offsets(depth, width, shift):
    return (
        lax.broadcasted_iota(jnp.int32, (depth, width), 0)
        - lax.broadcasted_iota(jnp.int32, (depth, width), 1)
        - shift
    )


def filter_kernel(plan, width, blocks_ref, trig_table, code_table, rows_ref, *refs):
    tiles, outs, first_bin, smooth_blocks, packing = plan
    full, rows_of_block, groups = packing
    outputs, (trig, codes, blocks, padded, arrived) = (
        refs[:tiles],
        refs[tiles:],
    )
    local, slices, bins = rows_ref.shape
    block_total = bins // LANES
    raw_wide = (smooth_blocks + 2) * LANES
    height = local * slices
    ahead = 2 * LANES

    place = lax.axis_index("segment") * lax.axis_size("angle") + lax.axis_index("angle")
    sources = [(rows_ref.at[i], padded.at[i, :, pl.ds(ahead, bins)]) for i in range(local)]
    sources = [
        (blocks_ref, blocks),
        *sources,
        (trig_table.at[place], trig),
        (code_table.at[place], codes),
    ]
    copies = [
        pltpu.make_async_copy(source, into, arrived.at[index])
        for index, (source, into) in enumerate(sources)
    ]
    for copy in copies:
        copy.start()
    behind = padded.shape[2] - ahead - bins
    padded[:, :, :ahead] = jnp.zeros((local, slices, ahead), jnp.float32)
    padded[:, :, ahead + bins :] = jnp.zeros((local, slices, behind), jnp.float32)

    away = offsets(512, LANES, BAND + first_bin)
    spread = jnp.abs(away)
    squared = jnp.maximum(spread * spread, 1).astype(jnp.float32)
    odd = jnp.logical_and(spread <= BAND, (spread & 1) == 1)
    ramp = jnp.where(odd, -1.0 / (math.pi * math.pi * squared), 0.0)
    ramp = split(jnp.where(away == 0, 0.25, ramp))
    decay = width[0]
    steps = (lax.broadcasted_iota(jnp.int32, (1, BAND), 1) + 1).astype(jnp.float32)
    total = 1.0 + 2.0 * jnp.sum(jnp.exp(-steps / decay), axis=1, keepdims=True)
    away = offsets(2 * 256, 256, BAND)
    spread = jnp.abs(away)
    paganin = jnp.where(
        spread <= BAND, jnp.exp(-spread.astype(jnp.float32) / decay) / total, 0.0
    )
    paganin = split(paganin)

    for copy in copies[: local + 1]:
        copy.wait()
    first = place * local
    mine = lax.axis_index("tile")
    starts, raw = [], []
    for turn in range(tiles):
        tile = lax.rem(mine - turn + tiles, tiles)
        for angle in range(local):
            start = blocks[tile, first + angle]
            starts.append(start)
            lanes = pl.ds(pl.multiple_of(start * LANES, LANES), raw_wide)
            raw.append(padded[angle, :, lanes])
    raw = jnp.concatenate(raw, axis=0)
    raw = [raw[:, at : at + LANES] for at in range(0, raw_wide, LANES)]
    smooth = []
    for pair in banded(raw, paganin, range(0, smooth_blocks, 2)):
        smooth += [pair[:, :LANES], pair[:, LANES:]]
    for j in range(smooth_blocks):
        if 1 <= j <= WIN // LANES:
            continue
        kept = []
        for index, start in enumerate(starts):
            block = start - 1 + j
            inside = jnp.logical_and(block >= 0, block < block_total)
            value = smooth[j][index * slices : (index + 1) * slices]
            kept.append(jnp.where(inside, value, 0.0))
        smooth[j] = jnp.concatenate(kept, axis=0)
    for j, value in enumerate(banded(smooth, ramp, range(outs))):
        for turn in range(tiles):
            part = value[turn * height : (turn + 1) * height]
            if j == full:
                part = pack(part, groups)
            if part.shape[0] % 16:
                rest = jnp.zeros((-part.shape[0] % 16, LANES), jnp.float32)
                part = jnp.concatenate([part, rest], axis=0)
            at = j * rows_of_block
            outputs[turn][at : at + part.shape[0], :] = part.astype(jnp.bfloat16)
    for copy in copies[local + 1 :]:
        copy.wait()


def pack(value, groups):
    rows, wide = value.shape[0] // groups, LANES // groups
    lane = lax.broadcasted_iota(jnp.int32, (rows, LANES), 1)
    packed = value[:rows]
    for group in range(1, groups):
        more = pltpu.roll(value[group * rows : (group + 1) * rows], group * wide, 1)
        packed = jnp.where(lane < group * wide, packed, more)
    return packed


def unpack(value, groups):
    wide = LANES // groups
    rolled = [pltpu.roll(value, (LANES - group * wide) % LANES, 1) for group in range(groups)]
    return jnp.concatenate(rolled, axis=0)


def read(table, index):
    return table[index >> LANE_BITS, index & (LANES - 1)]


def hat_kernel(plan, trig, codes, hats):
    part, half, tile_rows, angle_total = plan
    chunks, depth, pixels = hats.shape
    count = depth // SLOT
    place = lax.axis_index("segment") * lax.axis_size("angle") + lax.axis_index("angle")
    first_row = (place * ROWS_DEV).astype(jnp.float32) - (tile_rows - 1) / 2.0
    lane = lax.broadcasted_iota(jnp.int32, (8, pixels), 1)
    depth_step = lax.broadcasted_iota(jnp.int32, (8, pixels), 0).astype(jnp.float32)
    y = (lane // CHUNK).astype(jnp.float32) + first_row
    x = (lane % CHUNK).astype(jnp.float32)
    rest = jnp.zeros((-DEPTH % 16, pixels), jnp.float32)
    gap = jnp.zeros((SLOT - DEPTH - DEPTH % 16, pixels), jnp.bfloat16)

    def step(index, carry):
        angle = part * count + index
        cosine, sine = read(trig, angle), read(trig, angle_total + angle)
        at = pl.multiple_of(index * SLOT, SLOT)
        start = y * sine + x * cosine - depth_step
        for chunk in range(chunks):
            left = chunk * CHUNK - (TCOLS - 1) / 2.0
            code = read(codes, angle * chunks + chunk)
            low = ((code >> LANE_BITS) * SLOT + (code & (LANES - 1))).astype(jnp.float32)
            across = start + (left * cosine + (half - low))
            rows = [jnp.maximum(0.0, 1.0 - jnp.abs(across - 8.0 * j)) for j in range(DEPTH // 8)]
            rows = jnp.concatenate([*rows, rest], axis=0).astype(jnp.bfloat16)
            hats[chunk, pl.ds(at, rows.shape[0]), :] = rows
            hats[chunk, pl.ds(at + rows.shape[0], gap.shape[0]), :] = gap
        return carry

    lax.fori_loop(0, count, step, 0, unroll=2)


def project_kernel(plan, codes, *refs):
    parts, sources, arrays, segments, local, last, tiles, height, packing = plan
    full, rows_of_block, groups = packing
    windows, refs = refs[:arrays], refs[arrays:]
    windows = [(window, source) for window in windows for source in range(window.shape[0])]
    scratch = 3 if last else 1
    hats, before = refs[:segments], refs[segments : -1 - scratch]
    out, held = refs[-1 - scratch], refs[-scratch]
    if last:
        ready, sent = refs[-2:]
        copies = []
    chunks, depth, pixels = hats[0].shape
    tail_first = tiles * full * rows_of_block
    slices = height // local
    count = sources * local
    angle_count = depth // SLOT
    spread = lax.broadcasted_iota(jnp.int32, (height, LANES), 1)
    for at, (window, source) in enumerate(windows):
        if groups > 1:
            tails = window[source, tail_first:, :].astype(jnp.float32)
        for turn in range(tiles):
            pieces = []
            for j in range(full):
                rows = pl.ds((turn * full + j) * rows_of_block, rows_of_block)
                pieces.append(window[source, rows, :].astype(held.dtype)[:height])
            if groups > 1:
                tail = height // groups
                tail = tails[turn * tail : (turn + 1) * tail]
                pieces.append(unpack(tail, groups).astype(held.dtype))
            halves = [pltpu.roll(value, SLOT, 1) for value in pieces]
            for j in range(held.shape[1]):
                if j % 2 == 0:
                    value = pieces[j // 2]
                else:
                    value = jnp.where(spread < SLOT, halves[j // 2], halves[j // 2 + 1])
                for angle in range(local):
                    held[at * local + angle, j, turn * slices : (turn + 1) * slices, :] = value[
                        angle * slices : (angle + 1) * slices
                    ]
    lane = lax.broadcasted_iota(jnp.int32, (slices * tiles, LANES), 1)
    sums = []
    for chunk in range(chunks):
        value = before[0][chunk] if before else None
        for at, (by, part) in enumerate(parts):
            cut = []
            for first in range(0, count, PER):
                merged = None
                for spot in range(PER):
                    index = first + spot
                    code = read(codes, (by * angle_count + part * count + index) * chunks + chunk)
                    turn_by = (spot * SLOT + LANES - (code & (LANES - 1))) & (LANES - 1)
                    piece = pltpu.roll(held[at * count + index, code >> LANE_BITS], turn_by, 1)
                    merged = piece if spot == 0 else jnp.where(lane < spot * SLOT, merged, piece)
                cut.append(merged.astype(jnp.bfloat16))
            rows = pl.ds(part * count * SLOT, count * SLOT)
            more = jnp.dot(
                jnp.concatenate(cut, axis=1),
                hats[by][chunk, rows, :],
                preferred_element_type=jnp.float32,
            )
            value = more if value is None else value + more
        sums.append(value)
        if not last:
            out[chunk] = value
        if not last or (chunk + 1) * CHUNK % LANES:
            continue
        mine = lax.axis_index("tile")
        for row in range(ROWS_DEV):
            value = jnp.concatenate(
                [part[:, row * CHUNK : (row + 1) * CHUNK] for part in sums], axis=1
            )
            at = row * TCOLS + (chunk + 1) * CHUNK - LANES
            if slices % 8 == 0:
                for turn in range(tiles):
                    tile = lax.rem(mine + turn, tiles)
                    into = pl.ds(pl.multiple_of(tile * slices, slices), slices)
                    ready[into, at : at + LANES] = value[turn * slices : (turn + 1) * slices]
            else:
                ready[:, at : at + LANES] = pltpu.roll(value, mine * slices, 0)
            lanes = pl.ds(at, LANES)
            copies.append(
                pltpu.make_async_copy(
                    ready.at[:, lanes], out.at[0, :, lanes], sent.at[len(copies)]
                )
            )
            copies[-1].start()
        sums = []
    if last:
        for copy in copies:
            copy.wait()


def shifted(value, axis, by):
    size = lax.axis_size(axis)
    return lax.ppermute(value, axis, [(i, (i - by) % size) for i in range(size)])


def swapped(value, axis, by):
    return lax.ppermute(value, axis, [(i, i ^ by) for i in range(lax.axis_size(axis))])


def body(sinogram, paganin_width, window_block):
    local, slices, bins = sinogram.shape
    segments, spots, tiles = (lax.axis_size(name) for name in ("segment", "angle", "tile"))
    segment, spot = lax.axis_index("segment"), lax.axis_index("angle")
    groups = segments * spots
    angle_total = local * groups
    tile_rows = ROWS_DEV * groups
    reach = math.hypot((TCOLS - 1) / 2, (tile_rows - 1) / 2)
    first_bin = max(0, int(WIN / 2 - reach - 0.01)) // 16 * 16
    last_bin = min(WIN - 1, int(WIN / 2 + reach + 0.01) + 1)
    outs = -(-(last_bin + 1 - first_bin) // LANES)
    assert first_bin + (outs - 1) * LANES < WIN and first_bin < LANES
    assert spots & (spots - 1) == 0 and spots > 1
    smooth_blocks = -(-(outs + 3) // 2) * 2
    chunks, pixels = TCOLS // CHUNK, ROWS_DEV * CHUNK
    half = WIN / 2.0 - first_bin

    smem = pl.BlockSpec(memory_space=pltpu.SMEM)
    vmem = pl.BlockSpec(memory_space=pltpu.VMEM)
    hat_bytes = angle_total * SLOT * ROWS_DEV * TCOLS * 2
    params = pltpu.CompilerParams(vmem_limit_bytes=hat_bytes + 12 * 1024 * 1024)
    height = local * slices
    block_total = bins // LANES
    used = last_bin + 1 - first_bin - (outs - 1) * LANES
    row_groups = LANES // (1 << (used - 1).bit_length())
    if height % (8 * row_groups):
        row_groups = 1
    full = outs if row_groups == 1 else outs - 1
    rows_of_block = -(-height // 16) * 16
    tail = 0 if row_groups == 1 else height // row_groups
    packing = (full, rows_of_block, row_groups)
    bits = [1 << bit for bit in reversed(range(spots.bit_length() - 1))]
    exchanges = [(bits[0],)]
    for first in range(1, len(bits), 2):
        pair = bits[first : first + 2]
        exchanges.append((*pair, sum(pair)) if len(pair) == 2 else tuple(pair))
    reached = [0]
    for masks in exchanges:
        reached = [other ^ mask for mask in (0, *masks) for other in reached]
    order = np.repeat(np.array(reached), local), np.tile(np.arange(local), spots)
    where = np.arange(groups)[:, None]
    by = np.arange(segments)[:, None] + where[:, :, None] // spots
    angles = (where % spots ^ order[0]) * local + order[1]
    angles = by % segments * (spots * local) + angles[:, None]
    theta = math.pi * angles.reshape(groups, angle_total) / angle_total
    cosine, sine = np.cos(theta), np.sin(theta)
    left = np.arange(chunks) * CHUNK - (TCOLS - 1) / 2.0
    edges = np.minimum(cosine[..., None] * left, cosine[..., None] * (left + (CHUNK - 1)))
    top = where * ROWS_DEV - (tile_rows - 1) / 2.0
    rise = np.minimum(sine * top, sine * (top + (ROWS_DEV - 1)))
    lows = np.floor(edges + rise[..., None] + (half - 0.01)).astype(np.int32)
    blocks = np.minimum(lows // SLOT, PER * (outs - 1))
    codes = (blocks << LANE_BITS) + lows - blocks * SLOT

    def in_rows(values):
        values = values.reshape(groups, -1)
        rows = -(-values.shape[1] // (8 * LANES)) * 8
        values = np.pad(values, ((0, 0), (0, rows * LANES - values.shape[1])))
        return jnp.asarray(values.reshape(groups, rows, LANES))

    trig_table = in_rows(np.concatenate([cosine, sine], axis=1).astype(np.float32))
    code_table = in_rows(codes.astype(np.int32))

    *cut, trig, codes = pl.pallas_call(
        functools.partial(filter_kernel, (tiles, outs, first_bin, smooth_blocks, packing)),
        out_shape=[
            jax.ShapeDtypeStruct((full * rows_of_block + -(-tail // 16) * 16, LANES), jnp.bfloat16)
        ]
        * tiles
        + [pltpu.SMEM(v.shape[1:], v.dtype) for v in (trig_table, code_table)],
        in_specs=[smem] + [pl.BlockSpec(memory_space=pltpu.HBM)] * 4,
        out_specs=[vmem] * tiles + [smem] * 2,
        scratch_shapes=[
            pltpu.SMEM(window_block.T.shape, jnp.int32),
            pltpu.VMEM(
                (local, slices, (block_total - WIN // LANES + smooth_blocks + 2) * LANES),
                jnp.float32,
            ),
            pltpu.SemaphoreType.DMA((local + 3,)),
        ],
        compiler_params=params,
        name="filter",
    )(
        paganin_width,
        *(
            pltpu.with_memory_space_constraint(value, pltpu.HBM)
            for value in (window_block.T, trig_table, code_table, sinogram)
        ),
    )

    depth = spots * local * SLOT
    def hats_of(part, after):
        ready = lax.optimization_barrier((trig, codes, *after))[:2]
        return pl.pallas_call(
            functools.partial(hat_kernel, (part, half, tile_rows, angle_total)),
            out_shape=jax.ShapeDtypeStruct((chunks, depth, pixels), jnp.bfloat16),
            in_specs=[smem, smem],
            out_specs=vmem,
            compiler_params=params,
            cost_estimate=pl.CostEstimate(
                flops=chunks * depth * pixels * 16, bytes_accessed=0, transcendentals=0
            ),
            name="hats",
        )(*ready)

    hats = []

    def beside(moved, after, count):
        made = []
        for _ in range(min(count, segments - len(hats))):
            made.append(hats_of(len(hats), after))
            hats.append(None)
        moved, made = lax.optimization_barrier((moved, made))
        hats[len(hats) - len(made) :] = made
        return moved

    def joint(turn, mask):
        def index(spot, tile):
            return (spot ^ mask) * tiles + (tile - turn) % tiles

        pairs = [(at, index(at // tiles, at % tiles)) for at in range(spots * tiles)]
        return lax.ppermute(cut[turn], ("angle", "tile"), pairs)

    near = [(turn, mask) for mask in (0, *exchanges[0]) for turn in range(tiles)][1:]
    moved = beside([joint(*pair) for pair in near], cut, 1)
    pieces = jnp.stack([cut[0], *moved])
    whole = full * rows_of_block
    if tail:
        main = pieces[:, :whole].reshape(2, tiles * whole, LANES)
        tails = pieces[:, whole : whole + tail].reshape(2, tiles * tail, LANES)
        pieces = jnp.concatenate([main, tails], axis=1)
    else:
        pieces = pieces.reshape(2, tiles * whole, LANES)
    for masks in exchanges[1:-1]:
        moved = beside([swapped(pieces, "angle", mask) for mask in masks], (pieces,), 1)
        pieces = jnp.concatenate([pieces, *moved])
    held_type = jnp.bfloat16 if slices % 16 == 0 else jnp.float32
    sources = pieces.shape[0]

    sending = [
        pltpu.VMEM((slices * tiles, ROWS_DEV * TCOLS), jnp.float32),
        pltpu.SemaphoreType.DMA((ROWS_DEV * TCOLS // LANES,)),
    ]

    def project(parts, windows, sums, last=False):
        return pl.pallas_call(
            functools.partial(
                project_kernel,
                (parts, sources, len(windows), segments, local, last, tiles, height, packing),
            ),
            out_shape=jax.ShapeDtypeStruct(
                (1, slices * tiles, ROWS_DEV * TCOLS)
                if last
                else (chunks, slices * tiles, pixels),
                jnp.float32,
            ),
            in_specs=[smem] + [vmem] * (len(windows) + segments + len(sums)),
            out_specs=pl.BlockSpec(memory_space=pltpu.HBM) if last else vmem,
            scratch_shapes=[
                pltpu.VMEM(
                    (
                        len(parts) * sources * local,
                        PER * (outs - 1) + 1,
                        slices * tiles,
                        LANES,
                    ),
                    held_type,
                ),
                *(sending if last else []),
            ],
            compiler_params=params,
            cost_estimate=pl.CostEstimate(
                flops=32 * slices * tiles * chunks * depth * pixels,
                bytes_accessed=0,
                transcendentals=0,
            ),
            name="project",
        )(codes, *windows, *hats, *sums)

    others = range(1, segments)
    early = [pieces] + [shifted(pieces, "segment", by) for by in others]
    moved = [swapped(pieces, "angle", mask) for mask in exchanges[-1]]
    hats += [hats_of(part, (pieces,)) for part in range(len(hats), segments)]
    count = len(moved)
    if count > 1:
        early, moved[-1] = lax.optimization_barrier((early, moved[-1]))
    sums = project([(by, 0) for by in range(segments)], early, ())
    if count > 1:
        moved[:-1], sums = lax.optimization_barrier((moved[:-1], sums))
    else:
        moved, sums = lax.optimization_barrier((moved, sums))
    ahead = [shifted(moved[-1], "segment", by) for by in others]
    final = [(by, part) for by in others for part in range(1, count)]
    if final:
        rest = jnp.concatenate(moved[:-1])
        late = [shifted(rest, "segment", by) for by in others]
    own = [(0, part + 1) for part in range(count)]
    first = [(by, count) for by in others]
    if final:
        sums = project(own + first, [*moved, *ahead], (sums,))
        return project(final, late, (sums,), True)
    sums = project(own, moved, (sums,))
    return project(first, ahead, (sums,), True)


def solution(mesh):
    in_specs = (P(("segment", "angle"), "tile", None), P(), P())
    out_specs = P("tile", None, ("segment", "angle"))
    return jax.shard_map(body, mesh=mesh, in_specs=in_specs, out_specs=out_specs, check_vma=False)
```

```python
import functools
import math

import jax
import jax.numpy as jnp
import numpy as np
from jax import lax
from jax.experimental import pallas as pl
from jax.experimental.pallas import tpu as pltpu
from jax.sharding import PartitionSpec as P

WIN = 512
BAND = 128
ROWS_DEV = 8
TCOLS = 256
LANES = 128
LANE_BITS = 7
CHUNK = 32
DEPTH = 40
SLOT = 64
PER = LANES // SLOT


def split(value):
    high = value.astype(jnp.bfloat16)
    return high, (value - high.astype(jnp.float32)).astype(jnp.bfloat16)


def banded(blocks, taps, starts):
    tap_high, tap_low = taps
    count = tap_high.shape[0] // LANES
    dot = functools.partial(jnp.dot, preferred_element_type=jnp.float32)
    parts = [split(block) for block in blocks]
    high, low = (
        jnp.concatenate(
            [
                jnp.concatenate([part[which] for part in parts[at : at + count]], axis=1)
                for at in starts
            ],
            axis=0,
        )
        for which in range(2)
    )
    both = dot(jnp.concatenate([high, low], axis=0), tap_high)
    result = both[: high.shape[0]] + (both[high.shape[0] :] + dot(high, tap_low))
    rows = blocks[0].shape[0]
    return [result[index * rows : (index + 1) * rows] for index in range(len(starts))]


def offsets(depth, width, shift):
    return (
        lax.broadcasted_iota(jnp.int32, (depth, width), 0)
        - lax.broadcasted_iota(jnp.int32, (depth, width), 1)
        - shift
    )


def filter_kernel(plan, width, blocks_ref, trig_table, code_table, rows_ref, *refs):
    tiles, outs, first_bin, smooth_blocks, packing = plan
    full, rows_of_block, groups = packing
    outputs, (trig, codes, blocks, padded, arrived) = (
        refs[:tiles],
        refs[tiles:],
    )
    local, slices, bins = rows_ref.shape
    block_total = bins // LANES
    raw_wide = (smooth_blocks + 2) * LANES
    height = local * slices
    ahead = 2 * LANES

    place = lax.axis_index("segment") * lax.axis_size("angle") + lax.axis_index("angle")
    sources = [(rows_ref.at[i], padded.at[i, :, pl.ds(ahead, bins)]) for i in range(local)]
    sources = [
        *sources,
        (blocks_ref, blocks),
        (trig_table.at[place], trig),
        (code_table.at[place], codes),
    ]
    copies = [
        pltpu.make_async_copy(source, into, arrived.at[index])
        for index, (source, into) in enumerate(sources)
    ]
    for copy in copies:
        copy.start()
    behind = padded.shape[2] - ahead - bins
    padded[:, :, :ahead] = jnp.zeros((local, slices, ahead), jnp.float32)
    padded[:, :, ahead + bins :] = jnp.zeros((local, slices, behind), jnp.float32)

    away = offsets(512, LANES, BAND + first_bin)
    spread = jnp.abs(away)
    squared = jnp.maximum(spread * spread, 1).astype(jnp.float32)
    odd = jnp.logical_and(spread <= BAND, (spread & 1) == 1)
    ramp = jnp.where(odd, -1.0 / (math.pi * math.pi * squared), 0.0)
    ramp = split(jnp.where(away == 0, 0.25, ramp))
    decay = width[0]
    steps = (lax.broadcasted_iota(jnp.int32, (1, BAND), 1) + 1).astype(jnp.float32)
    total = 1.0 + 2.0 * jnp.sum(jnp.exp(-steps / decay), axis=1, keepdims=True)
    away = offsets(2 * 256, 256, BAND)
    spread = jnp.abs(away)
    paganin = jnp.where(
        spread <= BAND, jnp.exp(-spread.astype(jnp.float32) / decay) / total, 0.0
    )
    paganin = split(paganin)

    for copy in copies[: local + 1]:
        copy.wait()
    first = place * local
    mine = lax.axis_index("tile")
    starts, raw = [], []
    for turn in range(tiles):
        tile = lax.rem(mine - turn + tiles, tiles)
        for angle in range(local):
            start = blocks[tile, first + angle]
            starts.append(start)
            lanes = pl.ds(pl.multiple_of(start * LANES, LANES), raw_wide)
            raw.append(padded[angle, :, lanes])
    raw = jnp.concatenate(raw, axis=0)
    raw = [raw[:, at : at + LANES] for at in range(0, raw_wide, LANES)]
    smooth = []
    for pair in banded(raw, paganin, range(0, smooth_blocks, 2)):
        smooth += [pair[:, :LANES], pair[:, LANES:]]
    for j in range(smooth_blocks):
        if 1 <= j <= WIN // LANES:
            continue
        kept = []
        for index, start in enumerate(starts):
            block = start - 1 + j
            inside = jnp.logical_and(block >= 0, block < block_total)
            value = smooth[j][index * slices : (index + 1) * slices]
            kept.append(jnp.where(inside, value, 0.0))
        smooth[j] = jnp.concatenate(kept, axis=0)
    for j, value in enumerate(banded(smooth, ramp, range(outs))):
        for turn in range(tiles):
            part = value[turn * height : (turn + 1) * height]
            if j == full:
                part = pack(part, groups)
            if part.shape[0] % 16:
                rest = jnp.zeros((-part.shape[0] % 16, LANES), jnp.float32)
                part = jnp.concatenate([part, rest], axis=0)
            at = j * rows_of_block
            outputs[turn][at : at + part.shape[0], :] = part.astype(jnp.bfloat16)
    for copy in copies[local + 1 :]:
        copy.wait()


def pack(value, groups):
    rows, wide = value.shape[0] // groups, LANES // groups
    lane = lax.broadcasted_iota(jnp.int32, (rows, LANES), 1)
    packed = value[:rows]
    for group in range(1, groups):
        more = pltpu.roll(value[group * rows : (group + 1) * rows], group * wide, 1)
        packed = jnp.where(lane < group * wide, packed, more)
    return packed


def unpack(value, groups):
    wide = LANES // groups
    rolled = [pltpu.roll(value, (LANES - group * wide) % LANES, 1) for group in range(groups)]
    return jnp.concatenate(rolled, axis=0)


def read(table, index):
    return table[index >> LANE_BITS, index & (LANES - 1)]


def hat_kernel(plan, trig, codes, hats):
    part, half, tile_rows, angle_total = plan
    chunks, depth, pixels = hats.shape
    count = depth // SLOT
    place = lax.axis_index("segment") * lax.axis_size("angle") + lax.axis_index("angle")
    first_row = (place * ROWS_DEV).astype(jnp.float32) - (tile_rows - 1) / 2.0
    lane = lax.broadcasted_iota(jnp.int32, (8, pixels), 1)
    depth_step = lax.broadcasted_iota(jnp.int32, (8, pixels), 0).astype(jnp.float32)
    y = (lane // CHUNK).astype(jnp.float32) + first_row
    x = (lane % CHUNK).astype(jnp.float32)
    rest = jnp.zeros((-DEPTH % 16, pixels), jnp.float32)
    gap = jnp.zeros((SLOT - DEPTH - DEPTH % 16, pixels), jnp.bfloat16)

    def step(index, carry):
        angle = part * count + index
        cosine, sine = read(trig, angle), read(trig, angle_total + angle)
        at = pl.multiple_of(index * SLOT, SLOT)
        start = y * sine + x * cosine - depth_step
        for chunk in range(chunks):
            left = chunk * CHUNK - (TCOLS - 1) / 2.0
            code = read(codes, angle * chunks + chunk)
            low = ((code >> LANE_BITS) * SLOT + (code & (LANES - 1))).astype(jnp.float32)
            across = start + (left * cosine + (half - low))
            rows = [jnp.maximum(0.0, 1.0 - jnp.abs(across - 8.0 * j)) for j in range(DEPTH // 8)]
            rows = jnp.concatenate([*rows, rest], axis=0).astype(jnp.bfloat16)
            hats[chunk, pl.ds(at, rows.shape[0]), :] = rows
            hats[chunk, pl.ds(at + rows.shape[0], gap.shape[0]), :] = gap
        return carry

    lax.fori_loop(0, count, step, 0, unroll=2)


def project_kernel(plan, codes, *refs):
    parts, sources, arrays, segments, local, last, tiles, height, packing = plan
    full, rows_of_block, groups = packing
    windows, refs = refs[:arrays], refs[arrays:]
    windows = [(window, source) for window in windows for source in range(window.shape[0])]
    scratch = 3 if last else 1
    hats, before = refs[:segments], refs[segments : -1 - scratch]
    out, held = refs[-1 - scratch], refs[-scratch]
    if last:
        ready, sent = refs[-2:]
        copies = []
    chunks, depth, pixels = hats[0].shape
    tail_first = tiles * full * rows_of_block
    slices = height // local
    count = sources * local
    angle_count = depth // SLOT
    spread = lax.broadcasted_iota(jnp.int32, (height, LANES), 1)
    for at, (window, source) in enumerate(windows):
        if groups > 1:
            tails = window[source, tail_first:, :].astype(jnp.float32)
        for turn in range(tiles):
            pieces = []
            for j in range(full):
                rows = pl.ds((turn * full + j) * rows_of_block, rows_of_block)
                pieces.append(window[source, rows, :].astype(held.dtype)[:height])
            if groups > 1:
                tail = height // groups
                tail = tails[turn * tail : (turn + 1) * tail]
                pieces.append(unpack(tail, groups).astype(held.dtype))
            halves = [pltpu.roll(value, SLOT, 1) for value in pieces]
            for j in range(held.shape[1]):
                if j % 2 == 0:
                    value = pieces[j // 2]
                else:
                    value = jnp.where(spread < SLOT, halves[j // 2], halves[j // 2 + 1])
                for angle in range(local):
                    held[at * local + angle, j, turn * slices : (turn + 1) * slices, :] = value[
                        angle * slices : (angle + 1) * slices
                    ]
    lane = lax.broadcasted_iota(jnp.int32, (slices * tiles, LANES), 1)
    sums = []
    for chunk in range(chunks):
        value = before[0][chunk] if before else None
        for at, (by, part) in enumerate(parts):
            cut = []
            for first in range(0, count, PER):
                merged = None
                for spot in range(PER):
                    index = first + spot
                    code = read(codes, (by * angle_count + part * count + index) * chunks + chunk)
                    turn_by = (spot * SLOT + LANES - (code & (LANES - 1))) & (LANES - 1)
                    piece = pltpu.roll(held[at * count + index, code >> LANE_BITS], turn_by, 1)
                    merged = piece if spot == 0 else jnp.where(lane < spot * SLOT, merged, piece)
                cut.append(merged.astype(jnp.bfloat16))
            rows = pl.ds(part * count * SLOT, count * SLOT)
            more = jnp.dot(
                jnp.concatenate(cut, axis=1),
                hats[by][chunk, rows, :],
                preferred_element_type=jnp.float32,
            )
            value = more if value is None else value + more
        sums.append(value)
        if not last:
            out[chunk] = value
        if not last or (chunk + 1) * CHUNK % LANES:
            continue
        mine = lax.axis_index("tile")
        for row in range(ROWS_DEV):
            value = jnp.concatenate(
                [part[:, row * CHUNK : (row + 1) * CHUNK] for part in sums], axis=1
            )
            at = row * TCOLS + (chunk + 1) * CHUNK - LANES
            if slices % 8 == 0:
                for turn in range(tiles):
                    tile = lax.rem(mine + turn, tiles)
                    into = pl.ds(pl.multiple_of(tile * slices, slices), slices)
                    ready[into, at : at + LANES] = value[turn * slices : (turn + 1) * slices]
            else:
                ready[:, at : at + LANES] = pltpu.roll(value, mine * slices, 0)
            lanes = pl.ds(at, LANES)
            copies.append(
                pltpu.make_async_copy(
                    ready.at[:, lanes], out.at[0, :, lanes], sent.at[len(copies)]
                )
            )
            copies[-1].start()
        sums = []
    if last:
        for copy in copies:
            copy.wait()


def shifted(value, axis, by):
    size = lax.axis_size(axis)
    return lax.ppermute(value, axis, [(i, (i - by) % size) for i in range(size)])


def swapped(value, axis, by):
    return lax.ppermute(value, axis, [(i, i ^ by) for i in range(lax.axis_size(axis))])


def body(sinogram, paganin_width, window_block):
    local, slices, bins = sinogram.shape
    segments, spots, tiles = (lax.axis_size(name) for name in ("segment", "angle", "tile"))
    segment, spot = lax.axis_index("segment"), lax.axis_index("angle")
    groups = segments * spots
    angle_total = local * groups
    tile_rows = ROWS_DEV * groups
    reach = math.hypot((TCOLS - 1) / 2, (tile_rows - 1) / 2)
    first_bin = max(0, int(WIN / 2 - reach - 0.01)) // 16 * 16
    last_bin = min(WIN - 1, int(WIN / 2 + reach + 0.01) + 1)
    outs = -(-(last_bin + 1 - first_bin) // LANES)
    assert first_bin + (outs - 1) * LANES < WIN and first_bin < LANES
    assert spots & (spots - 1) == 0 and spots > 1
    smooth_blocks = -(-(outs + 3) // 2) * 2
    chunks, pixels = TCOLS // CHUNK, ROWS_DEV * CHUNK
    half = WIN / 2.0 - first_bin

    smem = pl.BlockSpec(memory_space=pltpu.SMEM)
    vmem = pl.BlockSpec(memory_space=pltpu.VMEM)
    hat_bytes = angle_total * SLOT * ROWS_DEV * TCOLS * 2
    params = pltpu.CompilerParams(vmem_limit_bytes=hat_bytes + 12 * 1024 * 1024)
    height = local * slices
    block_total = bins // LANES
    used = last_bin + 1 - first_bin - (outs - 1) * LANES
    row_groups = LANES // (1 << (used - 1).bit_length())
    if height % (8 * row_groups):
        row_groups = 1
    full = outs if row_groups == 1 else outs - 1
    rows_of_block = -(-height // 16) * 16
    tail = 0 if row_groups == 1 else height // row_groups
    packing = (full, rows_of_block, row_groups)
    bits = [1 << bit for bit in reversed(range(spots.bit_length() - 1))]
    exchanges = [(bits[0],)]
    for first in range(1, len(bits), 2):
        pair = bits[first : first + 2]
        exchanges.append((*pair, sum(pair)) if len(pair) == 2 else tuple(pair))
    reached = [0]
    for masks in exchanges:
        reached = [other ^ mask for mask in (0, *masks) for other in reached]
    order = np.repeat(np.array(reached), local), np.tile(np.arange(local), spots)
    where = np.arange(groups)[:, None]
    by = np.arange(segments)[:, None] + where[:, :, None] // spots
    angles = (where % spots ^ order[0]) * local + order[1]
    angles = by % segments * (spots * local) + angles[:, None]
    theta = math.pi * angles.reshape(groups, angle_total) / angle_total
    cosine, sine = np.cos(theta), np.sin(theta)
    left = np.arange(chunks) * CHUNK - (TCOLS - 1) / 2.0
    edges = np.minimum(cosine[..., None] * left, cosine[..., None] * (left + (CHUNK - 1)))
    top = where * ROWS_DEV - (tile_rows - 1) / 2.0
    rise = np.minimum(sine * top, sine * (top + (ROWS_DEV - 1)))
    lows = np.floor(edges + rise[..., None] + (half - 0.01)).astype(np.int32)
    blocks = np.minimum(lows // SLOT, PER * (outs - 1))
    codes = (blocks << LANE_BITS) + lows - blocks * SLOT

    def in_rows(values):
        values = values.reshape(groups, -1)
        rows = -(-values.shape[1] // (8 * LANES)) * 8
        values = np.pad(values, ((0, 0), (0, rows * LANES - values.shape[1])))
        return jnp.asarray(values.reshape(groups, rows, LANES))

    trig_table = in_rows(np.concatenate([cosine, sine], axis=1).astype(np.float32))
    code_table = in_rows(codes.astype(np.int32))

    *cut, trig, codes = pl.pallas_call(
        functools.partial(filter_kernel, (tiles, outs, first_bin, smooth_blocks, packing)),
        out_shape=[
            jax.ShapeDtypeStruct((full * rows_of_block + -(-tail // 16) * 16, LANES), jnp.bfloat16)
        ]
        * tiles
        + [pltpu.SMEM(v.shape[1:], v.dtype) for v in (trig_table, code_table)],
        in_specs=[smem] + [pl.BlockSpec(memory_space=pltpu.HBM)] * 4,
        out_specs=[vmem] * tiles + [smem] * 2,
        scratch_shapes=[
            pltpu.SMEM(window_block.T.shape, jnp.int32),
            pltpu.VMEM(
                (local, slices, (block_total - WIN // LANES + smooth_blocks + 2) * LANES),
                jnp.float32,
            ),
            pltpu.SemaphoreType.DMA((local + 3,)),
        ],
        compiler_params=params,
        name="filter",
    )(
        paganin_width,
        *(
            pltpu.with_memory_space_constraint(value, pltpu.HBM)
            for value in (window_block.T, trig_table, code_table, sinogram)
        ),
    )

    depth = spots * local * SLOT
    def hats_of(part, after):
        ready = lax.optimization_barrier((trig, codes, *after))[:2]
        return pl.pallas_call(
            functools.partial(hat_kernel, (part, half, tile_rows, angle_total)),
            out_shape=jax.ShapeDtypeStruct((chunks, depth, pixels), jnp.bfloat16),
            in_specs=[smem, smem],
            out_specs=vmem,
            compiler_params=params,
            cost_estimate=pl.CostEstimate(
                flops=chunks * depth * pixels * 16, bytes_accessed=0, transcendentals=0
            ),
            name="hats",
        )(*ready)

    hats = []

    def beside(moved, after, count):
        made = []
        for _ in range(min(count, segments - len(hats))):
            made.append(hats_of(len(hats), after))
            hats.append(None)
        moved, made = lax.optimization_barrier((moved, made))
        hats[len(hats) - len(made) :] = made
        return moved

    def joint(turn, mask):
        def index(spot, tile):
            return (spot ^ mask) * tiles + (tile - turn) % tiles

        pairs = [(at, index(at // tiles, at % tiles)) for at in range(spots * tiles)]
        return lax.ppermute(cut[turn], ("angle", "tile"), pairs)

    near = [(turn, mask) for mask in (0, *exchanges[0]) for turn in range(tiles)][1:]
    moved = beside([joint(*pair) for pair in near], cut, 1)
    pieces = jnp.stack([cut[0], *moved])
    whole = full * rows_of_block
    if tail:
        main = pieces[:, :whole].reshape(2, tiles * whole, LANES)
        tails = pieces[:, whole : whole + tail].reshape(2, tiles * tail, LANES)
        pieces = jnp.concatenate([main, tails], axis=1)
    else:
        pieces = pieces.reshape(2, tiles * whole, LANES)
    for masks in exchanges[1:-1]:
        moved = beside([swapped(pieces, "angle", mask) for mask in masks], (pieces,), 1)
        pieces = jnp.concatenate([pieces, *moved])
    held_type = jnp.bfloat16 if slices % 16 == 0 else jnp.float32
    sources = pieces.shape[0]

    sending = [
        pltpu.VMEM((slices * tiles, ROWS_DEV * TCOLS), jnp.float32),
        pltpu.SemaphoreType.DMA((ROWS_DEV * TCOLS // LANES,)),
    ]

    def project(parts, windows, sums, last=False):
        return pl.pallas_call(
            functools.partial(
                project_kernel,
                (parts, sources, len(windows), segments, local, last, tiles, height, packing),
            ),
            out_shape=jax.ShapeDtypeStruct(
                (1, slices * tiles, ROWS_DEV * TCOLS)
                if last
                else (chunks, slices * tiles, pixels),
                jnp.float32,
            ),
            in_specs=[smem] + [vmem] * (len(windows) + segments + len(sums)),
            out_specs=pl.BlockSpec(memory_space=pltpu.HBM) if last else vmem,
            scratch_shapes=[
                pltpu.VMEM(
                    (
                        len(parts) * sources * local,
                        PER * (outs - 1) + 1,
                        slices * tiles,
                        LANES,
                    ),
                    held_type,
                ),
                *(sending if last else []),
            ],
            compiler_params=params,
            cost_estimate=pl.CostEstimate(
                flops=32 * slices * tiles * chunks * depth * pixels,
                bytes_accessed=0,
                transcendentals=0,
            ),
            name="project",
        )(codes, *windows, *hats, *sums)

    others = range(1, segments)
    early = [pieces] + [shifted(pieces, "segment", by) for by in others]
    moved = [swapped(pieces, "angle", mask) for mask in exchanges[-1]]
    hats += [hats_of(part, (pieces,)) for part in range(len(hats), segments)]
    count = len(moved)
    if count > 1:
        early, moved[-1] = lax.optimization_barrier((early, moved[-1]))
    sums = project([(by, 0) for by in range(segments)], early, ())
    if count > 1:
        moved[:-1], sums = lax.optimization_barrier((moved[:-1], sums))
    else:
        moved, sums = lax.optimization_barrier((moved, sums))
    ahead = [shifted(moved[-1], "segment", by) for by in others]
    final = [(by, part) for by in others for part in range(1, count)]
    if final:
        rest = jnp.concatenate(moved[:-1])
        late = [shifted(rest, "segment", by) for by in others]
    own = [(0, part + 1) for part in range(count)]
    first = [(by, count) for by in others]
    if final:
        sums = project(own + first, [*moved, *ahead], (sums,))
        return project(final, late, (sums,), True)
    sums = project(own, moved, (sums,))
    return project(first, ahead, (sums,), True)


def solution(mesh):
    in_specs = (P(("segment", "angle"), "tile", None), P(), P())
    out_specs = P("tile", None, ("segment", "angle"))
    return jax.shard_map(body, mesh=mesh, in_specs=in_specs, out_specs=out_specs, check_vma=False)
```

```python
import functools
import math

import jax
import jax.numpy as jnp
import numpy as np
from jax import lax
from jax.experimental import pallas as pl
from jax.experimental.pallas import tpu as pltpu
from jax.sharding import PartitionSpec as P

WIN = 512
BAND = 128
ROWS_DEV = 8
TCOLS = 256
LANES = 128
LANE_BITS = 7
CHUNK = 32
DEPTH = 40
SLOT = 64
PER = LANES // SLOT


def split(value):
    high = value.astype(jnp.bfloat16)
    return high, (value - high.astype(jnp.float32)).astype(jnp.bfloat16)


def banded(blocks, taps, starts):
    tap_high, tap_low = taps
    count = tap_high.shape[0] // LANES
    dot = functools.partial(jnp.dot, preferred_element_type=jnp.float32)
    parts = [split(block) for block in blocks]
    high, low = (
        jnp.concatenate(
            [
                jnp.concatenate([part[which] for part in parts[at : at + count]], axis=1)
                for at in starts
            ],
            axis=0,
        )
        for which in range(2)
    )
    both = dot(jnp.concatenate([high, low], axis=0), tap_high)
    result = both[: high.shape[0]] + (both[high.shape[0] :] + dot(high, tap_low))
    rows = blocks[0].shape[0]
    return [result[index * rows : (index + 1) * rows] for index in range(len(starts))]


def offsets(depth, width, shift):
    return (
        lax.broadcasted_iota(jnp.int32, (depth, width), 0)
        - lax.broadcasted_iota(jnp.int32, (depth, width), 1)
        - shift
    )


def filter_kernel(plan, width, blocks_ref, trig_table, code_table, rows_ref, *refs):
    tiles, outs, first_bin, smooth_blocks, packing = plan
    full, rows_of_block, groups = packing
    outputs, (trig, codes, blocks, padded, arrived) = (
        refs[:tiles],
        refs[tiles:],
    )
    local, slices, bins = rows_ref.shape
    block_total = bins // LANES
    raw_wide = (smooth_blocks + 2) * LANES
    height = local * slices
    ahead = 2 * LANES

    place = lax.axis_index("segment") * lax.axis_size("angle") + lax.axis_index("angle")
    sources = [(rows_ref.at[i], padded.at[i, :, pl.ds(ahead, bins)]) for i in range(local)]
    sources = [
        *sources,
        (blocks_ref, blocks),
        (trig_table.at[place], trig),
        (code_table.at[place], codes),
    ]
    copies = [
        pltpu.make_async_copy(source, into, arrived.at[index])
        for index, (source, into) in enumerate(sources)
    ]
    for copy in copies:
        copy.start()
    behind = padded.shape[2] - ahead - bins
    padded[:, :, :ahead] = jnp.zeros((local, slices, ahead), jnp.float32)
    padded[:, :, ahead + bins :] = jnp.zeros((local, slices, behind), jnp.float32)

    away = offsets(512, LANES, BAND + first_bin)
    spread = jnp.abs(away)
    squared = jnp.maximum(spread * spread, 1).astype(jnp.float32)
    odd = jnp.logical_and(spread <= BAND, (spread & 1) == 1)
    ramp = jnp.where(odd, -1.0 / (math.pi * math.pi * squared), 0.0)
    ramp = split(jnp.where(away == 0, 0.25, ramp))
    decay = width[0]
    steps = (lax.broadcasted_iota(jnp.int32, (1, BAND), 1) + 1).astype(jnp.float32)
    total = 1.0 + 2.0 * jnp.sum(jnp.exp(-steps / decay), axis=1, keepdims=True)
    away = offsets(2 * 256, 256, BAND)
    spread = jnp.abs(away)
    paganin = jnp.where(
        spread <= BAND, jnp.exp(-spread.astype(jnp.float32) / decay) / total, 0.0
    )
    paganin = split(paganin)

    for copy in copies:
        copy.wait()
    first = place * local
    mine = lax.axis_index("tile")
    starts, raw = [], []
    for turn in range(tiles):
        tile = lax.rem(mine - turn + tiles, tiles)
        for angle in range(local):
            start = blocks[tile, first + angle]
            starts.append(start)
            lanes = pl.ds(pl.multiple_of(start * LANES, LANES), raw_wide)
            raw.append(padded[angle, :, lanes])
    raw = jnp.concatenate(raw, axis=0)
    raw = [raw[:, at : at + LANES] for at in range(0, raw_wide, LANES)]
    smooth = []
    for pair in banded(raw, paganin, range(0, smooth_blocks, 2)):
        smooth += [pair[:, :LANES], pair[:, LANES:]]
    for j in range(smooth_blocks):
        if 1 <= j <= WIN // LANES:
            continue
        kept = []
        for index, start in enumerate(starts):
            block = start - 1 + j
            inside = jnp.logical_and(block >= 0, block < block_total)
            value = smooth[j][index * slices : (index + 1) * slices]
            kept.append(jnp.where(inside, value, 0.0))
        smooth[j] = jnp.concatenate(kept, axis=0)
    for j, value in enumerate(banded(smooth, ramp, range(outs))):
        for turn in range(tiles):
            part = value[turn * height : (turn + 1) * height]
            if j == full:
                part = pack(part, groups)
            if part.shape[0] % 16:
                rest = jnp.zeros((-part.shape[0] % 16, LANES), jnp.float32)
                part = jnp.concatenate([part, rest], axis=0)
            at = j * rows_of_block
            outputs[turn][at : at + part.shape[0], :] = part.astype(jnp.bfloat16)


def pack(value, groups):
    rows, wide = value.shape[0] // groups, LANES // groups
    lane = lax.broadcasted_iota(jnp.int32, (rows, LANES), 1)
    packed = value[:rows]
    for group in range(1, groups):
        more = pltpu.roll(value[group * rows : (group + 1) * rows], group * wide, 1)
        packed = jnp.where(lane < group * wide, packed, more)
    return packed


def unpack(value, groups):
    wide = LANES // groups
    rolled = [pltpu.roll(value, (LANES - group * wide) % LANES, 1) for group in range(groups)]
    return jnp.concatenate(rolled, axis=0)


def read(table, index):
    return table[index >> LANE_BITS, index & (LANES - 1)]


def hat_kernel(plan, trig, codes, hats):
    part, half, tile_rows, angle_total = plan
    chunks, depth, pixels = hats.shape
    count = depth // SLOT
    place = lax.axis_index("segment") * lax.axis_size("angle") + lax.axis_index("angle")
    first_row = (place * ROWS_DEV).astype(jnp.float32) - (tile_rows - 1) / 2.0
    lane = lax.broadcasted_iota(jnp.int32, (8, pixels), 1)
    depth_step = lax.broadcasted_iota(jnp.int32, (8, pixels), 0).astype(jnp.float32)
    y = (lane // CHUNK).astype(jnp.float32) + first_row
    x = (lane % CHUNK).astype(jnp.float32)
    rest = jnp.zeros((-DEPTH % 16, pixels), jnp.float32)
    gap = jnp.zeros((SLOT - DEPTH - DEPTH % 16, pixels), jnp.bfloat16)

    def step(index, carry):
        angle = part * count + index
        cosine, sine = read(trig, angle), read(trig, angle_total + angle)
        at = pl.multiple_of(index * SLOT, SLOT)
        start = y * sine + x * cosine - depth_step
        for chunk in range(chunks):
            left = chunk * CHUNK - (TCOLS - 1) / 2.0
            code = read(codes, angle * chunks + chunk)
            low = ((code >> LANE_BITS) * SLOT + (code & (LANES - 1))).astype(jnp.float32)
            across = start + (left * cosine + (half - low))
            rows = [jnp.maximum(0.0, 1.0 - jnp.abs(across - 8.0 * j)) for j in range(DEPTH // 8)]
            rows = jnp.concatenate([*rows, rest], axis=0).astype(jnp.bfloat16)
            hats[chunk, pl.ds(at, rows.shape[0]), :] = rows
            hats[chunk, pl.ds(at + rows.shape[0], gap.shape[0]), :] = gap
        return carry

    lax.fori_loop(0, count, step, 0, unroll=4)


def project_kernel(plan, codes, *refs):
    parts, sources, arrays, segments, local, last, tiles, height, packing = plan
    full, rows_of_block, groups = packing
    windows, refs = refs[:arrays], refs[arrays:]
    windows = [(window, source) for window in windows for source in range(window.shape[0])]
    scratch = 3 if last else 1
    hats, before = refs[:segments], refs[segments : -1 - scratch]
    out, held = refs[-1 - scratch], refs[-scratch]
    if last:
        ready, sent = refs[-2:]
        copies = []
    chunks, depth, pixels = hats[0].shape
    tail_first = tiles * full * rows_of_block
    slices = height // local
    count = sources * local
    angle_count = depth // SLOT
    spread = lax.broadcasted_iota(jnp.int32, (height, LANES), 1)
    for at, (window, source) in enumerate(windows):
        if groups > 1:
            tails = window[source, tail_first:, :].astype(jnp.float32)
        for turn in range(tiles):
            pieces = []
            for j in range(full):
                rows = pl.ds((turn * full + j) * rows_of_block, rows_of_block)
                pieces.append(window[source, rows, :].astype(held.dtype)[:height])
            if groups > 1:
                tail = height // groups
                tail = tails[turn * tail : (turn + 1) * tail]
                pieces.append(unpack(tail, groups).astype(held.dtype))
            halves = [pltpu.roll(value, SLOT, 1) for value in pieces]
            for j in range(held.shape[1]):
                if j % 2 == 0:
                    value = pieces[j // 2]
                else:
                    value = jnp.where(spread < SLOT, halves[j // 2], halves[j // 2 + 1])
                for angle in range(local):
                    held[at * local + angle, j, turn * slices : (turn + 1) * slices, :] = value[
                        angle * slices : (angle + 1) * slices
                    ]
    lane = lax.broadcasted_iota(jnp.int32, (slices * tiles, LANES), 1)
    sums = []
    for chunk in range(chunks):
        value = before[0][chunk] if before else None
        for at, (by, part) in enumerate(parts):
            cut = []
            for first in range(0, count, PER):
                merged = None
                for spot in range(PER):
                    index = first + spot
                    code = read(codes, (by * angle_count + part * count + index) * chunks + chunk)
                    turn_by = (spot * SLOT + LANES - (code & (LANES - 1))) & (LANES - 1)
                    piece = pltpu.roll(held[at * count + index, code >> LANE_BITS], turn_by, 1)
                    merged = piece if spot == 0 else jnp.where(lane < spot * SLOT, merged, piece)
                cut.append(merged.astype(jnp.bfloat16))
            rows = pl.ds(part * count * SLOT, count * SLOT)
            more = jnp.dot(
                jnp.concatenate(cut, axis=1),
                hats[by][chunk, rows, :],
                preferred_element_type=jnp.float32,
            )
            value = more if value is None else value + more
        sums.append(value)
        if not last:
            out[chunk] = value
        if not last or (chunk + 1) * CHUNK % LANES:
            continue
        mine = lax.axis_index("tile")
        for row in range(ROWS_DEV):
            value = jnp.concatenate(
                [part[:, row * CHUNK : (row + 1) * CHUNK] for part in sums], axis=1
            )
            at = row * TCOLS + (chunk + 1) * CHUNK - LANES
            if slices % 8 == 0:
                for turn in range(tiles):
                    tile = lax.rem(mine + turn, tiles)
                    into = pl.ds(pl.multiple_of(tile * slices, slices), slices)
                    ready[into, at : at + LANES] = value[turn * slices : (turn + 1) * slices]
            else:
                ready[:, at : at + LANES] = pltpu.roll(value, mine * slices, 0)
            lanes = pl.ds(at, LANES)
            copies.append(
                pltpu.make_async_copy(
                    ready.at[:, lanes], out.at[0, :, lanes], sent.at[len(copies)]
                )
            )
            copies[-1].start()
        sums = []
    if last:
        for copy in copies:
            copy.wait()


def shifted(value, axis, by):
    size = lax.axis_size(axis)
    return lax.ppermute(value, axis, [(i, (i - by) % size) for i in range(size)])


def swapped(value, axis, by):
    return lax.ppermute(value, axis, [(i, i ^ by) for i in range(lax.axis_size(axis))])


def body(sinogram, paganin_width, window_block):
    local, slices, bins = sinogram.shape
    segments, spots, tiles = (lax.axis_size(name) for name in ("segment", "angle", "tile"))
    segment, spot = lax.axis_index("segment"), lax.axis_index("angle")
    groups = segments * spots
    angle_total = local * groups
    tile_rows = ROWS_DEV * groups
    reach = math.hypot((TCOLS - 1) / 2, (tile_rows - 1) / 2)
    first_bin = max(0, int(WIN / 2 - reach - 0.01)) // 16 * 16
    last_bin = min(WIN - 1, int(WIN / 2 + reach + 0.01) + 1)
    outs = -(-(last_bin + 1 - first_bin) // LANES)
    assert first_bin + (outs - 1) * LANES < WIN and first_bin < LANES
    assert spots & (spots - 1) == 0 and spots > 1
    smooth_blocks = -(-(outs + 3) // 2) * 2
    chunks, pixels = TCOLS // CHUNK, ROWS_DEV * CHUNK
    half = WIN / 2.0 - first_bin

    smem = pl.BlockSpec(memory_space=pltpu.SMEM)
    vmem = pl.BlockSpec(memory_space=pltpu.VMEM)
    hat_bytes = angle_total * SLOT * ROWS_DEV * TCOLS * 2
    params = pltpu.CompilerParams(vmem_limit_bytes=hat_bytes + 12 * 1024 * 1024)
    height = local * slices
    block_total = bins // LANES
    used = last_bin + 1 - first_bin - (outs - 1) * LANES
    row_groups = LANES // (1 << (used - 1).bit_length())
    if height % (8 * row_groups):
        row_groups = 1
    full = outs if row_groups == 1 else outs - 1
    rows_of_block = -(-height // 16) * 16
    tail = 0 if row_groups == 1 else height // row_groups
    packing = (full, rows_of_block, row_groups)
    bits = [1 << bit for bit in reversed(range(spots.bit_length() - 1))]
    exchanges = [(bits[0],)]
    for first in range(1, len(bits), 2):
        pair = bits[first : first + 2]
        exchanges.append((*pair, sum(pair)) if len(pair) == 2 else tuple(pair))
    reached = [0]
    for masks in exchanges:
        reached = [other ^ mask for mask in (0, *masks) for other in reached]
    order = np.repeat(np.array(reached), local), np.tile(np.arange(local), spots)
    where = np.arange(groups)[:, None]
    by = np.arange(segments)[:, None] + where[:, :, None] // spots
    angles = (where % spots ^ order[0]) * local + order[1]
    angles = by % segments * (spots * local) + angles[:, None]
    theta = math.pi * angles.reshape(groups, angle_total) / angle_total
    cosine, sine = np.cos(theta), np.sin(theta)
    left = np.arange(chunks) * CHUNK - (TCOLS - 1) / 2.0
    edges = np.minimum(cosine[..., None] * left, cosine[..., None] * (left + (CHUNK - 1)))
    top = where * ROWS_DEV - (tile_rows - 1) / 2.0
    rise = np.minimum(sine * top, sine * (top + (ROWS_DEV - 1)))
    lows = np.floor(edges + rise[..., None] + (half - 0.01)).astype(np.int32)
    blocks = np.minimum(lows // SLOT, PER * (outs - 1))
    codes = (blocks << LANE_BITS) + lows - blocks * SLOT

    def in_rows(values):
        values = values.reshape(groups, -1)
        rows = -(-values.shape[1] // (8 * LANES)) * 8
        values = np.pad(values, ((0, 0), (0, rows * LANES - values.shape[1])))
        return jnp.asarray(values.reshape(groups, rows, LANES))

    trig_table = in_rows(np.concatenate([cosine, sine], axis=1).astype(np.float32))
    code_table = in_rows(codes.astype(np.int32))

    *cut, trig, codes = pl.pallas_call(
        functools.partial(filter_kernel, (tiles, outs, first_bin, smooth_blocks, packing)),
        out_shape=[
            jax.ShapeDtypeStruct((full * rows_of_block + -(-tail // 16) * 16, LANES), jnp.bfloat16)
        ]
        * tiles
        + [pltpu.SMEM(v.shape[1:], v.dtype) for v in (trig_table, code_table)],
        in_specs=[smem] + [pl.BlockSpec(memory_space=pltpu.HBM)] * 4,
        out_specs=[vmem] * tiles + [smem] * 2,
        scratch_shapes=[
            pltpu.SMEM(window_block.T.shape, jnp.int32),
            pltpu.VMEM(
                (local, slices, (block_total - WIN // LANES + smooth_blocks + 2) * LANES),
                jnp.float32,
            ),
            pltpu.SemaphoreType.DMA((local + 3,)),
        ],
        compiler_params=params,
        name="filter",
    )(
        paganin_width,
        *(
            pltpu.with_memory_space_constraint(value, pltpu.HBM)
            for value in (window_block.T, trig_table, code_table, sinogram)
        ),
    )

    depth = spots * local * SLOT
    def hats_of(part, after):
        ready = lax.optimization_barrier((trig, codes, *after))[:2]
        return pl.pallas_call(
            functools.partial(hat_kernel, (part, half, tile_rows, angle_total)),
            out_shape=jax.ShapeDtypeStruct((chunks, depth, pixels), jnp.bfloat16),
            in_specs=[smem, smem],
            out_specs=vmem,
            compiler_params=params,
            cost_estimate=pl.CostEstimate(
                flops=chunks * depth * pixels * 16, bytes_accessed=0, transcendentals=0
            ),
            name="hats",
        )(*ready)

    hats = []

    def beside(moved, after, count):
        made = []
        for _ in range(min(count, segments - len(hats))):
            made.append(hats_of(len(hats), after))
            hats.append(None)
        moved, made = lax.optimization_barrier((moved, made))
        hats[len(hats) - len(made) :] = made
        return moved

    def joint(turn, mask):
        def index(spot, tile):
            return (spot ^ mask) * tiles + (tile - turn) % tiles

        pairs = [(at, index(at // tiles, at % tiles)) for at in range(spots * tiles)]
        return lax.ppermute(cut[turn], ("angle", "tile"), pairs)

    near = [(turn, mask) for mask in (0, *exchanges[0]) for turn in range(tiles)][1:]
    moved = beside([joint(*pair) for pair in near], cut, 1)
    pieces = jnp.stack([cut[0], *moved])
    whole = full * rows_of_block
    if tail:
        main = pieces[:, :whole].reshape(2, tiles * whole, LANES)
        tails = pieces[:, whole : whole + tail].reshape(2, tiles * tail, LANES)
        pieces = jnp.concatenate([main, tails], axis=1)
    else:
        pieces = pieces.reshape(2, tiles * whole, LANES)
    for masks in exchanges[1:-1]:
        moved = beside([swapped(pieces, "angle", mask) for mask in masks], (pieces,), 1)
        pieces = jnp.concatenate([pieces, *moved])
    held_type = jnp.bfloat16 if slices % 16 == 0 else jnp.float32
    sources = pieces.shape[0]

    sending = [
        pltpu.VMEM((slices * tiles, ROWS_DEV * TCOLS), jnp.float32),
        pltpu.SemaphoreType.DMA((ROWS_DEV * TCOLS // LANES,)),
    ]

    def project(parts, windows, sums, last=False):
        return pl.pallas_call(
            functools.partial(
                project_kernel,
                (parts, sources, len(windows), segments, local, last, tiles, height, packing),
            ),
            out_shape=jax.ShapeDtypeStruct(
                (1, slices * tiles, ROWS_DEV * TCOLS)
                if last
                else (chunks, slices * tiles, pixels),
                jnp.float32,
            ),
            in_specs=[smem] + [vmem] * (len(windows) + segments + len(sums)),
            out_specs=pl.BlockSpec(memory_space=pltpu.HBM) if last else vmem,
            scratch_shapes=[
                pltpu.VMEM(
                    (
                        len(parts) * sources * local,
                        PER * (outs - 1) + 1,
                        slices * tiles,
                        LANES,
                    ),
                    held_type,
                ),
                *(sending if last else []),
            ],
            compiler_params=params,
            cost_estimate=pl.CostEstimate(
                flops=32 * slices * tiles * chunks * depth * pixels,
                bytes_accessed=0,
                transcendentals=0,
            ),
            name="project",
        )(codes, *windows, *hats, *sums)

    others = range(1, segments)
    early = [pieces] + [shifted(pieces, "segment", by) for by in others]
    moved = [swapped(pieces, "angle", mask) for mask in exchanges[-1]]
    hats += [hats_of(part, (pieces,)) for part in range(len(hats), segments)]
    count = len(moved)
    if count > 1:
        early, moved[-1] = lax.optimization_barrier((early, moved[-1]))
    sums = project([(by, 0) for by in range(segments)], early, ())
    if count > 1:
        moved[:-1], sums = lax.optimization_barrier((moved[:-1], sums))
    else:
        moved, sums = lax.optimization_barrier((moved, sums))
    ahead = [shifted(moved[-1], "segment", by) for by in others]
    final = [(by, part) for by in others for part in range(1, count)]
    if final:
        rest = jnp.concatenate(moved[:-1])
        late = [shifted(rest, "segment", by) for by in others]
    own = [(0, part + 1) for part in range(count)]
    first = [(by, count) for by in others]
    if final:
        sums = project(own + first, [*moved, *ahead], (sums,))
        return project(final, late, (sums,), True)
    sums = project(own, moved, (sums,))
    return project(first, ahead, (sums,), True)


def solution(mesh):
    in_specs = (P(("segment", "angle"), "tile", None), P(), P())
    out_specs = P("tile", None, ("segment", "angle"))
    return jax.shard_map(body, mesh=mesh, in_specs=in_specs, out_specs=out_specs, check_vma=False)
```
